32 devices in a mesh: grp: 2 (over y), lat: 4 (over z), lon: 2 (over x), comp: 2 (over core).
Axes of the slice: x: 2, y: 2, z: 4, core: 2. Of those that a mesh axis runs over, the one named last changes fastest.
Arguments:
- atmos_state: bfloat16 [48, 32, 768], P(None, ('grp', 'lat', 'comp'), 'lon'), parts along dimension 1, may hold values from -6 to 6
- ocean_state: bfloat16 [40, 32, 768], P(None, ('grp', 'lat', 'comp'), 'lon'), parts along dimension 1, may hold values from -6 to 6
- ocean_mask: int32 [32, 768], P(('grp', 'lat', 'comp'), 'lon'), parts along dimension 0, may hold values 0 or 1
- atmos_in_w: bfloat16 [2, 9, 256, 48], replicated, may hold values from -0.3125 to 0.3125
- atmos_out_w: bfloat16 [2, 9, 48, 256], replicated, may hold values from -0.125 to 0.125
- ocean_in_w: bfloat16 [2, 9, 128, 48], replicated, may hold values from -0.3125 to 0.3125
- ocean_out_w: bfloat16 [2, 9, 40, 128], replicated, may hold values from -0.1875 to 0.1875
- flux_proj: bfloat16 [8, 48], replicated, may hold values from -0.875 to 0.875
- regrid_blocks: bfloat16 [64, 128, 128], replicated, may hold values from -0.5 to 0.5
- regrid_source_block: int32 [16, 2, 8, 2], P(('grp', 'lat', 'comp'), 'lon'), parts along dimension 0, may hold values from -1 to 5, as said below
- regrid_target_block: int32 [16, 2, 8, 2], P(('grp', 'lat', 'comp'), 'lon'), parts along dimension 0, may hold values from 0 to 5
- regrid_weight_block: int32 [16, 2, 8, 2], P(('grp', 'lat', 'comp'), 'lon'), parts along dimension 0, may hold values from 0 to 63
Outputs:
- atmos_next: bfloat16 [48, 32, 768], P(None, ('grp', 'lat', 'comp'), 'lon'), parts along dimension 1
- ocean_next: bfloat16 [40, 32, 768], P(None, ('grp', 'lat', 'comp'), 'lon'), parts along dimension 1
- surface_temp_on_atmosphere: float32 [32, 768], P(('grp', 'lat', 'comp'), 'lon'), parts along dimension 0
The draws below stay inside these ranges and needn't reach their ends.
There are 2 independent parts, one for each index of `grp`. The reference program is written for one: setup_inputs(seed, part) draws one part's arguments, and reference() takes and returns one part's arrays. A program takes and returns all parts, laid end to end along the dimension named above; an argument that names none is the same for every part. Nothing has to cross between parts.
Inputs may be any that keep to these rules, and one draw needn't show every extreme that they name: `regrid_source_block`: empty slots hold -1, live ones a sub-block of the source tile; each tile has both slots to the next latitude tile (t + 1 modulo 8) live, and the share of live slots differs from one latitude tile to another.
All inputs are finite; a program needn't handle non-finite values. No bound on the sum of `ocean_mask` on one device may be relied on, other than what follows from the above.
Results may differ from the reference program's by a relative error of at most 0.02.
Values may be sent and summed in bfloat16 or wider, within the bound.
No kernel may reach another device: no remote copies, remote signals or barrier semaphores. Data moves between devices by JAX's collectives and lax.ppermute only.
A program may use at most 64 MiB of HBM per device.

```python
import jax
import jax.numpy as jnp
from jax import lax

C_A = 48
HA = 256
C_O = 40
HO = 128
NF = 8
NB = 2
BC = 128
NW = 64
CAP = 2
RA = 2
WA = 384
NTL = 8
SB = 6
NLAT = 16
NLON = 768
N_LON = 2


def draw_regrid_source_block(key, part):
    key_blocks, key_rolls, key_rates = jax.random.split(key, 3)
    shape = (NTL, N_LON, NTL, CAP)
    blocks = jax.random.randint(key_blocks, shape, 0, SB)
    rolls = jax.random.randint(key_rolls, shape, 0, 8)
    rates = jax.random.randint(key_rates, (NTL, 1, 1, 1), 2, 8)
    source_ids = jnp.arange(NTL, dtype=jnp.int32)[:, None, None, None]
    neighbor_index = jnp.arange(NTL, dtype=jnp.int32)[None, None, :, None]
    forced = neighbor_index == (source_ids + 1) % NTL
    live = (rolls < rates) | forced
    return jnp.where(live, blocks, -1).astype(jnp.int32)


def plant(drawn, rng, smallest, largest):
    longest = drawn.shape.index(max(drawn.shape))
    spots = []
    for shift in (0, 1):
        where = [jax.random.randint(jax.random.fold_in(rng, axis), (), 0, length) for axis, length in enumerate(drawn.shape)]
        where[longest] = (where[longest] + shift) % drawn.shape[longest]
        spots.append(tuple(where))
    return drawn.at[spots[0]].set(smallest).at[spots[1]].set(largest)


def block_levels(rng, dims, cuts, smallest, largest):
    gain, own = 1.0, jax.random.fold_in(rng, 6)
    for dim, shards_of in cuts:
        draws = jnp.exp(jax.random.uniform(jax.random.fold_in(own, dim), (shards_of,), jnp.float32, smallest / len(cuts), largest / len(cuts)))
        gain = gain * jnp.repeat(draws, dims[dim] // shards_of).reshape([-1 if axis == dim else 1 for axis in range(len(dims))])
    return gain


def noise(own_key, extent, scale, limit, shards=(), held_as=jnp.bfloat16):
    result = jax.random.normal(own_key, extent, jnp.float32) * scale
    if len(shards) > 0:
        result = block_levels(own_key, extent, shards, -0.22, 0.18) * result
    return jnp.clip(result, min=-limit, max=limit).astype(held_as)


def setup_inputs(seed: int = 0, part: int = 0) -> dict:
    streams_of = jax.random.split(jax.random.key(seed), 13)
    own_keys = jax.random.split(jax.random.fold_in(streams_of[12], part), 13)
    return {
        "atmos_state": noise(own_keys[0], (C_A, NLAT, NLON), 1.0, 6.0, ((1, 8), (2, 2))),
        "ocean_state": noise(own_keys[1], (C_O, NLAT, NLON), 1.0, 6.0, ((1, 8), (2, 2))),
        "ocean_mask": plant((jax.random.randint(own_keys[2], (NLAT, NLON), 0, 3) < 2).astype(jnp.int32), jax.random.fold_in(own_keys[2], 1), 0, 1),
        "atmos_in_w": noise(streams_of[3], (NB, 9, HA, C_A), (9 * C_A) ** -0.5, 0.3125),
        "atmos_out_w": noise(streams_of[4], (NB, 9, C_A, HA), (9 * HA) ** -0.5, 0.125),
        "ocean_in_w": noise(streams_of[5], (NB, 9, HO, C_O + NF), (9 * (C_O + NF)) ** -0.5, 0.3125),
        "ocean_out_w": noise(streams_of[6], (NB, 9, C_O, HO), (9 * HO) ** -0.5, 0.1875),
        "flux_proj": noise(streams_of[7], (NF, C_A), C_A ** -0.5, 0.875),
        "regrid_blocks": noise(streams_of[8], (NW, BC, BC), BC ** -0.5, 0.5),
        "regrid_source_block": draw_regrid_source_block(jax.random.fold_in(jax.random.fold_in(streams_of[12], part), 71), part),
        "regrid_target_block": plant(jax.random.randint(own_keys[10], (NTL, N_LON, NTL, CAP), 0, SB), jax.random.fold_in(own_keys[10], 1), 0, SB - 1).astype(jnp.int32),
        "regrid_weight_block": plant(jax.random.randint(own_keys[11], (NTL, N_LON, NTL, CAP), 0, NW), jax.random.fold_in(own_keys[11], 1), 0, NW - 1).astype(jnp.int32),
    }


def conv_field(field, taps):
    block_height, block_breadth = field.shape[1], field.shape[2]
    padded = jnp.pad(field.astype(jnp.float32), ((0, 0), (1, 1), (0, 0)))
    padded = jnp.concatenate([padded[:, :, -1:], padded, padded[:, :, :1]], axis=2)
    total = jnp.zeros((taps.shape[1], block_height, block_breadth), jnp.float32)
    for row_tap in range(3):
        for col_tap in range(3):
            window = padded[:, row_tap:row_tap + block_height, col_tap:col_tap + block_breadth]
            total = total + jnp.einsum("hc,crw->hrw", taps[row_tap * 3 + col_tap].astype(jnp.float32), window)
    return total


def conv_block(state, extra, w_in, w_out, wet):
    source = state if extra is None else jnp.concatenate([state, extra], axis=0)
    hidden = jax.nn.gelu(conv_field(source, w_in)).astype(jnp.bfloat16)
    total = state.astype(jnp.float32) + conv_field(hidden, w_out)
    if wet is not None:
        total = total * wet
    return total.astype(jnp.bfloat16)


def grid_into_tiles(field):
    chans = field.shape[0]
    tiles = field.reshape(chans, NTL, RA, N_LON, WA).transpose(1, 3, 0, 2, 4)
    return tiles.reshape(NTL, N_LON, chans, SB, BC)


def tiles_into_grid(tiles):
    chans = tiles.shape[2]
    grid = tiles.reshape(NTL, N_LON, chans, RA, WA).transpose(2, 0, 3, 1, 4)
    return grid.reshape(chans, NTL * RA, N_LON * WA)


def pick_blocks(tiles_lon, index_lon):
    return jnp.take(tiles_lon, index_lon, axis=1)


def reference(atmos_state, ocean_state, ocean_mask, atmos_in_w, atmos_out_w, ocean_in_w, ocean_out_w, flux_proj, regrid_blocks, regrid_source_block, regrid_target_block, regrid_weight_block):
    atmosphere_model = atmos_state
    for layer in range(NB):
        atmosphere_model = conv_block(atmosphere_model, None, atmos_in_w[layer], atmos_out_w[layer], None)
    surface_flux = jnp.einsum("fc,crw->frw", flux_proj.astype(jnp.float32), atmosphere_model.astype(jnp.float32)).astype(jnp.bfloat16)
    flux_tiles = grid_into_tiles(surface_flux).astype(jnp.float32)
    blocks_wide = regrid_blocks.astype(jnp.float32)
    neighbor_index = jnp.arange(NTL, dtype=jnp.int32)[None, :, None]
    longitude_index = jnp.arange(N_LON, dtype=jnp.int32)[:, None, None]

    def send_step(carry, inputs):
        tiles_src, sources, destination_blocks, weights_idx = inputs
        live = sources >= 0
        clipped = jnp.maximum(sources, 0).astype(jnp.int32)
        chosen = jax.vmap(pick_blocks)(tiles_src, clipped)
        collected_values = blocks_wide[weights_idx]
        contrib = jnp.einsum("lfpcb,lpcbd->lpcfd", chosen, collected_values)
        contrib = jnp.where(live[..., None, None], contrib, jnp.zeros((), jnp.float32))
        contrib = lax.optimization_barrier(contrib.astype(jnp.bfloat16)).astype(jnp.float32)
        carry = carry.at[neighbor_index, longitude_index, destination_blocks.astype(jnp.int32)].add(contrib)
        return carry, None

    start = jnp.zeros((NTL, N_LON, SB, NF, BC), jnp.float32)
    received, unused = lax.scan(send_step, start, (flux_tiles, regrid_source_block, regrid_target_block, regrid_weight_block))
    ocean_flux = tiles_into_grid(received.transpose(0, 1, 3, 2, 4)).astype(jnp.bfloat16)

    wet = ocean_mask.astype(jnp.float32)[None]
    ocean_model = (ocean_state.astype(jnp.float32) * wet).astype(jnp.bfloat16)
    for layer in range(NB):
        ocean_model = conv_block(ocean_model, ocean_flux, ocean_in_w[layer], ocean_out_w[layer], wet)

    surface_temp_tile = grid_into_tiles(ocean_model[0:1])[:, :, 0].astype(jnp.float32)

    def return_exchange(carry, inputs):
        sources, destination_blocks, weights_idx = inputs
        live = sources >= 0
        clipped = jnp.maximum(sources, 0).astype(jnp.int32)
        block_values = surface_temp_tile[neighbor_index, longitude_index, destination_blocks.astype(jnp.int32)]
        collected_values = blocks_wide[weights_idx]
        contrib = jnp.einsum("lpcbd,lpcd->lpcb", collected_values, block_values)
        contrib = jnp.where(live[..., None], contrib, jnp.zeros((), jnp.float32))
        local = jnp.zeros((N_LON, SB, BC), jnp.float32).at[longitude_index, clipped].add(contrib)
        return carry, local

    discarded_second, surface_temp_pieces = lax.scan(return_exchange, jnp.zeros((), jnp.float32), (regrid_source_block, regrid_target_block, regrid_weight_block))
    surface_temp_on_atmosphere = tiles_into_grid(surface_temp_pieces[:, :, None])[0]
    return atmosphere_model, ocean_model, surface_temp_on_atmosphere
```

```python
import functools

import jax
import jax.numpy as jnp
from jax import lax
from jax.experimental import pallas as pl
from jax.experimental.pallas import tpu as pltpu
from jax.sharding import PartitionSpec as P

BF = jnp.bfloat16
F32 = jnp.float32
EDGE = 8
STRIP = 4 * EDGE


def with_halo(cells, sides, width):
    for axis, dim in sides:
        count = lax.axis_size(axis)
        head = lax.slice_in_dim(cells, 0, width, axis=dim)
        tail = lax.slice_in_dim(cells, cells.shape[dim] - width, cells.shape[dim], axis=dim)
        cells = jnp.concatenate(
            [
                lax.ppermute(tail, axis, [(i, (i + 1) % count) for i in range(count)]),
                cells,
                lax.ppermute(head, axis, [((i + 1) % count, i) for i in range(count)]),
            ],
            axis=dim,
        )
    return cells


def clear_poles(wide, width):
    block_height = wide.shape[1]
    position = lax.axis_index(("lat", "comp"))
    final = lax.axis_size(("lat", "comp")) - 1
    row_ids = lax.iota(jnp.int32, block_height)
    outside = (position == 0) & (row_ids < width) | (position == final) & (
        row_ids >= block_height - width
    )
    return jnp.where(outside[None, :, None], jnp.zeros((), wide.dtype), wide)


def padded_rims(field):
    wide = with_halo(field, ((("lat", "comp"), 1), ("lon", 2)), 1)
    return clear_poles(wide, 1)


def apply_taps(padded, weights, block_height, block_breadth):
    total = jnp.zeros((weights.shape[1], block_height, block_breadth), jnp.float32)
    for row_tap in range(3):
        for col_tap in range(3):
            window = padded[:, row_tap : row_tap + block_height, col_tap : col_tap + block_breadth]
            total = total + jnp.einsum(
                "hc,crw->hrw",
                weights[row_tap * 3 + col_tap],
                window,
                preferred_element_type=jnp.float32,
            )
    return total


def conv_block(state, extra, w_in, w_out, wet):
    block_height, block_breadth = (state.shape[1], state.shape[2])
    source = state if extra is None else jnp.concatenate([state, extra], axis=0)
    hidden = jax.nn.gelu(apply_taps(padded_rims(source), w_in, block_height, block_breadth)).astype(
        jnp.bfloat16
    )
    hidden = padded_rims(hidden)
    total = state.astype(jnp.float32) + apply_taps(hidden, w_out, block_height, block_breadth)
    if wet is not None:
        total = total * wet
    return total.astype(jnp.bfloat16)


def send_fluxes(block_values, destination_blocks):
    arrived, arrived_targets = (
        lax.all_to_all(block_values, ("lat", "comp"), split_axis=0, concat_axis=0, tiled=True),
        lax.all_to_all(
            destination_blocks, ("lat", "comp"), split_axis=0, concat_axis=0, tiled=True
        ),
    )
    return (arrived, arrived_targets)


def send_back(block_values):
    return lax.all_to_all(block_values, ("lat", "comp"), split_axis=0, concat_axis=0, tiled=True)


def per_device(
    atmos_state,
    ocean_state,
    ocean_mask,
    atmos_in_w,
    atmos_out_w,
    ocean_in_w,
    ocean_out_w,
    flux_proj,
    regrid_blocks,
    regrid_source_block,
    regrid_target_block,
    regrid_weight_block,
):
    block_height, block_breadth = (atmos_state.shape[1], atmos_state.shape[2])
    cells_per_block = regrid_blocks.shape[1]
    subblock_count = block_height * block_breadth // cells_per_block
    peer_count = regrid_source_block.shape[2]
    slot_count = regrid_source_block.shape[3]
    flux_count = flux_proj.shape[0]
    atmosphere_model = atmos_state
    for layer in range(atmos_in_w.shape[0]):
        atmosphere_model = conv_block(
            atmosphere_model, None, atmos_in_w[layer], atmos_out_w[layer], None
        )
    surface_flux = jnp.einsum(
        "fc,crw->frw", flux_proj, atmosphere_model, preferred_element_type=jnp.float32
    ).astype(jnp.bfloat16)
    flux_blocks = surface_flux.reshape(flux_count, subblock_count, cells_per_block)
    sources = regrid_source_block.reshape(peer_count * slot_count)
    destination_blocks = regrid_target_block.reshape(peer_count * slot_count)
    weight_ids = regrid_weight_block.reshape(peer_count * slot_count)
    sub_ids = lax.iota(jnp.int32, subblock_count)
    select_blocks = (sources[:, None] == sub_ids[None, :]).astype(jnp.bfloat16)
    chosen = jnp.einsum(
        "ps,fsb->pfb", select_blocks, flux_blocks, preferred_element_type=jnp.float32
    ).astype(jnp.bfloat16)
    collected_values = jnp.take(regrid_blocks, weight_ids, axis=0)
    contrib = jnp.einsum(
        "pfb,pbd->pfd", chosen, collected_values, preferred_element_type=jnp.float32
    ).astype(jnp.bfloat16)
    arrived, arrived_targets = send_fluxes(
        contrib.reshape(peer_count, slot_count, flux_count, cells_per_block),
        destination_blocks.reshape(peer_count, slot_count),
    )
    place_blocks = (
        arrived_targets.reshape(peer_count * slot_count)[:, None] == sub_ids[None, :]
    ).astype(jnp.bfloat16)
    ocean_flux = jnp.einsum(
        "ps,pfd->fsd",
        place_blocks,
        arrived.reshape(peer_count * slot_count, flux_count, cells_per_block),
        preferred_element_type=jnp.float32,
    )
    ocean_flux = ocean_flux.astype(jnp.bfloat16).reshape(flux_count, block_height, block_breadth)
    wet = ocean_mask.astype(jnp.float32)[None]
    ocean_model = (ocean_state.astype(jnp.float32) * wet).astype(jnp.bfloat16)
    for layer in range(ocean_in_w.shape[0]):
        ocean_model = conv_block(
            ocean_model, ocean_flux, ocean_in_w[layer], ocean_out_w[layer], wet
        )
    surface_temp_block = ocean_model[0].reshape(subblock_count, cells_per_block)
    outgoing = jnp.einsum(
        "qb,be->qe", place_blocks, surface_temp_block, preferred_element_type=jnp.float32
    ).astype(jnp.bfloat16)
    received_back = send_back(outgoing.reshape(peer_count, slot_count, cells_per_block))
    received_back = received_back.reshape(peer_count * slot_count, cells_per_block)
    surface_temp_contributions = jnp.einsum(
        "tge,te->tg", collected_values, received_back, preferred_element_type=jnp.float32
    )
    surface_temp_grid = jnp.einsum(
        "yl,yo->lo",
        select_blocks.astype(jnp.float32),
        surface_temp_contributions,
        preferred_element_type=jnp.float32,
    )
    return (atmosphere_model, ocean_model, surface_temp_grid.reshape(block_height, block_breadth))


def gelu(v):
    u = v * (0.7978845608 + 0.0356774081 * (v * v))
    half = 0.5 * v
    return half + half * jnp.tanh(u)


def west(v):
    return pltpu.roll(v, 1, 1)


def east(v):
    return pltpu.roll(v, v.shape[1] - 1, 1)


def store_row(s_ref, slot, row, chans):
    base = slot * 3 * chans
    if not isinstance(base, int):
        base = pl.multiple_of(base, 16)
    taps = jnp.concatenate([west(row), row, east(row)], axis=0).astype(BF)
    s_ref[pl.ds(base, 3 * chans), :] = taps


def clear_ends(s_ref, rows, chans):
    zero = jnp.zeros((3 * chans, s_ref.shape[1]), BF)
    s_ref[0 : 3 * chans, :] = zero
    s_ref[(rows + 1) * 3 * chans : (rows + 2) * 3 * chans, :] = zero


def column_sum(z, outs):
    return z[outs : 2 * outs] + west(z[0:outs]) + east(z[2 * outs : 3 * outs])


def main_block(s_ref, w_in, w_out, chans, outs, rows, width, emit):
    span = 9 * chans
    ahead, behind = None, None
    for pair in range(rows // 2):
        r = 2 * pair
        taps = jnp.concatenate(
            [
                s_ref[r * 3 * chans : r * 3 * chans + span, :],
                s_ref[(r + 1) * 3 * chans : (r + 1) * 3 * chans + span, :],
            ],
            axis=1,
        )
        hidden = gelu(jnp.dot(w_in, taps, preferred_element_type=F32)).astype(BF)
        z = jnp.dot(w_out, hidden, preferred_element_type=F32)
        part = [
            [z[a * 3 * outs : (a + 1) * 3 * outs, q * width : (q + 1) * width] for q in range(2)]
            for a in range(3)
        ]
        if pair > 0:
            emit(r - 1, column_sum(ahead + part[2][0], outs))
            now = behind + part[1][0] + part[2][1]
        else:
            now = part[1][0] + part[2][1]
        emit(r, column_sum(now, outs))
        ahead = part[0][0] + part[1][1]
        behind = part[0][1]
    emit(rows - 1, column_sum(ahead, outs))


def lanes_of(shape):
    return lax.broadcasted_iota(jnp.int32, shape, len(shape) - 1)


def edges_of(rows):
    shape = (rows[0].shape[0], 128)
    lane = lanes_of(shape)
    total = jnp.zeros(shape, F32)
    for i, row in enumerate(rows):
        at = i * STRIP + EDGE
        left = pltpu.roll(row[:, 0:128], at, 1)
        total = jnp.where((lane >= at) & (lane < at + EDGE), left, total)
        at = at + EDGE
        width = row.shape[1]
        right = pltpu.roll(row[:, width - 128 : width], (at + EDGE) % 128, 1)
        total = jnp.where((lane >= at) & (lane < at + EDGE), right, total)
    return total


def with_neighbour(own, other):
    place = lanes_of(own.shape) % STRIP
    left = pltpu.roll(other, 128 - 2 * EDGE, 1)
    right = pltpu.roll(other, 2 * EDGE, 1)
    return jnp.where(place < EDGE, left, jnp.where(place >= 3 * EDGE, right, own))


def strip_shift(v, a, b):
    width = v.shape[1]
    moved = pltpu.roll(v, (-((a - 1) * STRIP + b - 1)) % width, 1) if (a, b) != (1, 1) else v
    lane = lanes_of(v.shape)
    if a == 0:
        moved = jnp.where(lane < STRIP, 0.0, moved)
    if a == 2:
        moved = jnp.where(lane >= width - STRIP, 0.0, moved)
    return moved


def strip_block(source, w_in, w_out, outs):
    taps = jnp.concatenate(
        [strip_shift(source, a, b) for a in range(3) for b in range(3)], axis=0
    ).astype(BF)
    hidden = gelu(jnp.dot(w_in, taps, preferred_element_type=F32)).astype(BF)
    z = jnp.dot(w_out, hidden, preferred_element_type=F32)
    total = z[4 * outs : 5 * outs]
    for tap in range(9):
        if tap != 4:
            total = total + strip_shift(z[tap * outs : (tap + 1) * outs], tap // 3, tap % 3)
    return total


def mend_row(row, strip, r):
    width = row.shape[1]
    at = (r % 4) * STRIP + EDGE
    lane = lanes_of((row.shape[0], 128))
    left = pltpu.roll(strip, (-at) % 128, 1)
    right = pltpu.roll(strip, (-(at + 2 * EDGE)) % 128, 1)
    head = jnp.where(lane < 4, left, row[:, 0:128])
    tail = jnp.where(lane >= 124, right, row[:, width - 128 : width])
    return jnp.concatenate([head, row[:, 128 : width - 128], tail], axis=1)


def edge_kernel(place_ref, *refs):
    tiles, out_ref = refs[:-1], refs[-1]
    lat, comp = place_ref[0], place_ref[1]
    count = len(tiles) // 2
    for k in range(count):
        near = edges_of([tiles[k][r].astype(F32) for r in range(2)])
        far = edges_of([tiles[count + k][r].astype(F32) for r in range(2)])
        both = pltpu.roll(near, 64 * comp, 1) + pltpu.roll(far, 64 * (1 - comp), 1)
        out_ref[lat ^ k] = both.astype(BF)


def atmos_kernel(place_ref, *refs):
    tiles, (win_ref, wout_ref, out_ref, s0_ref, s1_ref) = refs[:8], refs[8:]
    lat, comp = place_ref[0], place_ref[1]
    rows, chans, width = out_ref.shape
    clear_ends(s0_ref, rows, chans)
    clear_ends(s1_ref, rows, chans)
    for i, tile in enumerate(tiles):
        base = 4 * (lat ^ (i % 4)) + 2 * (comp if i < 4 else 1 - comp)
        for r in range(2):
            store_row(s0_ref, base + r + 1, tile[r].astype(F32), chans)
    stacks = (s0_ref, s1_ref)
    layers = win_ref.shape[0]
    for layer in range(layers):
        source = stacks[layer % 2]

        def emit(r, y):
            base = (3 * (r + 1) + 1) * chans
            total = source[base : base + chans, :].astype(F32) + y
            if layer == layers - 1:
                out_ref[r] = total.astype(BF)
            else:
                store_row(stacks[(layer + 1) % 2], r + 1, total.astype(BF).astype(F32), chans)

        main_block(source, win_ref[layer], wout_ref[layer], chans, chans, rows, width, emit)


def flux_kernel(place_ref, own_ref, other_ref, main_ref, win_ref, wout_ref, proj_ref, blocks_ref,
                *refs):
    tiles = refs[:8]
    next_ref, field_ref, extra_ref, edge_ref, merged, flux, total, table, index, sem = refs[8:]
    lat, comp = place_ref[0], place_ref[1]
    rows, chans, width = main_ref.shape
    fluxes = proj_ref.shape[0]
    per_row = width // 128
    subs = 2 * per_row
    slots = 2 * rows // 2

    for i, tile in enumerate(tiles):
        t = 2 * (lat ^ (i % 4)) + (comp if i < 4 else 1 - comp)
        row = tile[0, 32:48, 0:128].astype(F32)[9:10]
        table[pl.ds(t, 1), :] = row.astype(jnp.int32)
    copy = pltpu.make_async_copy(table, index, sem)
    copy.start()

    strip = jnp.concatenate(
        [
            with_neighbour(own_ref[q].astype(F32), other_ref[q].astype(F32))
            for q in range(own_ref.shape[0])
        ],
        axis=1,
    )
    for layer in range(win_ref.shape[0]):
        strip = strip + strip_block(strip, win_ref[layer], wout_ref[layer], chans)
        strip = strip.astype(BF).astype(F32)

    for r in range(rows):
        q = r // 4
        row = mend_row(main_ref[r].astype(F32), strip[:, 128 * q : 128 * (q + 1)], r).astype(BF)
        merged[r] = row
        f = jnp.dot(proj_ref[...], row, preferred_element_type=F32)
        for b in range(per_row):
            flux[(r // 2) * subs + (r % 2) * per_row + b] = f[:, 128 * b : 128 * (b + 1)].astype(
                BF
            ).astype(F32)
    base = 4 * lat + 2 * comp
    for r in range(2):
        next_ref[r] = merged[base + r]

    total[...] = jnp.zeros(total.shape, F32)
    copy.wait()

    def one_tile(t, carry):
        for slot in range(slots):
            source = index[t, slot]
            live = source >= 0
            target = jnp.where(live, index[t, slots + slot], 6)
            block = blocks_ref[index[t, 2 * slots + slot]]
            value = flux[t * subs + jnp.maximum(source, 0)].astype(BF)
            piece = jnp.dot(value, block, preferred_element_type=F32)
            at = (slot // 2) * 8 + target
            total[at] = total[at] + piece.astype(BF).astype(F32)
        return carry

    lax.fori_loop(0, rows // 2, one_tile, 0)

    for i, tile in enumerate(tiles):
        t = 2 * (lat ^ (i % 4)) + (comp if i < 4 else 1 - comp)
        ends = []
        for r in range(2):
            arrived = jnp.concatenate(
                [total[8 * t + r * per_row + b] for b in range(per_row)], axis=1
            )
            state = tile[r].astype(F32)
            outs = state.shape[0] - fluxes
            row = jnp.concatenate([state[0:outs], arrived], axis=0)
            field_ref[2 * t + r] = row.astype(BF)
            extra_ref[2 * t + r] = state[outs:]
            ends.append(jnp.concatenate([row, state[outs:]], axis=0))
        both = edges_of(ends)
        half = comp if i < 4 else 1 - comp
        edge_ref_at = lat ^ (i % 4)
        moved = pltpu.roll(both, 64 * half, 1)
        if i < 4:
            edge_ref[edge_ref_at] = moved.astype(BF)
        else:
            edge_ref[edge_ref_at] = (edge_ref[edge_ref_at].astype(F32) + moved).astype(BF)


def ocean_kernel(field_ref, extra_ref, win_ref, wout_ref, out_ref, s0_ref, s1_ref):
    rows, chans, width = field_ref.shape
    outs = out_ref.shape[1]
    clear_ends(s0_ref, rows, chans)
    clear_ends(s1_ref, rows, chans)
    for r in range(rows):
        store_row(s0_ref, r + 1, field_ref[r].astype(F32), chans)
    stacks = (s0_ref, s1_ref)
    layers = win_ref.shape[0]
    for layer in range(layers):
        source = stacks[layer % 2]

        def emit(r, y):
            base = (3 * (r + 1) + 1) * chans
            state = source[base : base + chans, :].astype(F32)
            wet = extra_ref[r, 0:1, :]
            total = wet * (state[0:outs] + y)
            if layer == layers - 1:
                out_ref[r] = total.astype(BF)
            else:
                row = jnp.concatenate([total.astype(BF).astype(F32), state[outs:]], axis=0)
                store_row(stacks[(layer + 1) % 2], r + 1, row, chans)

        main_block(source, win_ref[layer], wout_ref[layer], chans, outs, rows, width, emit)


def finish_kernel(place_ref, slots_ref, own_ref, other_ref, main_ref, win_ref, wout_ref, blocks_ref,
                  next_ref, temp_ref, surface, total):
    lat, comp = place_ref[0], place_ref[1]
    rows, outs, width = main_ref.shape
    chans = win_ref.shape[2] // 9
    per_row = width // 128
    strip = jnp.concatenate(
        [
            with_neighbour(own_ref[q].astype(F32), other_ref[q].astype(F32))
            for q in range(own_ref.shape[0])
        ],
        axis=1,
    )
    wet = strip[chans : chans + 1]
    state, fixed = strip[0:outs], strip[outs:chans]
    for layer in range(win_ref.shape[0]):
        source = jnp.concatenate([state, fixed], axis=0)
        state = wet * (state + strip_block(source, win_ref[layer], wout_ref[layer], outs))
        state = state.astype(BF).astype(F32)

    for r in range(rows):
        q = r // 4
        top = mend_row(main_ref[r, 0:16, :].astype(F32)[0:8], state[0:8, 128 * q : 128 * (q + 1)], r)
        for b in range(per_row):
            surface[(r // 2) * 8 + (r % 2) * per_row + b] = top[:, 128 * b : 128 * (b + 1)]

    base = 4 * lat + 2 * comp
    own = jnp.zeros((outs, 128), F32)
    for q in range(own_ref.shape[0]):
        own = jnp.where(lat == q, state[:, 128 * q : 128 * (q + 1)], own)
    own = pltpu.roll(own, jnp.where(comp == 1, 64, 0), 1)
    for r in range(2):
        next_ref[r] = mend_row(main_ref[base + r].astype(F32), own, r).astype(BF)

    total[...] = jnp.zeros(total.shape, F32)
    slots = slots_ref.shape[1]
    for slot in range(slots):
        source = slots_ref[0, slot]
        target = slots_ref[1, slot]
        block = blocks_ref[slots_ref[2, slot]]
        value = surface[(slot // 2) * 8 + target].astype(BF)
        piece = lax.dot_general(value, block, (((1,), (1,)), ((), ())), preferred_element_type=F32)
        at = jnp.where(source >= 0, source, 6)
        total[at] = total[at] + piece
    for r in range(2):
        temp_ref[r : r + 1, :] = jnp.concatenate(
            [total[r * per_row + b][0:1] for b in range(per_row)], axis=1
        )


def call(kernel, out_shape, operands, scratch=(), smem=1, flops=0):
    specs = [
        pl.BlockSpec(memory_space=pltpu.SMEM if i < smem else pltpu.VMEM)
        for i in range(len(operands))
    ]
    out_specs = jax.tree.map(lambda _: pl.BlockSpec(memory_space=pltpu.VMEM), out_shape)
    return pl.pallas_call(
        kernel,
        out_shape=out_shape,
        in_specs=specs,
        out_specs=out_specs,
        scratch_shapes=list(scratch),
        compiler_params=pltpu.CompilerParams(vmem_limit_bytes=40 * 2**20),
        cost_estimate=pl.CostEstimate(flops=flops, bytes_accessed=2**20, transcendentals=0),
    )(*operands)


def column_device(
    atmos_state,
    ocean_state,
    ocean_mask,
    atmos_in_w,
    atmos_out_w,
    ocean_in_w,
    ocean_out_w,
    flux_proj,
    regrid_blocks,
    regrid_source_block,
    regrid_target_block,
    regrid_weight_block,
):
    chans, height, width = atmos_state.shape
    outs = ocean_state.shape[0]
    lats = lax.axis_size("lat")
    tiles = lats * lax.axis_size("comp")
    rows = tiles * height
    layers, _, hidden_a, _ = atmos_in_w.shape
    hidden_o = ocean_in_w.shape[2]
    fluxes = flux_proj.shape[0]
    place = jnp.stack([lax.axis_index("lat"), lax.axis_index("comp")]).astype(jnp.int32)

    def far(v, k):
        return lax.ppermute(v, "lat", [(i, i ^ k) for i in range(lats)])

    def swap(v, axis):
        return lax.ppermute(v, axis, [(0, 1), (1, 0)])

    def column(mine):
        near = [mine] + [far(mine, k) for k in range(1, lats)]
        return near + [swap(v, "comp") for v in near]

    atmos = column(jnp.transpose(atmos_state, (1, 0, 2)))

    slots = jnp.stack(
        [
            v.reshape(-1)
            for v in (regrid_source_block, regrid_target_block, regrid_weight_block)
        ]
    )
    index_row = jnp.pad(slots.reshape(-1).astype(BF), (0, width - slots.size))
    wet = ocean_mask.astype(BF)[:, None, :]
    payload = jnp.concatenate(
        [
            jnp.transpose(ocean_state, (1, 0, 2)) * wet,
            wet,
            jnp.broadcast_to(index_row[None, None], (height, 1, width)),
            jnp.zeros((height, 6, width), BF),
        ],
        axis=1,
    )
    ocean = column(payload)

    def taps_in(w):
        return jnp.transpose(w, (0, 2, 1, 3)).reshape(w.shape[0], w.shape[2], 9 * w.shape[3])

    def taps_out(w):
        return w.reshape(w.shape[0], 9 * w.shape[2], w.shape[3])

    win_a, wout_a = taps_in(atmos_in_w), taps_out(atmos_out_w)
    win_o, wout_o = taps_in(ocean_in_w), taps_out(ocean_out_w)

    def conv_flops(hidden, outs):
        return 2 * layers * rows * width * 9 * hidden * (chans + outs)

    edges = call(edge_kernel, jax.ShapeDtypeStruct((lats, chans, 128), BF), [place, *atmos])
    edges_other = swap(edges, "lon")
    stack = (rows + 2) * 3 * chans
    main = call(
        atmos_kernel,
        jax.ShapeDtypeStruct((rows, chans, width), BF),
        [place, *atmos, win_a, wout_a],
        [pltpu.VMEM((stack, width), BF), pltpu.VMEM((stack, width), BF)],
        flops=conv_flops(hidden_a, chans),
    )
    subs = height * width // 128
    atmos_next, field, extra, ocean_edges = call(
        flux_kernel,
        (
            jax.ShapeDtypeStruct((height, chans, width), BF),
            jax.ShapeDtypeStruct((rows, chans, width), BF),
            jax.ShapeDtypeStruct((rows, fluxes, width), F32),
            jax.ShapeDtypeStruct((lats, chans + fluxes, 128), BF),
        ),
        [place, edges, edges_other, main, win_a, wout_a, flux_proj, regrid_blocks, *ocean],
        [
            pltpu.VMEM((rows, chans, width), BF),
            pltpu.VMEM((tiles * subs, fluxes, 128), F32),
            pltpu.VMEM((tiles * 8, fluxes, 128), F32),
            pltpu.VMEM((tiles, 128), jnp.int32),
            pltpu.SMEM((tiles, 128), jnp.int32),
            pltpu.SemaphoreType.DMA,
        ],
    )
    ocean_edges_other = swap(ocean_edges, "lon")
    ocean_main = call(
        ocean_kernel,
        jax.ShapeDtypeStruct((rows, outs, width), BF),
        [field, extra, win_o, wout_o],
        [pltpu.VMEM((stack, width), BF), pltpu.VMEM((stack, width), BF)],
        smem=0,
        flops=conv_flops(hidden_o, outs),
    )
    ocean_next, surface_temp = call(
        finish_kernel,
        (
            jax.ShapeDtypeStruct((height, outs, width), BF),
            jax.ShapeDtypeStruct((height, width), F32),
        ),
        [place, slots, ocean_edges, ocean_edges_other, ocean_main, win_o, wout_o, regrid_blocks],
        [pltpu.VMEM((tiles * 8, 8, 128), F32), pltpu.VMEM((8, 8, 128), F32)],
        smem=2,
    )
    return (
        jnp.transpose(atmos_next, (1, 0, 2)),
        jnp.transpose(ocean_next, (1, 0, 2)),
        surface_temp,
    )


def solution(mesh):
    in_specs = (
        P(None, ("grp", "lat", "comp"), "lon"),
        P(None, ("grp", "lat", "comp"), "lon"),
        P(("grp", "lat", "comp"), "lon"),
        P(),
        P(),
        P(),
        P(),
        P(),
        P(),
        P(("grp", "lat", "comp"), "lon", None, None),
        P(("grp", "lat", "comp"), "lon", None, None),
        P(("grp", "lat", "comp"), "lon", None, None),
    )
    out_specs = (
        P(None, ("grp", "lat", "comp"), "lon"),
        P(None, ("grp", "lat", "comp"), "lon"),
        P(("grp", "lat", "comp"), "lon"),
    )
    shape = mesh.shape
    short = (shape["lat"], shape["comp"], shape["lon"]) == (4, 2, 2)
    return jax.shard_map(
        column_device if short else per_device,
        mesh=mesh,
        in_specs=in_specs,
        out_specs=out_specs,
        check_vma=False,
    )
```

```python
import functools

import jax
import jax.numpy as jnp
from jax import lax
from jax.experimental import pallas as pl
from jax.experimental.pallas import tpu as pltpu
from jax.sharding import PartitionSpec as P

BF = jnp.bfloat16
F32 = jnp.float32
EDGE = 8
STRIP = 4 * EDGE


def with_halo(cells, sides, width):
    for axis, dim in sides:
        count = lax.axis_size(axis)
        head = lax.slice_in_dim(cells, 0, width, axis=dim)
        tail = lax.slice_in_dim(cells, cells.shape[dim] - width, cells.shape[dim], axis=dim)
        cells = jnp.concatenate(
            [
                lax.ppermute(tail, axis, [(i, (i + 1) % count) for i in range(count)]),
                cells,
                lax.ppermute(head, axis, [((i + 1) % count, i) for i in range(count)]),
            ],
            axis=dim,
        )
    return cells


def clear_poles(wide, width):
    block_height = wide.shape[1]
    position = lax.axis_index(("lat", "comp"))
    final = lax.axis_size(("lat", "comp")) - 1
    row_ids = lax.iota(jnp.int32, block_height)
    outside = (position == 0) & (row_ids < width) | (position == final) & (
        row_ids >= block_height - width
    )
    return jnp.where(outside[None, :, None], jnp.zeros((), wide.dtype), wide)


def padded_rims(field):
    wide = with_halo(field, ((("lat", "comp"), 1), ("lon", 2)), 1)
    return clear_poles(wide, 1)


def apply_taps(padded, weights, block_height, block_breadth):
    total = jnp.zeros((weights.shape[1], block_height, block_breadth), jnp.float32)
    for row_tap in range(3):
        for col_tap in range(3):
            window = padded[:, row_tap : row_tap + block_height, col_tap : col_tap + block_breadth]
            total = total + jnp.einsum(
                "hc,crw->hrw",
                weights[row_tap * 3 + col_tap],
                window,
                preferred_element_type=jnp.float32,
            )
    return total


def conv_block(state, extra, w_in, w_out, wet):
    block_height, block_breadth = (state.shape[1], state.shape[2])
    source = state if extra is None else jnp.concatenate([state, extra], axis=0)
    hidden = jax.nn.gelu(apply_taps(padded_rims(source), w_in, block_height, block_breadth)).astype(
        jnp.bfloat16
    )
    hidden = padded_rims(hidden)
    total = state.astype(jnp.float32) + apply_taps(hidden, w_out, block_height, block_breadth)
    if wet is not None:
        total = total * wet
    return total.astype(jnp.bfloat16)


def send_fluxes(block_values, destination_blocks):
    arrived, arrived_targets = (
        lax.all_to_all(block_values, ("lat", "comp"), split_axis=0, concat_axis=0, tiled=True),
        lax.all_to_all(
            destination_blocks, ("lat", "comp"), split_axis=0, concat_axis=0, tiled=True
        ),
    )
    return (arrived, arrived_targets)


def send_back(block_values):
    return lax.all_to_all(block_values, ("lat", "comp"), split_axis=0, concat_axis=0, tiled=True)


def per_device(
    atmos_state,
    ocean_state,
    ocean_mask,
    atmos_in_w,
    atmos_out_w,
    ocean_in_w,
    ocean_out_w,
    flux_proj,
    regrid_blocks,
    regrid_source_block,
    regrid_target_block,
    regrid_weight_block,
):
    block_height, block_breadth = (atmos_state.shape[1], atmos_state.shape[2])
    cells_per_block = regrid_blocks.shape[1]
    subblock_count = block_height * block_breadth // cells_per_block
    peer_count = regrid_source_block.shape[2]
    slot_count = regrid_source_block.shape[3]
    flux_count = flux_proj.shape[0]
    atmosphere_model = atmos_state
    for layer in range(atmos_in_w.shape[0]):
        atmosphere_model = conv_block(
            atmosphere_model, None, atmos_in_w[layer], atmos_out_w[layer], None
        )
    surface_flux = jnp.einsum(
        "fc,crw->frw", flux_proj, atmosphere_model, preferred_element_type=jnp.float32
    ).astype(jnp.bfloat16)
    flux_blocks = surface_flux.reshape(flux_count, subblock_count, cells_per_block)
    sources = regrid_source_block.reshape(peer_count * slot_count)
    destination_blocks = regrid_target_block.reshape(peer_count * slot_count)
    weight_ids = regrid_weight_block.reshape(peer_count * slot_count)
    sub_ids = lax.iota(jnp.int32, subblock_count)
    select_blocks = (sources[:, None] == sub_ids[None, :]).astype(jnp.bfloat16)
    chosen = jnp.einsum(
        "ps,fsb->pfb", select_blocks, flux_blocks, preferred_element_type=jnp.float32
    ).astype(jnp.bfloat16)
    collected_values = jnp.take(regrid_blocks, weight_ids, axis=0)
    contrib = jnp.einsum(
        "pfb,pbd->pfd", chosen, collected_values, preferred_element_type=jnp.float32
    ).astype(jnp.bfloat16)
    arrived, arrived_targets = send_fluxes(
        contrib.reshape(peer_count, slot_count, flux_count, cells_per_block),
        destination_blocks.reshape(peer_count, slot_count),
    )
    place_blocks = (
        arrived_targets.reshape(peer_count * slot_count)[:, None] == sub_ids[None, :]
    ).astype(jnp.bfloat16)
    ocean_flux = jnp.einsum(
        "ps,pfd->fsd",
        place_blocks,
        arrived.reshape(peer_count * slot_count, flux_count, cells_per_block),
        preferred_element_type=jnp.float32,
    )
    ocean_flux = ocean_flux.astype(jnp.bfloat16).reshape(flux_count, block_height, block_breadth)
    wet = ocean_mask.astype(jnp.float32)[None]
    ocean_model = (ocean_state.astype(jnp.float32) * wet).astype(jnp.bfloat16)
    for layer in range(ocean_in_w.shape[0]):
        ocean_model = conv_block(
            ocean_model, ocean_flux, ocean_in_w[layer], ocean_out_w[layer], wet
        )
    surface_temp_block = ocean_model[0].reshape(subblock_count, cells_per_block)
    outgoing = jnp.einsum(
        "qb,be->qe", place_blocks, surface_temp_block, preferred_element_type=jnp.float32
    ).astype(jnp.bfloat16)
    received_back = send_back(outgoing.reshape(peer_count, slot_count, cells_per_block))
    received_back = received_back.reshape(peer_count * slot_count, cells_per_block)
    surface_temp_contributions = jnp.einsum(
        "tge,te->tg", collected_values, received_back, preferred_element_type=jnp.float32
    )
    surface_temp_grid = jnp.einsum(
        "yl,yo->lo",
        select_blocks.astype(jnp.float32),
        surface_temp_contributions,
        preferred_element_type=jnp.float32,
    )
    return (atmosphere_model, ocean_model, surface_temp_grid.reshape(block_height, block_breadth))


def gelu(v):
    u = v * (0.7978845608 + 0.0356774081 * (v * v))
    half = 0.5 * v
    return half + half * jnp.tanh(u)


def west(v):
    return pltpu.roll(v, 1, 1)


def east(v):
    return pltpu.roll(v, v.shape[1] - 1, 1)


def store_row(s_ref, slot, row, chans):
    base = slot * 3 * chans
    if not isinstance(base, int):
        base = pl.multiple_of(base, 16)
    taps = jnp.concatenate([west(row), row, east(row)], axis=0).astype(BF)
    s_ref[pl.ds(base, 3 * chans), :] = taps


def clear_ends(s_ref, rows, chans):
    zero = jnp.zeros((3 * chans, s_ref.shape[1]), BF)
    s_ref[0 : 3 * chans, :] = zero
    s_ref[(rows + 1) * 3 * chans : (rows + 2) * 3 * chans, :] = zero


def column_sum(z, outs):
    return z[outs : 2 * outs] + west(z[0:outs]) + east(z[2 * outs : 3 * outs])


def main_block(s_ref, w_in, w_out, chans, outs, rows, width, emit):
    span = 9 * chans
    ahead, behind = None, None
    for pair in range(rows // 2):
        r = 2 * pair
        taps = jnp.concatenate(
            [
                s_ref[r * 3 * chans : r * 3 * chans + span, :],
                s_ref[(r + 1) * 3 * chans : (r + 1) * 3 * chans + span, :],
            ],
            axis=1,
        )
        hidden = gelu(jnp.dot(w_in, taps, preferred_element_type=F32)).astype(BF)
        z = jnp.dot(w_out, hidden, preferred_element_type=F32)
        part = [
            [z[a * 3 * outs : (a + 1) * 3 * outs, q * width : (q + 1) * width] for q in range(2)]
            for a in range(3)
        ]
        if pair > 0:
            emit(r - 1, column_sum(ahead + part[2][0], outs))
            now = behind + part[1][0] + part[2][1]
        else:
            now = part[1][0] + part[2][1]
        emit(r, column_sum(now, outs))
        ahead = part[0][0] + part[1][1]
        behind = part[0][1]
    emit(rows - 1, column_sum(ahead, outs))


def turned(w_ref, layer):
    return jnp.transpose(w_ref[layer])


def lanes_of(shape):
    return lax.broadcasted_iota(jnp.int32, shape, len(shape) - 1)


def edges_of(rows):
    shape = (rows[0].shape[0], 128)
    lane = lanes_of(shape)
    total = jnp.zeros(shape, F32)
    for i, row in enumerate(rows):
        at = i * STRIP + EDGE
        left = pltpu.roll(row[:, 0:128], at, 1)
        total = jnp.where((lane >= at) & (lane < at + EDGE), left, total)
        at = at + EDGE
        width = row.shape[1]
        right = pltpu.roll(row[:, width - 128 : width], (at + EDGE) % 128, 1)
        total = jnp.where((lane >= at) & (lane < at + EDGE), right, total)
    return total


def with_neighbour(own, other):
    place = lanes_of(own.shape) % STRIP
    left = pltpu.roll(other, 128 - 2 * EDGE, 1)
    right = pltpu.roll(other, 2 * EDGE, 1)
    return jnp.where(place < EDGE, left, jnp.where(place >= 3 * EDGE, right, own))


def strip_shift(v, a, b):
    width = v.shape[1]
    moved = pltpu.roll(v, (-((a - 1) * STRIP + b - 1)) % width, 1) if (a, b) != (1, 1) else v
    lane = lanes_of(v.shape)
    if a == 0:
        moved = jnp.where(lane < STRIP, 0.0, moved)
    if a == 2:
        moved = jnp.where(lane >= width - STRIP, 0.0, moved)
    return moved


def strip_block(source, w_in, w_out, outs):
    taps = jnp.concatenate(
        [strip_shift(source, a, b) for a in range(3) for b in range(3)], axis=0
    ).astype(BF)
    hidden = gelu(jnp.dot(w_in, taps, preferred_element_type=F32)).astype(BF)
    z = jnp.dot(w_out, hidden, preferred_element_type=F32)
    total = z[4 * outs : 5 * outs]
    for tap in range(9):
        if tap != 4:
            total = total + strip_shift(z[tap * outs : (tap + 1) * outs], tap // 3, tap % 3)
    return total


def mend_row(row, strip, r):
    width = row.shape[1]
    at = (r % 4) * STRIP + EDGE
    lane = lanes_of((row.shape[0], 128))
    left = pltpu.roll(strip, (-at) % 128, 1)
    right = pltpu.roll(strip, (-(at + 2 * EDGE)) % 128, 1)
    head = jnp.where(lane < 4, left, row[:, 0:128])
    tail = jnp.where(lane >= 124, right, row[:, width - 128 : width])
    return jnp.concatenate([head, row[:, 128 : width - 128], tail], axis=1)


def pack_atmos_kernel(atmos_ref, tile_ref):
    for r in range(tile_ref.shape[0]):
        tile_ref[r] = atmos_ref[:, r, :]


def pack_ocean_kernel(source_hbm, target_hbm, weight_hbm, ocean_hbm, mask_hbm, tile_ref, source_ref,
                      target_ref, weight_ref, ocean_ref, mask_ref, sems):
    given = (source_hbm, target_hbm, weight_hbm, ocean_hbm, mask_hbm)
    numbers = (source_ref, target_ref, weight_ref)
    held = (*numbers, ocean_ref, mask_ref)
    copies = [pltpu.make_async_copy(v, h, sems.at[i]) for i, (v, h) in enumerate(zip(given, held))]
    for copy in copies:
        copy.start()
    for copy in copies:
        copy.wait()
    height, span, width = tile_ref.shape
    slots, peers = source_ref.shape[2:]
    listed = [ref[0, 0, s : s + 1, :].astype(F32) for ref in numbers for s in range(slots)]
    listed.append(jnp.zeros((1, width - len(listed) * peers), F32))
    listed = jnp.concatenate(listed, axis=1)
    rest = jnp.zeros((span - ocean_ref.shape[0] - 2, width), F32)
    for r in range(height):
        wet = mask_ref[r : r + 1, :].astype(F32)
        state = ocean_ref[:, r, :].astype(F32) * wet
        tile_ref[r] = jnp.concatenate([state, wet, listed, rest], axis=0).astype(BF)


def stack_kernel(place_ref, *refs):
    tiles, (stack_ref, edge_ref) = refs[:8], refs[8:]
    lat, comp = place_ref[0], place_ref[1]
    chans, width = tiles[0].shape[1:]
    chips = edge_ref.shape[0]
    clear_ends(stack_ref, 4 * chips, chans)
    for k in range(chips):
        both = jnp.zeros((chans, 128), F32)
        for half, tile in ((comp, tiles[k]), (1 - comp, tiles[chips + k])):
            pair = [tile[r].astype(F32) for r in range(2)]
            for r in range(2):
                store_row(stack_ref, 4 * (lat ^ k) + 2 * half + r + 1, pair[r], chans)
            both = both + pltpu.roll(edges_of(pair), 64 * half, 1)
        edge_ref[lat ^ k] = both.astype(BF)


def first_kernel(stack_ref, win_ref, wout_ref, next_ref):
    chans = wout_ref.shape[1] // 9
    width = stack_ref.shape[1]
    rows = stack_ref.shape[0] // (3 * chans) - 2
    clear_ends(next_ref, rows, chans)

    def emit(r, y):
        base = (3 * (r + 1) + 1) * chans
        total = stack_ref[base : base + chans, :].astype(F32) + y
        store_row(next_ref, r + 1, total.astype(BF).astype(F32), chans)

    main_block(stack_ref, turned(win_ref, 0), wout_ref[0], chans, chans, rows, width, emit)


def second_kernel(place_ref, stack_ref, win_ref, wout_ref, *refs):
    ocean_tiles, (out_ref, ocean_ref, sems) = refs[:4], refs[4:]
    lat = place_ref[0]
    rows, chans, width = out_ref.shape
    copies = [
        pltpu.make_async_copy(tile, ocean_ref.at[lat ^ k], sems.at[k])
        for k, tile in enumerate(ocean_tiles)
    ]
    for copy in copies:
        copy.start()

    def emit(r, y):
        base = (3 * (r + 1) + 1) * chans
        out_ref[r] = (stack_ref[base : base + chans, :].astype(F32) + y).astype(BF)

    main_block(stack_ref, turned(win_ref, 1), wout_ref[1], chans, chans, rows, width, emit)
    for copy in copies:
        copy.wait()


def flux_kernel(place_ref, own_ref, other_ref, main_ref, win_ref, wout_ref, proj_ref, next_ref,
                flux_ref, merged):
    lat, comp = place_ref[0], place_ref[1]
    rows, chans, width = main_ref.shape
    per_row = width // 128
    strip = jnp.concatenate(
        [
            with_neighbour(own_ref[q].astype(F32), other_ref[q].astype(F32))
            for q in range(own_ref.shape[0])
        ],
        axis=1,
    )
    for layer in range(win_ref.shape[0]):
        strip = strip + strip_block(strip, turned(win_ref, layer), wout_ref[layer], chans)
        strip = strip.astype(BF).astype(F32)

    for r in range(rows):
        q = r // 4
        row = mend_row(main_ref[r].astype(F32), strip[:, 128 * q : 128 * (q + 1)], r).astype(BF)
        merged[r] = row
        f = jnp.dot(proj_ref[...], row, preferred_element_type=F32)
        for b in range(per_row):
            flux_ref[r * per_row + b] = f[:, 128 * b : 128 * (b + 1)].astype(BF).astype(F32)
    base = 4 * lat + 2 * comp
    for r in range(2):
        next_ref[:, r, :] = merged[base + r]


def regrid_kernel(place_ref, flux_ref, blocks_ref, near_ref, far_ref, field_ref, extra_ref,
                  edge_ref, table, total, index, sem):
    comp = place_ref[1]
    chips = near_ref.shape[0]
    rows, chans, width = field_ref.shape
    fluxes = flux_ref.shape[1]
    outs = chans - fluxes
    per_row = width // 128
    subs = 2 * per_row
    peers = 2 * chips
    slots = rows

    for chip in range(chips):
        for near, tiles in ((0, near_ref), (1, far_ref)):
            t = 2 * chip + jnp.where(comp == near, 0, 1)
            row = tiles[chip, 0, 32:48, 0:128].astype(F32)[9:10]
            table[pl.ds(t, 1), :] = row.astype(jnp.int32)
    copy = pltpu.make_async_copy(table, index, sem)
    copy.start()
    total[...] = jnp.zeros(total.shape, F32)
    copy.wait()

    def one_tile(t, carry):
        for slot in range(slots):
            source = index[t, slot]
            live = source >= 0
            target = jnp.where(live, index[t, slots + slot], 6)
            block = blocks_ref[index[t, 2 * slots + slot]]
            value = flux_ref[t * subs + jnp.maximum(source, 0)].astype(BF)
            piece = jnp.dot(value, block, preferred_element_type=F32)
            at = (slot % peers) * 8 + target
            total[at] = total[at] + piece.astype(BF).astype(F32)
        return carry

    lax.fori_loop(0, rows // 2, one_tile, 0)

    for chip in range(chips):
        both = jnp.zeros((chans + fluxes, 128), F32)
        for near, tiles in ((0, near_ref), (1, far_ref)):
            half = jnp.where(comp == near, 0, 1)
            t = 2 * chip + half
            ends = []
            for r in range(2):
                arrived = jnp.concatenate(
                    [total[8 * t + r * per_row + b] for b in range(per_row)], axis=1
                )
                state = tiles[chip, r].astype(F32)
                row = jnp.concatenate([state[0:outs], arrived], axis=0)
                field_ref[2 * t + r] = row.astype(BF)
                extra_ref[2 * t + r] = state[outs:]
                ends.append(jnp.concatenate([row, state[outs:]], axis=0))
            both = both + pltpu.roll(edges_of(ends), 64 * half, 1)
        edge_ref[chip] = both.astype(BF)


def ocean_kernel(field_ref, extra_ref, win_ref, wout_ref, out_ref, s0_ref, s1_ref):
    rows, chans, width = field_ref.shape
    outs = out_ref.shape[1]
    clear_ends(s0_ref, rows, chans)
    clear_ends(s1_ref, rows, chans)
    for r in range(rows):
        store_row(s0_ref, r + 1, field_ref[r].astype(F32), chans)
    stacks = (s0_ref, s1_ref)
    layers = win_ref.shape[0]
    for layer in range(layers):
        source = stacks[layer % 2]

        def emit(r, y):
            base = (3 * (r + 1) + 1) * chans
            state = source[base : base + chans, :].astype(F32)
            wet = extra_ref[r, 0:1, :]
            total = wet * (state[0:outs] + y)
            if layer == layers - 1:
                out_ref[r] = total.astype(BF)
            else:
                row = jnp.concatenate([total.astype(BF).astype(F32), state[outs:]], axis=0)
                store_row(stacks[(layer + 1) % 2], r + 1, row, chans)

        main_block(source, turned(win_ref, layer), wout_ref[layer], chans, outs, rows, width, emit)


def finish_kernel(place_ref, table_ref, own_ref, other_ref, main_ref, win_ref, wout_ref, blocks_ref,
                  next_ref, temp_ref, surface, total, index, sem):
    copy = pltpu.make_async_copy(table_ref, index, sem)
    copy.start()
    lat, comp = place_ref[0], place_ref[1]
    rows, outs, width = main_ref.shape
    chans = win_ref.shape[1] // 9
    per_row = width // 128
    strip = jnp.concatenate(
        [
            with_neighbour(own_ref[q].astype(F32), other_ref[q].astype(F32))
            for q in range(own_ref.shape[0])
        ],
        axis=1,
    )
    wet = strip[chans : chans + 1]
    state, fixed = strip[0:outs], strip[outs:chans]
    for layer in range(win_ref.shape[0]):
        source = jnp.concatenate([state, fixed], axis=0)
        state = wet * (state + strip_block(source, turned(win_ref, layer), wout_ref[layer], outs))
        state = state.astype(BF).astype(F32)

    for r in range(rows):
        q = r // 4
        top = mend_row(main_ref[r, 0:16, :].astype(F32)[0:8], state[0:8, 128 * q : 128 * (q + 1)], r)
        for b in range(per_row):
            surface[(r // 2) * 8 + (r % 2) * per_row + b] = top[:, 128 * b : 128 * (b + 1)]

    base = 4 * lat + 2 * comp
    own = jnp.zeros((outs, 128), F32)
    for q in range(own_ref.shape[0]):
        own = jnp.where(lat == q, state[:, 128 * q : 128 * (q + 1)], own)
    own = pltpu.roll(own, jnp.where(comp == 1, 64, 0), 1)
    for r in range(2):
        next_ref[:, r, :] = mend_row(main_ref[base + r].astype(F32), own, r).astype(BF)

    total[...] = jnp.zeros(total.shape, F32)
    copy.wait()
    slots = rows
    t = 2 * lat + comp
    for slot in range(slots):
        source = index[t, slot]
        target = index[t, slots + slot]
        block = blocks_ref[index[t, 2 * slots + slot]]
        value = surface[(slot % (rows // 2)) * 8 + target].astype(BF)
        piece = lax.dot_general(value, block, (((1,), (1,)), ((), ())), preferred_element_type=F32)
        at = jnp.where(source >= 0, source, 6)
        total[at] = total[at] + piece
    for r in range(2):
        temp_ref[r : r + 1, :] = jnp.concatenate(
            [total[r * per_row + b][0:1] for b in range(per_row)], axis=1
        )


def call(kernel, out_shape, operands, scratch=(), smem=1, anywhere=0, flops=0):
    held = len(operands) - smem - anywhere
    spaces = [pltpu.SMEM] * smem + [pltpu.VMEM] * held + [pltpu.HBM] * anywhere
    specs = [pl.BlockSpec(memory_space=space) for space in spaces]
    out_specs = jax.tree.map(lambda _: pl.BlockSpec(memory_space=pltpu.VMEM), out_shape)
    return pl.pallas_call(
        kernel,
        out_shape=out_shape,
        in_specs=specs,
        out_specs=out_specs,
        scratch_shapes=list(scratch),
        compiler_params=pltpu.CompilerParams(vmem_limit_bytes=40 * 2**20),
        cost_estimate=pl.CostEstimate(flops=flops, bytes_accessed=2**20, transcendentals=0),
    )(*operands)


def column_device(
    atmos_state,
    ocean_state,
    ocean_mask,
    atmos_in_w,
    atmos_out_w,
    ocean_in_w,
    ocean_out_w,
    flux_proj,
    regrid_blocks,
    regrid_source_block,
    regrid_target_block,
    regrid_weight_block,
):
    chans, height, width = atmos_state.shape
    outs = ocean_state.shape[0]
    lats = lax.axis_size("lat")
    tiles = lats * lax.axis_size("comp")
    rows = tiles * height
    layers, _, hidden_a, _ = atmos_in_w.shape
    hidden_o = ocean_in_w.shape[2]
    fluxes = flux_proj.shape[0]
    place = jnp.stack([lax.axis_index("lat"), lax.axis_index("comp")]).astype(jnp.int32)

    def far(v, k):
        return lax.ppermute(v, "lat", [(i, i ^ k) for i in range(lats)])

    def swap(v, axis):
        return lax.ppermute(v, axis, [(0, 1), (1, 0)])

    def conv_flops(hidden, outs):
        return 2 * layers * rows * width * 9 * hidden * (chans + outs)

    tile = jax.ShapeDtypeStruct((height, chans, width), BF)
    atmos_tile = call(pack_atmos_kernel, tile, [atmos_state], smem=0)
    slots = (regrid_source_block, regrid_target_block, regrid_weight_block)
    given = [*(jnp.transpose(v, (0, 1, 3, 2)) for v in slots), ocean_state, ocean_mask]
    ocean_tile = call(
        pack_ocean_kernel,
        tile,
        given,
        [*(pltpu.VMEM(v.shape, v.dtype) for v in given), pltpu.SemaphoreType.DMA((len(given),))],
        smem=0,
        anywhere=len(given),
    )
    near = [atmos_tile] + [far(atmos_tile, k) for k in range(1, lats)]
    column = near + [swap(v, "comp") for v in near]
    ocean_near = [ocean_tile] + [far(ocean_tile, k) for k in range(1, lats)]

    def taps_in(w):
        return jnp.transpose(w, (0, 1, 3, 2)).reshape(w.shape[0], 9 * w.shape[3], w.shape[2])

    def taps_out(w):
        return w.reshape(w.shape[0], 9 * w.shape[2], w.shape[3])

    win_a, wout_a = taps_in(atmos_in_w), taps_out(atmos_out_w)
    win_o, wout_o = taps_in(ocean_in_w), taps_out(ocean_out_w)

    stack = (rows + 2) * 3 * chans
    stack_shape = jax.ShapeDtypeStruct((stack, width), BF)
    atmos_stack, edges = call(
        stack_kernel,
        (stack_shape, jax.ShapeDtypeStruct((lats, chans, 128), BF)),
        [place, *column],
        flops=conv_flops(hidden_a, chans),
    )
    edges_other = swap(edges, "lon")
    atmos_stack = call(
        first_kernel,
        stack_shape,
        [atmos_stack, win_a, wout_a],
        smem=0,
        flops=4 * conv_flops(hidden_a, chans),
    )
    main, ocean_near = call(
        second_kernel,
        (
            jax.ShapeDtypeStruct((rows, chans, width), BF),
            jax.ShapeDtypeStruct((lats, height, chans, width), BF),
        ),
        [place, atmos_stack, win_a, wout_a, *ocean_near],
        [pltpu.SemaphoreType.DMA((lats,))],
        flops=4 * conv_flops(hidden_a, chans),
        anywhere=lats,
    )
    ocean_far = swap(ocean_near, "comp")
    subs = height * width // 128
    atmos_next, flux = call(
        flux_kernel,
        (
            jax.ShapeDtypeStruct((chans, height, width), BF),
            jax.ShapeDtypeStruct((tiles * subs, fluxes, 128), F32),
        ),
        [place, edges, edges_other, main, win_a, wout_a, flux_proj],
        [pltpu.VMEM((rows, chans, width), BF)],
        flops=4 * conv_flops(hidden_a, chans),
    )
    field, extra, ocean_edges, table = call(
        regrid_kernel,
        (
            jax.ShapeDtypeStruct((rows, chans, width), BF),
            jax.ShapeDtypeStruct((rows, fluxes, width), F32),
            jax.ShapeDtypeStruct((lats, chans + fluxes, 128), BF),
            jax.ShapeDtypeStruct((tiles, 128), jnp.int32),
        ),
        [place, flux, regrid_blocks, ocean_near, ocean_far],
        [
            pltpu.VMEM((tiles * 8, fluxes, 128), F32),
            pltpu.SMEM((tiles, 128), jnp.int32),
            pltpu.SemaphoreType.DMA,
        ],
    )
    ocean_edges_other = swap(ocean_edges, "lon")
    ocean_main = call(
        ocean_kernel,
        jax.ShapeDtypeStruct((rows, outs, width), BF),
        [field, extra, win_o, wout_o],
        [pltpu.VMEM((stack, width), BF), pltpu.VMEM((stack, width), BF)],
        smem=0,
        flops=4 * conv_flops(hidden_o, outs),
    )
    ocean_next, surface_temp = call(
        finish_kernel,
        (
            jax.ShapeDtypeStruct((outs, height, width), BF),
            jax.ShapeDtypeStruct((height, width), F32),
        ),
        [place, table, ocean_edges, ocean_edges_other, ocean_main, win_o, wout_o, regrid_blocks],
        [
            pltpu.VMEM((tiles * 8, 8, 128), F32),
            pltpu.VMEM((8, 8, 128), F32),
            pltpu.SMEM((tiles, 128), jnp.int32),
            pltpu.SemaphoreType.DMA,
        ],
    )
    return atmos_next, ocean_next, surface_temp


def solution(mesh):
    in_specs = (
        P(None, ("grp", "lat", "comp"), "lon"),
        P(None, ("grp", "lat", "comp"), "lon"),
        P(("grp", "lat", "comp"), "lon"),
        P(),
        P(),
        P(),
        P(),
        P(),
        P(),
        P(("grp", "lat", "comp"), "lon", None, None),
        P(("grp", "lat", "comp"), "lon", None, None),
        P(("grp", "lat", "comp"), "lon", None, None),
    )
    out_specs = (
        P(None, ("grp", "lat", "comp"), "lon"),
        P(None, ("grp", "lat", "comp"), "lon"),
        P(("grp", "lat", "comp"), "lon"),
    )
    shape = mesh.shape
    short = (shape["lat"], shape["comp"], shape["lon"]) == (4, 2, 2)
    return jax.shard_map(
        column_device if short else per_device,
        mesh=mesh,
        in_specs=in_specs,
        out_specs=out_specs,
        check_vma=False,
    )
```

```python
import functools

import jax
import jax.numpy as jnp
from jax import lax
from jax.experimental import pallas as pl
from jax.experimental.pallas import tpu as pltpu
from jax.sharding import PartitionSpec as P

BF = jnp.bfloat16
F32 = jnp.float32
EDGE = 8
STRIP = 4 * EDGE


def with_halo(cells, sides, width):
    for axis, dim in sides:
        count = lax.axis_size(axis)
        head = lax.slice_in_dim(cells, 0, width, axis=dim)
        tail = lax.slice_in_dim(cells, cells.shape[dim] - width, cells.shape[dim], axis=dim)
        cells = jnp.concatenate(
            [
                lax.ppermute(tail, axis, [(i, (i + 1) % count) for i in range(count)]),
                cells,
                lax.ppermute(head, axis, [((i + 1) % count, i) for i in range(count)]),
            ],
            axis=dim,
        )
    return cells


def clear_poles(wide, width):
    block_height = wide.shape[1]
    position = lax.axis_index(("lat", "comp"))
    final = lax.axis_size(("lat", "comp")) - 1
    row_ids = lax.iota(jnp.int32, block_height)
    outside = (position == 0) & (row_ids < width) | (position == final) & (
        row_ids >= block_height - width
    )
    return jnp.where(outside[None, :, None], jnp.zeros((), wide.dtype), wide)


def padded_rims(field):
    wide = with_halo(field, ((("lat", "comp"), 1), ("lon", 2)), 1)
    return clear_poles(wide, 1)


def apply_taps(padded, weights, block_height, block_breadth):
    total = jnp.zeros((weights.shape[1], block_height, block_breadth), jnp.float32)
    for row_tap in range(3):
        for col_tap in range(3):
            window = padded[:, row_tap : row_tap + block_height, col_tap : col_tap + block_breadth]
            total = total + jnp.einsum(
                "hc,crw->hrw",
                weights[row_tap * 3 + col_tap],
                window,
                preferred_element_type=jnp.float32,
            )
    return total


def conv_block(state, extra, w_in, w_out, wet):
    block_height, block_breadth = (state.shape[1], state.shape[2])
    source = state if extra is None else jnp.concatenate([state, extra], axis=0)
    hidden = jax.nn.gelu(apply_taps(padded_rims(source), w_in, block_height, block_breadth)).astype(
        jnp.bfloat16
    )
    hidden = padded_rims(hidden)
    total = state.astype(jnp.float32) + apply_taps(hidden, w_out, block_height, block_breadth)
    if wet is not None:
        total = total * wet
    return total.astype(jnp.bfloat16)


def send_fluxes(block_values, destination_blocks):
    arrived, arrived_targets = (
        lax.all_to_all(block_values, ("lat", "comp"), split_axis=0, concat_axis=0, tiled=True),
        lax.all_to_all(
            destination_blocks, ("lat", "comp"), split_axis=0, concat_axis=0, tiled=True
        ),
    )
    return (arrived, arrived_targets)


def send_back(block_values):
    return lax.all_to_all(block_values, ("lat", "comp"), split_axis=0, concat_axis=0, tiled=True)


def per_device(
    atmos_state,
    ocean_state,
    ocean_mask,
    atmos_in_w,
    atmos_out_w,
    ocean_in_w,
    ocean_out_w,
    flux_proj,
    regrid_blocks,
    regrid_source_block,
    regrid_target_block,
    regrid_weight_block,
):
    block_height, block_breadth = (atmos_state.shape[1], atmos_state.shape[2])
    cells_per_block = regrid_blocks.shape[1]
    subblock_count = block_height * block_breadth // cells_per_block
    peer_count = regrid_source_block.shape[2]
    slot_count = regrid_source_block.shape[3]
    flux_count = flux_proj.shape[0]
    atmosphere_model = atmos_state
    for layer in range(atmos_in_w.shape[0]):
        atmosphere_model = conv_block(
            atmosphere_model, None, atmos_in_w[layer], atmos_out_w[layer], None
        )
    surface_flux = jnp.einsum(
        "fc,crw->frw", flux_proj, atmosphere_model, preferred_element_type=jnp.float32
    ).astype(jnp.bfloat16)
    flux_blocks = surface_flux.reshape(flux_count, subblock_count, cells_per_block)
    sources = regrid_source_block.reshape(peer_count * slot_count)
    destination_blocks = regrid_target_block.reshape(peer_count * slot_count)
    weight_ids = regrid_weight_block.reshape(peer_count * slot_count)
    sub_ids = lax.iota(jnp.int32, subblock_count)
    select_blocks = (sources[:, None] == sub_ids[None, :]).astype(jnp.bfloat16)
    chosen = jnp.einsum(
        "ps,fsb->pfb", select_blocks, flux_blocks, preferred_element_type=jnp.float32
    ).astype(jnp.bfloat16)
    collected_values = jnp.take(regrid_blocks, weight_ids, axis=0)
    contrib = jnp.einsum(
        "pfb,pbd->pfd", chosen, collected_values, preferred_element_type=jnp.float32
    ).astype(jnp.bfloat16)
    arrived, arrived_targets = send_fluxes(
        contrib.reshape(peer_count, slot_count, flux_count, cells_per_block),
        destination_blocks.reshape(peer_count, slot_count),
    )
    place_blocks = (
        arrived_targets.reshape(peer_count * slot_count)[:, None] == sub_ids[None, :]
    ).astype(jnp.bfloat16)
    ocean_flux = jnp.einsum(
        "ps,pfd->fsd",
        place_blocks,
        arrived.reshape(peer_count * slot_count, flux_count, cells_per_block),
        preferred_element_type=jnp.float32,
    )
    ocean_flux = ocean_flux.astype(jnp.bfloat16).reshape(flux_count, block_height, block_breadth)
    wet = ocean_mask.astype(jnp.float32)[None]
    ocean_model = (ocean_state.astype(jnp.float32) * wet).astype(jnp.bfloat16)
    for layer in range(ocean_in_w.shape[0]):
        ocean_model = conv_block(
            ocean_model, ocean_flux, ocean_in_w[layer], ocean_out_w[layer], wet
        )
    surface_temp_block = ocean_model[0].reshape(subblock_count, cells_per_block)
    outgoing = jnp.einsum(
        "qb,be->qe", place_blocks, surface_temp_block, preferred_element_type=jnp.float32
    ).astype(jnp.bfloat16)
    received_back = send_back(outgoing.reshape(peer_count, slot_count, cells_per_block))
    received_back = received_back.reshape(peer_count * slot_count, cells_per_block)
    surface_temp_contributions = jnp.einsum(
        "tge,te->tg", collected_values, received_back, preferred_element_type=jnp.float32
    )
    surface_temp_grid = jnp.einsum(
        "yl,yo->lo",
        select_blocks.astype(jnp.float32),
        surface_temp_contributions,
        preferred_element_type=jnp.float32,
    )
    return (atmosphere_model, ocean_model, surface_temp_grid.reshape(block_height, block_breadth))


def gelu(v):
    u = v * (0.7978845608 + 0.0356774081 * (v * v))
    half = 0.5 * v
    return half + half * jnp.tanh(u)


def west(v):
    return pltpu.roll(v, 1, 1)


def east(v):
    return pltpu.roll(v, v.shape[1] - 1, 1)


def store_row(s_ref, slot, row, chans):
    base = slot * 3 * chans
    if not isinstance(base, int):
        base = pl.multiple_of(base, 16)
    taps = jnp.concatenate([west(row), row, east(row)], axis=0).astype(BF)
    s_ref[pl.ds(base, 3 * chans), :] = taps


def clear_ends(s_ref, rows, chans):
    zero = jnp.zeros((3 * chans, s_ref.shape[1]), BF)
    s_ref[0 : 3 * chans, :] = zero
    s_ref[(rows + 1) * 3 * chans : (rows + 2) * 3 * chans, :] = zero


def column_sum(z, outs):
    return z[outs : 2 * outs] + west(z[0:outs]) + east(z[2 * outs : 3 * outs])


def main_block(s_ref, w_in, w_out, outs, rows, width, emit, shift=1, valid=None):
    chans = w_in.shape[1] // 9
    span = 9 * chans
    ahead, behind = None, None
    for r in rows[::2]:
        at = [(r + q - 1 + shift) * 3 * chans for q in range(2)]
        taps = jnp.concatenate([s_ref[i : i + span, :] for i in at], axis=1)
        hidden = gelu(jnp.dot(w_in, taps, preferred_element_type=F32))
        if valid is not None:
            kept = [jnp.full((1, width), valid(r + q), F32) for q in range(2)]
            hidden = hidden * jnp.concatenate(kept, axis=1)
        z = jnp.dot(w_out, hidden.astype(BF), preferred_element_type=F32)
        part = [
            [z[a * 3 * outs : (a + 1) * 3 * outs, q * width : (q + 1) * width] for q in range(2)]
            for a in range(3)
        ]
        if ahead is not None:
            emit(r - 1, column_sum(ahead + part[2][0], outs))
            emit(r, column_sum(behind + part[1][0] + part[2][1], outs))
        elif valid is None:
            emit(r, column_sum(part[1][0] + part[2][1], outs))
        ahead = part[0][0] + part[1][1]
        behind = part[0][1]
    if valid is None:
        emit(rows[-1], column_sum(ahead, outs))


def turned(w_ref, layer):
    return jnp.transpose(w_ref[layer])


def lanes_of(shape):
    return lax.broadcasted_iota(jnp.int32, shape, len(shape) - 1)


def edges_of(rows):
    shape = (rows[0].shape[0], 128)
    lane = lanes_of(shape)
    total = jnp.zeros(shape, F32)
    for i, row in enumerate(rows):
        at = i * STRIP + EDGE
        left = pltpu.roll(row[:, 0:128], at, 1)
        total = jnp.where((lane >= at) & (lane < at + EDGE), left, total)
        at = at + EDGE
        width = row.shape[1]
        right = pltpu.roll(row[:, width - 128 : width], (at + EDGE) % 128, 1)
        total = jnp.where((lane >= at) & (lane < at + EDGE), right, total)
    return total


def with_neighbour(own, other):
    place = lanes_of(own.shape) % STRIP
    left = pltpu.roll(other, 128 - 2 * EDGE, 1)
    right = pltpu.roll(other, 2 * EDGE, 1)
    return jnp.where(place < EDGE, left, jnp.where(place >= 3 * EDGE, right, own))


def strip_shift(v, a, b, poles):
    width = v.shape[1]
    moved = pltpu.roll(v, (-((a - 1) * STRIP + b - 1)) % width, 1) if (a, b) != (1, 1) else v
    lane = lanes_of(v.shape)
    if poles and a == 0:
        moved = jnp.where(lane < STRIP, 0.0, moved)
    if poles and a == 2:
        moved = jnp.where(lane >= width - STRIP, 0.0, moved)
    return moved


def strip_block(source, w_in, w_out, outs, kept=None):
    poles = kept is None
    taps = jnp.concatenate(
        [strip_shift(source, a, b, poles) for a in range(3) for b in range(3)], axis=0
    ).astype(BF)
    hidden = gelu(jnp.dot(w_in, taps, preferred_element_type=F32))
    if not poles:
        hidden = hidden * kept
    z = jnp.dot(w_out, hidden.astype(BF), preferred_element_type=F32)
    total = z[4 * outs : 5 * outs]
    for tap in range(9):
        if tap != 4:
            total = total + strip_shift(z[tap * outs : (tap + 1) * outs], tap // 3, tap % 3, poles)
    return total


def mend_row(row, strip, r):
    width = row.shape[1]
    at = (r % 4) * STRIP + EDGE
    lane = lanes_of((row.shape[0], 128))
    left = pltpu.roll(strip, (-at) % 128, 1)
    right = pltpu.roll(strip, (-(at + 2 * EDGE)) % 128, 1)
    head = jnp.where(lane < 4, left, row[:, 0:128])
    tail = jnp.where(lane >= 124, right, row[:, width - 128 : width])
    return jnp.concatenate([head, row[:, 128 : width - 128], tail], axis=1)


def pack_atmos_kernel(atmos_ref, tile_ref):
    for r in range(tile_ref.shape[0]):
        tile_ref[r] = atmos_ref[:, r, :]


def pack_ocean_kernel(source_hbm, target_hbm, weight_hbm, ocean_hbm, mask_hbm, tile_ref, source_ref,
                      target_ref, weight_ref, ocean_ref, mask_ref, sems):
    given = (source_hbm, target_hbm, weight_hbm, ocean_hbm, mask_hbm)
    numbers = (source_ref, target_ref, weight_ref)
    held = (*numbers, ocean_ref, mask_ref)
    copies = [pltpu.make_async_copy(v, h, sems.at[i]) for i, (v, h) in enumerate(zip(given, held))]
    for copy in copies:
        copy.start()
    for copy in copies:
        copy.wait()
    height, span, width = tile_ref.shape
    slots, peers = source_ref.shape[2:]
    listed = [ref[0, 0, s : s + 1, :].astype(F32) for ref in numbers for s in range(slots)]
    listed.append(jnp.zeros((1, width - len(listed) * peers), F32))
    listed = jnp.concatenate(listed, axis=1)
    rest = jnp.zeros((span - ocean_ref.shape[0] - 2, width), F32)
    for r in range(height):
        wet = mask_ref[r : r + 1, :].astype(F32)
        state = ocean_ref[:, r, :].astype(F32) * wet
        tile_ref[r] = jnp.concatenate([state, wet, listed, rest], axis=0).astype(BF)


def stack_kernel(place_ref, own_ref, side_ref, cross_ref, even_ref, odd_ref, stack_ref, edge_ref):
    lat, comp = place_ref[0], place_ref[1]
    chans, width = own_ref.shape[1:]
    low = lat % 2 == 0
    places = (
        (own_ref, 2),
        (side_ref, 3 - 2 * comp),
        (cross_ref, 1 + 2 * comp),
        (even_ref, jnp.where(low, 4, 0)),
        (odd_ref, jnp.where(low, 0, 4)),
    )
    for tile, at in places:
        for r in range(2):
            store_row(stack_ref, 2 * at + r, tile[r].astype(F32), chans)
    for q in range(edge_ref.shape[0]):
        both = jnp.zeros((chans, 128), F32)
        for half in range(2):
            r = 4 * q + 2 * half
            if r < stack_ref.shape[0] // (3 * chans):
                at = [(3 * (r + i) + 1) * chans for i in range(2)]
                ends = edges_of([stack_ref[i : i + chans, :].astype(F32) for i in at])
                both = both + pltpu.roll(ends, 64 * half, 1)
        edge_ref[q] = both.astype(BF)


def centre(ref, slot, chans):
    at = (3 * slot + 1) * chans
    if not isinstance(at, int):
        at = pl.multiple_of(at, 16)
    return ref[pl.ds(at, chans), :].astype(F32)


def window_rule(place_ref):
    first = 4 * place_ref[0] + 2 * place_ref[1] - 4
    limit = place_ref[2]
    return first, lambda r: jnp.where((first + r >= 0) & (first + r < limit), 1.0, 0.0)


def strip_of(own_ref, other_ref):
    tiles = range(own_ref.shape[0])
    both = [with_neighbour(own_ref[q].astype(F32), other_ref[q].astype(F32)) for q in tiles]
    return jnp.concatenate(both, axis=1)


def first_kernel(place_ref, stack_ref, win_ref, wout_ref, next_ref):
    chans, width = wout_ref.shape[1] // 9, stack_ref.shape[1]
    valid = window_rule(place_ref)[1]

    def keep(r, y):
        total = (centre(stack_ref, r, chans) + y).astype(BF).astype(F32)
        store_row(next_ref, r, total * valid(r), chans)

    main_block(stack_ref, turned(win_ref, 0), wout_ref[0], chans, range(1, 9), width, keep, 0, valid)


def second_kernel(place_ref, stack_ref, own_ref, other_ref, win_ref, wout_ref, proj_ref, ocean_ref,
                  next_ref, sent_ref):
    chans, width = wout_ref.shape[1] // 9, stack_ref.shape[1]
    per_row = width // 128
    first, valid = window_rule(place_ref)
    w_in = [turned(win_ref, layer) for layer in range(2)]
    main = {}

    def finish(r, y):
        main[r - 4] = (centre(stack_ref, r, chans) + y).astype(BF).astype(F32)

    strip = strip_of(own_ref, other_ref)
    lane = lanes_of((1, strip.shape[1]))
    inside = (lane >= -first * STRIP) & (lane < (place_ref[2] - first) * STRIP)
    kept = jnp.where(inside, 1.0, 0.0)
    strip = strip + strip_block(strip, w_in[0], wout_ref[0], chans, kept)
    strip = strip.astype(BF).astype(F32) * kept
    main_block(stack_ref, w_in[1], wout_ref[1], chans, range(3, 7), width, finish, 0, valid)
    strip = strip + strip_block(strip, w_in[1], wout_ref[1], chans, kept)

    mended = [mend_row(main[r], strip[:, 128:256], r).astype(BF) for r in range(2)]
    for r in range(2):
        next_ref[:, r, :] = mended[r]
    flux = jnp.dot(proj_ref[...], jnp.concatenate(mended, axis=1), preferred_element_type=F32)
    blocks = [flux[:, 128 * b : 128 * (b + 1)] for b in range(2 * per_row)]
    numbers = ocean_ref[0, 32:48, 0:128].astype(F32)[9:10]
    rest = jnp.zeros((15, 128), F32)
    head = jnp.concatenate([*blocks, numbers, rest], axis=0).astype(BF)
    at = head.shape[0]
    sent_ref[0:at, :] = head
    for r in range(2):
        for b in range(per_row):
            sent_ref[at : at + chans, :] = ocean_ref[r, :, 128 * b : 128 * (b + 1)]
            at = at + chans


def regrid_kernel(place_ref, blocks_ref, atmos_ref, *refs):
    sent, (stack_ref, wet_ref, edge_ref, table, next_hbm, flux_ref, total, index, sem, next_sem) = (
        refs[:8],
        refs[8:],
    )
    leaving = pltpu.make_async_copy(atmos_ref, next_hbm, next_sem)
    leaving.start()
    lat, comp = place_ref[0], place_ref[1]
    peers = len(sent)
    chips = peers // 2
    fluxes = flux_ref.shape[1]
    subs = flux_ref.shape[0] // peers
    per_row = subs // 2
    rows = wet_ref.shape[0]
    chans = stack_ref.shape[0] // (3 * (rows + 2))
    outs = chans - fluxes
    slots = 2 * peers
    places = [2 * (lat ^ (i % chips)) + (comp if i < chips else 1 - comp) for i in range(peers)]
    head = subs * fluxes + 16
    for t, ref in zip(places, sent):
        row = ref[head - 16 : head, :].astype(F32)[0:1]
        table[pl.ds(t, 1), :] = row.astype(jnp.int32)
    copy = pltpu.make_async_copy(table, index, sem)
    copy.start()
    total[...] = jnp.zeros(total.shape, F32)
    for t, ref in zip(places, sent):
        values = ref[0 : head - 16, :].astype(F32)
        for b in range(subs):
            flux_ref[t * subs + b] = values[b * fluxes : (b + 1) * fluxes]
    clear_ends(stack_ref, rows, chans)
    copy.wait()

    def one_tile(t, carry):
        pieces = []
        for slot in range(slots):
            source = jnp.maximum(index[t, slot], 0)
            block = blocks_ref[index[t, 2 * slots + slot]]
            value = flux_ref[t * subs + source].astype(BF)
            piece = jnp.dot(value, block, preferred_element_type=F32)
            pieces.append(piece.astype(BF).astype(F32))
        for slot in range(slots):
            target = jnp.where(index[t, slot] >= 0, index[t, slots + slot], 6)
            at = (slot % peers) * 8 + target
            total[at] = total[at] + pieces[slot]
        return carry

    lax.fori_loop(0, peers, one_tile, 0, unroll=2)

    def tile_row(ref, r):
        at = [head + (r * per_row + b) * chans for b in range(per_row)]
        return jnp.concatenate([ref[i : i + chans, :] for i in at], axis=1).astype(F32)

    for k in range(chips):
        both = jnp.zeros((chans + fluxes, 128), F32)
        for i in (k, chips + k):
            t = places[i]
            ends = []
            for r in range(2):
                arrived = jnp.concatenate(
                    [total[8 * t + r * per_row + b] for b in range(per_row)], axis=1
                )
                state = tile_row(sent[i], r)
                row = jnp.concatenate([state[0:outs], arrived.astype(BF).astype(F32)], axis=0)
                store_row(stack_ref, 2 * t + r + 1, row, chans)
                wet_ref[2 * t + r] = state[outs:]
                ends.append(jnp.concatenate([row, state[outs:]], axis=0))
            both = both + pltpu.roll(edges_of(ends), 64 * (comp if i < chips else 1 - comp), 1)
        edge_ref[lat ^ k] = both.astype(BF)
    leaving.wait()


def ocean_kernel(stack_ref, wet_ref, win_ref, wout_ref, next_ref):
    chans, outs = win_ref.shape[1] // 9, wout_ref.shape[1] // 9
    rows, width = wet_ref.shape[0], stack_ref.shape[1]
    clear_ends(next_ref, rows, chans)

    def emit(r, y):
        state = centre(stack_ref, r + 1, chans)
        total = (wet_ref[r, 0:1, :] * (state[0:outs] + y)).astype(BF).astype(F32)
        store_row(next_ref, r + 1, jnp.concatenate([total, state[outs:]], axis=0), chans)

    main_block(stack_ref, turned(win_ref, 0), wout_ref[0], outs, range(rows), width, emit)


def finish_kernel(place_ref, table_ref, stack_ref, wet_ref, own_ref, other_ref, win_ref, wout_ref,
                  blocks_ref, next_ref, temp_ref, hidden_ref, surface, total, index, sem):
    copy = pltpu.make_async_copy(table_ref, index, sem)
    copy.start()
    lat, comp = place_ref[0], place_ref[1]
    t = 2 * lat + comp
    chans, outs = win_ref.shape[1] // 9, wout_ref.shape[1] // 9
    hidden = win_ref.shape[2]
    rows, width = wet_ref.shape[0], stack_ref.shape[1]
    per_row = width // 128
    w_in = [turned(win_ref, layer) for layer in range(2)]
    total[...] = jnp.zeros(total.shape, F32)

    strip = strip_of(own_ref, other_ref)
    wet = strip[chans : chans + 1]
    state, fixed = strip[0:outs], strip[outs:chans]
    state = wet * (state + strip_block(strip[0:chans], w_in[0], wout_ref[0], outs))
    state = state.astype(BF).astype(F32)

    last = wout_ref[1].astype(F32)
    none = jnp.zeros((5, hidden), F32)
    w_temp = jnp.concatenate(
        [v for a in range(3) for v in (*(last[(3 * a + b) * outs][None] for b in range(3)), none)]
        + [jnp.zeros((8, hidden), F32)],
        axis=0,
    ).astype(BF)
    ends = jnp.zeros((hidden, width), BF)
    hidden_ref[0] = ends
    hidden_ref[rows + 1] = ends
    parts = {}
    for r in range(0, rows, 2):
        at = [(r + q) * 3 * chans for q in range(2)]
        taps = jnp.concatenate([stack_ref[i : i + 9 * chans, :] for i in at], axis=1)
        active = gelu(jnp.dot(w_in[1], taps, preferred_element_type=F32)).astype(BF)
        for q in range(2):
            hidden_ref[r + q + 1] = active[:, q * width : (q + 1) * width]
        z = jnp.dot(w_temp, active, preferred_element_type=F32)
        for a in range(3):
            for q in range(2):
                part = z[8 * a : 8 * a + 8, q * width : (q + 1) * width]
                row = r + q - a + 1
                parts[row] = parts[row] + part if row in parts else part

    source = jnp.concatenate([state, fixed], axis=0)
    state = wet * (state + strip_block(source, w_in[1], wout_ref[1], outs))
    state = state.astype(BF).astype(F32)

    for r in range(rows):
        y = parts[r]
        y = y[1:2] + west(y)[0:1] + east(y)[2:3]
        top = wet_ref[r, 0:1, :] * (centre(stack_ref, r + 1, chans)[0:8] + y)
        q = r // 4
        top = mend_row(top, state[0:8, 128 * q : 128 * (q + 1)], r)
        for b in range(per_row):
            surface[(r // 2) * 8 + (r % 2) * per_row + b] = top[:, 128 * b : 128 * (b + 1)]

    edge = jnp.zeros((outs, 128), F32)
    for q in range(own_ref.shape[0]):
        edge = jnp.where(lat == q, state[:, 128 * q : 128 * (q + 1)], edge)
    edge = pltpu.roll(edge, jnp.where(comp == 1, 64, 0), 1)
    z = [
        jnp.dot(
            wout_ref[1],
            jnp.concatenate([hidden_ref[2 * t + 2 * p + q] for q in range(2)], axis=1),
            preferred_element_type=F32,
        )
        for p in range(2)
    ]
    for r in range(2):
        y = sum(
            z[(r + a) // 2][
                3 * a * outs : 3 * (a + 1) * outs, (r + a) % 2 * width : ((r + a) % 2 + 1) * width
            ]
            for a in range(3)
        )
        row = centre(stack_ref, 2 * t + r + 1, chans)[0:outs] + column_sum(y, outs)
        next_ref[:, r, :] = mend_row(wet_ref[2 * t + r, 0:1, :] * row, edge, r).astype(BF)

    copy.wait()
    peers = rows // 2
    slots = 2 * peers
    for slot in range(slots):
        source = index[t, slot]
        target = index[t, slots + slot]
        block = blocks_ref[index[t, 2 * slots + slot]]
        value = surface[(slot % peers) * 8 + target].astype(BF)
        piece = lax.dot_general(value, block, (((1,), (1,)), ((), ())), preferred_element_type=F32)
        at = jnp.where(source >= 0, source, 6)
        total[at] = total[at] + piece
    for r in range(2):
        temp_ref[r : r + 1, :] = jnp.concatenate(
            [total[r * per_row + b][0:1] for b in range(per_row)], axis=1
        )


def call(kernel, out_shape, operands, scratch=(), smem=1, anywhere=0, flops=0, leaving=None):
    held = len(operands) - smem - anywhere
    spaces = [pltpu.SMEM] * smem + [pltpu.VMEM] * held + [pltpu.HBM] * anywhere
    out_specs = jax.tree.map(lambda _: pl.BlockSpec(memory_space=pltpu.VMEM), out_shape)
    if leaving is not None:
        out_shape = (*out_shape, leaving)
        out_specs = (*out_specs, pl.BlockSpec(memory_space=pl.ANY))
    return pl.pallas_call(
        kernel,
        out_shape=out_shape,
        in_specs=[pl.BlockSpec(memory_space=space) for space in spaces],
        out_specs=out_specs,
        scratch_shapes=list(scratch),
        compiler_params=pltpu.CompilerParams(vmem_limit_bytes=40 * 2**20),
        cost_estimate=pl.CostEstimate(flops=flops, bytes_accessed=2**20, transcendentals=0),
    )(*operands)


def column_device(
    atmos_state,
    ocean_state,
    ocean_mask,
    atmos_in_w,
    atmos_out_w,
    ocean_in_w,
    ocean_out_w,
    flux_proj,
    regrid_blocks,
    regrid_source_block,
    regrid_target_block,
    regrid_weight_block,
):
    chans, height, width = atmos_state.shape
    outs = ocean_state.shape[0]
    lats = lax.axis_size("lat")
    tiles = lats * lax.axis_size("comp")
    rows = tiles * height
    layers, _, hidden_a, _ = atmos_in_w.shape
    hidden_o = ocean_in_w.shape[2]
    fluxes = flux_proj.shape[0]
    place = jnp.stack([lax.axis_index("lat"), lax.axis_index("comp"), rows]).astype(jnp.int32)

    def far(v, k):
        return lax.ppermute(v, "lat", [(i, i ^ k) for i in range(lats)])

    def swap(v, axis):
        return lax.ppermute(v, axis, [(0, 1), (1, 0)])

    def conv_flops(hidden, outs):
        return 2 * layers * rows * width * 9 * hidden * (chans + outs)

    tile = jax.ShapeDtypeStruct((height, chans, width), BF)
    atmos_tile = call(
        pack_atmos_kernel, tile, [atmos_state], smem=0, flops=conv_flops(hidden_a, chans)
    )
    slots = (regrid_source_block, regrid_target_block, regrid_weight_block)
    given = [*(jnp.transpose(v, (0, 1, 3, 2)) for v in slots), ocean_state, ocean_mask]
    ocean_tile = call(
        pack_ocean_kernel,
        tile,
        given,
        [*(pltpu.VMEM(v.shape, v.dtype) for v in given), pltpu.SemaphoreType.DMA((len(given),))],
        smem=0,
        anywhere=len(given),
    )
    cross = [(i, i + 1) for i in range(1, tiles - 1, 2)]
    odd = [(i, i + 1) for i in range(1, lats - 1, 2)]

    def both_ways(pairs):
        return pairs + [(j, i) for i, j in pairs]

    near = [
        atmos_tile,
        swap(atmos_tile, "comp"),
        lax.ppermute(atmos_tile, ("lat", "comp"), both_ways(cross)),
        far(atmos_tile, 1),
        lax.ppermute(atmos_tile, "lat", both_ways(odd)),
    ]
    def taps_in(w):
        return jnp.transpose(w, (0, 1, 3, 2)).reshape(w.shape[0], 9 * w.shape[3], w.shape[2])

    def taps_out(w):
        return w.reshape(w.shape[0], 9 * w.shape[2], w.shape[3])

    win_a, wout_a = taps_in(atmos_in_w), taps_out(atmos_out_w)
    win_o, wout_o = taps_in(ocean_in_w), taps_out(ocean_out_w)

    window = height * len(near)
    stack_shape = (window * 3 * chans, width)
    atmos_stack, edges = call(
        stack_kernel,
        (
            jax.ShapeDtypeStruct(stack_shape, BF),
            jax.ShapeDtypeStruct((pl.cdiv(window * STRIP, 128), chans, 128), BF),
        ),
        [place, *near],
        flops=conv_flops(hidden_a, chans),
    )
    edges_other = swap(edges, "lon")
    atmos_stack = call(
        first_kernel,
        jax.ShapeDtypeStruct(stack_shape, BF),
        [place, atmos_stack, win_a, wout_a],
        flops=4 * conv_flops(hidden_a, chans),
    )
    subs = height * width // 128
    atmos_next, sent = call(
        second_kernel,
        (
            jax.ShapeDtypeStruct((chans, height, width), BF),
            jax.ShapeDtypeStruct((subs * (fluxes + chans) + 16, 128), BF),
        ),
        [place, atmos_stack, edges, edges_other, win_a, wout_a, flux_proj, ocean_tile],
        flops=4 * conv_flops(hidden_a, chans),
    )
    others = {k: far(sent, k) for k in reversed(range(1, lats))}
    sent = [sent] + [others[k] for k in range(1, lats)]
    sent = sent + [swap(v, "comp") for v in sent]
    stack_shape = ((rows + 2) * 3 * chans, width)
    ocean_stack, wet, ocean_edges, table, atmos_next = call(
        regrid_kernel,
        (
            jax.ShapeDtypeStruct(stack_shape, BF),
            jax.ShapeDtypeStruct((rows, fluxes, width), F32),
            jax.ShapeDtypeStruct((lats, chans + fluxes, 128), BF),
            jax.ShapeDtypeStruct((tiles, 128), jnp.int32),
        ),
        [place, regrid_blocks, atmos_next, *sent],
        [
            pltpu.VMEM((tiles * subs, fluxes, 128), F32),
            pltpu.VMEM((tiles * 8, fluxes, 128), F32),
            pltpu.SMEM((tiles, 128), jnp.int32),
            pltpu.SemaphoreType.DMA,
            pltpu.SemaphoreType.DMA,
        ],
        flops=conv_flops(hidden_o, outs),
        leaving=jax.ShapeDtypeStruct((chans, height, width), BF),
    )
    ocean_edges_other = swap(ocean_edges, "lon")
    ocean_stack = call(
        ocean_kernel,
        jax.ShapeDtypeStruct(stack_shape, BF),
        [ocean_stack, wet, win_o, wout_o],
        smem=0,
        flops=4 * conv_flops(hidden_o, outs),
    )
    ocean_next, surface_temp = call(
        finish_kernel,
        (
            jax.ShapeDtypeStruct((outs, height, width), BF),
            jax.ShapeDtypeStruct((height, width), F32),
        ),
        [
            place,
            table,
            ocean_stack,
            wet,
            ocean_edges,
            ocean_edges_other,
            win_o,
            wout_o,
            regrid_blocks,
        ],
        [
            pltpu.VMEM((rows + 2, hidden_o, width), BF),
            pltpu.VMEM((tiles * 8, 8, 128), F32),
            pltpu.VMEM((8, 8, 128), F32),
            pltpu.SMEM((tiles, 128), jnp.int32),
            pltpu.SemaphoreType.DMA,
        ],
    )
    return atmos_next, ocean_next, surface_temp


def solution(mesh):
    in_specs = (
        P(None, ("grp", "lat", "comp"), "lon"),
        P(None, ("grp", "lat", "comp"), "lon"),
        P(("grp", "lat", "comp"), "lon"),
        P(),
        P(),
        P(),
        P(),
        P(),
        P(),
        P(("grp", "lat", "comp"), "lon", None, None),
        P(("grp", "lat", "comp"), "lon", None, None),
        P(("grp", "lat", "comp"), "lon", None, None),
    )
    out_specs = (
        P(None, ("grp", "lat", "comp"), "lon"),
        P(None, ("grp", "lat", "comp"), "lon"),
        P(("grp", "lat", "comp"), "lon"),
    )
    shape = mesh.shape
    short = (shape["lat"], shape["comp"], shape["lon"]) == (4, 2, 2)
    return jax.shard_map(
        column_device if short else per_device,
        mesh=mesh,
        in_specs=in_specs,
        out_specs=out_specs,
        check_vma=False,
    )
```

```python
import functools

import jax
import jax.numpy as jnp
from jax import lax
from jax.experimental import pallas as pl
from jax.experimental.pallas import tpu as pltpu
from jax.sharding import PartitionSpec as P

BF = jnp.bfloat16
F32 = jnp.float32
EDGE = 8
STRIP = 4 * EDGE


def with_halo(cells, sides, width):
    for axis, dim in sides:
        count = lax.axis_size(axis)
        head = lax.slice_in_dim(cells, 0, width, axis=dim)
        tail = lax.slice_in_dim(cells, cells.shape[dim] - width, cells.shape[dim], axis=dim)
        cells = jnp.concatenate(
            [
                lax.ppermute(tail, axis, [(i, (i + 1) % count) for i in range(count)]),
                cells,
                lax.ppermute(head, axis, [((i + 1) % count, i) for i in range(count)]),
            ],
            axis=dim,
        )
    return cells


def clear_poles(wide, width):
    block_height = wide.shape[1]
    position = lax.axis_index(("lat", "comp"))
    final = lax.axis_size(("lat", "comp")) - 1
    row_ids = lax.iota(jnp.int32, block_height)
    outside = (position == 0) & (row_ids < width) | (position == final) & (
        row_ids >= block_height - width
    )
    return jnp.where(outside[None, :, None], jnp.zeros((), wide.dtype), wide)


def padded_rims(field):
    wide = with_halo(field, ((("lat", "comp"), 1), ("lon", 2)), 1)
    return clear_poles(wide, 1)


def apply_taps(padded, weights, block_height, block_breadth):
    total = jnp.zeros((weights.shape[1], block_height, block_breadth), jnp.float32)
    for row_tap in range(3):
        for col_tap in range(3):
            window = padded[:, row_tap : row_tap + block_height, col_tap : col_tap + block_breadth]
            total = total + jnp.einsum(
                "hc,crw->hrw",
                weights[row_tap * 3 + col_tap],
                window,
                preferred_element_type=jnp.float32,
            )
    return total


def conv_block(state, extra, w_in, w_out, wet):
    block_height, block_breadth = (state.shape[1], state.shape[2])
    source = state if extra is None else jnp.concatenate([state, extra], axis=0)
    hidden = jax.nn.gelu(apply_taps(padded_rims(source), w_in, block_height, block_breadth)).astype(
        jnp.bfloat16
    )
    hidden = padded_rims(hidden)
    total = state.astype(jnp.float32) + apply_taps(hidden, w_out, block_height, block_breadth)
    if wet is not None:
        total = total * wet
    return total.astype(jnp.bfloat16)


def send_fluxes(block_values, destination_blocks):
    arrived, arrived_targets = (
        lax.all_to_all(block_values, ("lat", "comp"), split_axis=0, concat_axis=0, tiled=True),
        lax.all_to_all(
            destination_blocks, ("lat", "comp"), split_axis=0, concat_axis=0, tiled=True
        ),
    )
    return (arrived, arrived_targets)


def send_back(block_values):
    return lax.all_to_all(block_values, ("lat", "comp"), split_axis=0, concat_axis=0, tiled=True)


def per_device(
    atmos_state,
    ocean_state,
    ocean_mask,
    atmos_in_w,
    atmos_out_w,
    ocean_in_w,
    ocean_out_w,
    flux_proj,
    regrid_blocks,
    regrid_source_block,
    regrid_target_block,
    regrid_weight_block,
):
    block_height, block_breadth = (atmos_state.shape[1], atmos_state.shape[2])
    cells_per_block = regrid_blocks.shape[1]
    subblock_count = block_height * block_breadth // cells_per_block
    peer_count = regrid_source_block.shape[2]
    slot_count = regrid_source_block.shape[3]
    flux_count = flux_proj.shape[0]
    atmosphere_model = atmos_state
    for layer in range(atmos_in_w.shape[0]):
        atmosphere_model = conv_block(
            atmosphere_model, None, atmos_in_w[layer], atmos_out_w[layer], None
        )
    surface_flux = jnp.einsum(
        "fc,crw->frw", flux_proj, atmosphere_model, preferred_element_type=jnp.float32
    ).astype(jnp.bfloat16)
    flux_blocks = surface_flux.reshape(flux_count, subblock_count, cells_per_block)
    sources = regrid_source_block.reshape(peer_count * slot_count)
    destination_blocks = regrid_target_block.reshape(peer_count * slot_count)
    weight_ids = regrid_weight_block.reshape(peer_count * slot_count)
    sub_ids = lax.iota(jnp.int32, subblock_count)
    select_blocks = (sources[:, None] == sub_ids[None, :]).astype(jnp.bfloat16)
    chosen = jnp.einsum(
        "ps,fsb->pfb", select_blocks, flux_blocks, preferred_element_type=jnp.float32
    ).astype(jnp.bfloat16)
    collected_values = jnp.take(regrid_blocks, weight_ids, axis=0)
    contrib = jnp.einsum(
        "pfb,pbd->pfd", chosen, collected_values, preferred_element_type=jnp.float32
    ).astype(jnp.bfloat16)
    arrived, arrived_targets = send_fluxes(
        contrib.reshape(peer_count, slot_count, flux_count, cells_per_block),
        destination_blocks.reshape(peer_count, slot_count),
    )
    place_blocks = (
        arrived_targets.reshape(peer_count * slot_count)[:, None] == sub_ids[None, :]
    ).astype(jnp.bfloat16)
    ocean_flux = jnp.einsum(
        "ps,pfd->fsd",
        place_blocks,
        arrived.reshape(peer_count * slot_count, flux_count, cells_per_block),
        preferred_element_type=jnp.float32,
    )
    ocean_flux = ocean_flux.astype(jnp.bfloat16).reshape(flux_count, block_height, block_breadth)
    wet = ocean_mask.astype(jnp.float32)[None]
    ocean_model = (ocean_state.astype(jnp.float32) * wet).astype(jnp.bfloat16)
    for layer in range(ocean_in_w.shape[0]):
        ocean_model = conv_block(
            ocean_model, ocean_flux, ocean_in_w[layer], ocean_out_w[layer], wet
        )
    surface_temp_block = ocean_model[0].reshape(subblock_count, cells_per_block)
    outgoing = jnp.einsum(
        "qb,be->qe", place_blocks, surface_temp_block, preferred_element_type=jnp.float32
    ).astype(jnp.bfloat16)
    received_back = send_back(outgoing.reshape(peer_count, slot_count, cells_per_block))
    received_back = received_back.reshape(peer_count * slot_count, cells_per_block)
    surface_temp_contributions = jnp.einsum(
        "tge,te->tg", collected_values, received_back, preferred_element_type=jnp.float32
    )
    surface_temp_grid = jnp.einsum(
        "yl,yo->lo",
        select_blocks.astype(jnp.float32),
        surface_temp_contributions,
        preferred_element_type=jnp.float32,
    )
    return (atmosphere_model, ocean_model, surface_temp_grid.reshape(block_height, block_breadth))


def gelu(v):
    u = v * (0.7978845608 + 0.0356774081 * (v * v))
    half = 0.5 * v
    return half + half * jnp.tanh(u)


def west(v):
    return pltpu.roll(v, 1, 1)


def east(v):
    return pltpu.roll(v, v.shape[1] - 1, 1)


def store_row(s_ref, slot, row, chans):
    base = slot * 3 * chans
    if not isinstance(base, int):
        base = pl.multiple_of(base, 16)
    taps = jnp.concatenate([west(row), row, east(row)], axis=0).astype(BF)
    s_ref[pl.ds(base, 3 * chans), :] = taps


def clear_ends(s_ref, rows, chans):
    zero = jnp.zeros((3 * chans, s_ref.shape[1]), BF)
    s_ref[0 : 3 * chans, :] = zero
    s_ref[(rows + 1) * 3 * chans : (rows + 2) * 3 * chans, :] = zero


def column_sum(z, outs):
    return z[outs : 2 * outs] + west(z[0:outs]) + east(z[2 * outs : 3 * outs])


def main_block(s_ref, w_in, w_out, outs, rows, width, emit, shift=1, valid=None):
    chans = w_in.shape[1] // 9
    span = 9 * chans
    ahead, behind = None, None
    for r in rows[::2]:
        at = [(r + q - 1 + shift) * 3 * chans for q in range(2)]
        taps = jnp.concatenate([s_ref[i : i + span, :] for i in at], axis=1)
        hidden = gelu(jnp.dot(w_in, taps, preferred_element_type=F32))
        if valid is not None:
            kept = [jnp.full((1, width), valid(r + q), F32) for q in range(2)]
            hidden = hidden * jnp.concatenate(kept, axis=1)
        z = jnp.dot(w_out, hidden.astype(BF), preferred_element_type=F32)
        part = [
            [z[a * 3 * outs : (a + 1) * 3 * outs, q * width : (q + 1) * width] for q in range(2)]
            for a in range(3)
        ]
        if ahead is not None:
            emit(r - 1, column_sum(ahead + part[2][0], outs))
            emit(r, column_sum(behind + part[1][0] + part[2][1], outs))
        elif valid is None:
            emit(r, column_sum(part[1][0] + part[2][1], outs))
        ahead = part[0][0] + part[1][1]
        behind = part[0][1]
    if valid is None:
        emit(rows[-1], column_sum(ahead, outs))


def turned(w_ref, layer):
    return jnp.transpose(w_ref[layer])


def lanes_of(shape):
    return lax.broadcasted_iota(jnp.int32, shape, len(shape) - 1)


def edges_of(rows):
    shape = (rows[0].shape[0], 128)
    lane = lanes_of(shape)
    total = jnp.zeros(shape, F32)
    for i, row in enumerate(rows):
        at = i * STRIP + EDGE
        left = pltpu.roll(row[:, 0:128], at, 1)
        total = jnp.where((lane >= at) & (lane < at + EDGE), left, total)
        at = at + EDGE
        width = row.shape[1]
        right = pltpu.roll(row[:, width - 128 : width], (at + EDGE) % 128, 1)
        total = jnp.where((lane >= at) & (lane < at + EDGE), right, total)
    return total


def with_neighbour(own, other):
    place = lanes_of(own.shape) % STRIP
    left = pltpu.roll(other, 128 - 2 * EDGE, 1)
    right = pltpu.roll(other, 2 * EDGE, 1)
    return jnp.where(place < EDGE, left, jnp.where(place >= 3 * EDGE, right, own))


def strip_shift(v, a, b, poles):
    width = v.shape[1]
    moved = pltpu.roll(v, (-((a - 1) * STRIP + b - 1)) % width, 1) if (a, b) != (1, 1) else v
    lane = lanes_of(v.shape)
    if poles and a == 0:
        moved = jnp.where(lane < STRIP, 0.0, moved)
    if poles and a == 2:
        moved = jnp.where(lane >= width - STRIP, 0.0, moved)
    return moved


def strip_block(source, w_in, w_out, outs, kept=None):
    poles = kept is None
    taps = jnp.concatenate(
        [strip_shift(source, a, b, poles) for a in range(3) for b in range(3)], axis=0
    ).astype(BF)
    hidden = gelu(jnp.dot(w_in, taps, preferred_element_type=F32))
    if not poles:
        hidden = hidden * kept
    z = jnp.dot(w_out, hidden.astype(BF), preferred_element_type=F32)
    total = z[4 * outs : 5 * outs]
    for tap in range(9):
        if tap != 4:
            total = total + strip_shift(z[tap * outs : (tap + 1) * outs], tap // 3, tap % 3, poles)
    return total


def mend_row(row, strip, r):
    width = row.shape[1]
    at = (r % 4) * STRIP + EDGE
    lane = lanes_of((row.shape[0], 128))
    left = pltpu.roll(strip, (-at) % 128, 1)
    right = pltpu.roll(strip, (-(at + 2 * EDGE)) % 128, 1)
    head = jnp.where(lane < 4, left, row[:, 0:128])
    tail = jnp.where(lane >= 124, right, row[:, width - 128 : width])
    return jnp.concatenate([head, row[:, 128 : width - 128], tail], axis=1)


def pack_atmos_kernel(atmos_ref, tile_ref):
    for r in range(tile_ref.shape[0]):
        tile_ref[r] = atmos_ref[:, r, :]


def pack_ocean_kernel(source_hbm, target_hbm, weight_hbm, ocean_hbm, mask_hbm, tile_ref, source_ref,
                      target_ref, weight_ref, ocean_ref, mask_ref, sems):
    given = (source_hbm, target_hbm, weight_hbm, ocean_hbm, mask_hbm)
    numbers = (source_ref, target_ref, weight_ref)
    held = (*numbers, ocean_ref, mask_ref)
    copies = [pltpu.make_async_copy(v, h, sems.at[i]) for i, (v, h) in enumerate(zip(given, held))]
    for copy in copies:
        copy.start()
    for copy in copies:
        copy.wait()
    height, span, width = tile_ref.shape
    slots, peers = source_ref.shape[2:]
    listed = [ref[0, 0, s : s + 1, :].astype(F32) for ref in numbers for s in range(slots)]
    listed.append(jnp.zeros((1, width - len(listed) * peers), F32))
    listed = jnp.concatenate(listed, axis=1)
    rest = jnp.zeros((span - ocean_ref.shape[0] - 2, width), F32)
    for r in range(height):
        wet = mask_ref[r : r + 1, :].astype(F32)
        state = ocean_ref[:, r, :].astype(F32) * wet
        tile_ref[r] = jnp.concatenate([state, wet, listed, rest], axis=0).astype(BF)


def stack_kernel(place_ref, own_ref, side_ref, cross_ref, even_ref, odd_ref, stack_ref, edge_ref):
    lat, comp = place_ref[0], place_ref[1]
    chans, width = own_ref.shape[1:]
    valid = window_rule(place_ref)[1]
    low = lat % 2 == 0
    places = (
        (own_ref, 2),
        (side_ref, 3 - 2 * comp),
        (cross_ref, 1 + 2 * comp),
        (even_ref, jnp.where(low, 4, 0)),
        (odd_ref, jnp.where(low, 0, 4)),
    )
    for tile, at in places:
        for r in range(2):
            row = 2 * at + r
            store_row(stack_ref, row, tile[r].astype(F32) * valid(row), chans)
    for q in range(edge_ref.shape[0]):
        both = jnp.zeros((chans, 128), F32)
        for half in range(2):
            r = 4 * q + 2 * half
            if r < stack_ref.shape[0] // (3 * chans):
                at = [(3 * (r + i) + 1) * chans for i in range(2)]
                ends = edges_of([stack_ref[i : i + chans, :].astype(F32) for i in at])
                both = both + pltpu.roll(ends, 64 * half, 1)
        edge_ref[q] = both.astype(BF)


def centre(ref, slot, chans):
    at = (3 * slot + 1) * chans
    if not isinstance(at, int):
        at = pl.multiple_of(at, 16)
    return ref[pl.ds(at, chans), :].astype(F32)


def window_rule(place_ref):
    first = 4 * place_ref[0] + 2 * place_ref[1] - 4
    limit = place_ref[2]
    return first, lambda r: jnp.where((first + r >= 0) & (first + r < limit), 1.0, 0.0)


def strip_of(own_ref, other_ref):
    tiles = range(own_ref.shape[0])
    both = [with_neighbour(own_ref[q].astype(F32), other_ref[q].astype(F32)) for q in tiles]
    return jnp.concatenate(both, axis=1)


def first_kernel(place_ref, stack_ref, win_ref, wout_ref, next_ref):
    chans, width = wout_ref.shape[1] // 9, stack_ref.shape[1]
    valid = window_rule(place_ref)[1]

    def keep(r, y):
        total = (centre(stack_ref, r, chans) + y).astype(BF).astype(F32)
        store_row(next_ref, r, total * valid(r), chans)

    main_block(stack_ref, turned(win_ref, 0), wout_ref[0], chans, range(1, 9), width, keep, 0, valid)


def second_kernel(place_ref, stack_ref, own_ref, other_ref, win_ref, wout_ref, proj_ref, ocean_ref,
                  next_ref, sent_ref):
    chans, width = wout_ref.shape[1] // 9, stack_ref.shape[1]
    per_row = width // 128
    first, valid = window_rule(place_ref)
    w_in = [turned(win_ref, layer) for layer in range(2)]
    main = {}

    def finish(r, y):
        main[r - 4] = (centre(stack_ref, r, chans) + y).astype(BF).astype(F32)

    strip = strip_of(own_ref, other_ref)
    lane = lanes_of((1, strip.shape[1]))
    inside = (lane >= -first * STRIP) & (lane < (place_ref[2] - first) * STRIP)
    kept = jnp.where(inside, 1.0, 0.0)
    strip = strip + strip_block(strip, w_in[0], wout_ref[0], chans, kept)
    strip = strip.astype(BF).astype(F32) * kept
    main_block(stack_ref, w_in[1], wout_ref[1], chans, range(3, 7), width, finish, 0, valid)
    strip = strip + strip_block(strip, w_in[1], wout_ref[1], chans, kept)

    mended = [mend_row(main[r], strip[:, 128:256], r).astype(BF) for r in range(2)]
    for r in range(2):
        next_ref[:, r, :] = mended[r]
    flux = jnp.dot(proj_ref[...], jnp.concatenate(mended, axis=1), preferred_element_type=F32)
    blocks = [flux[:, 128 * b : 128 * (b + 1)] for b in range(2 * per_row)]
    numbers = ocean_ref[0, 32:48, 0:128].astype(F32)[9:10]
    state = [ocean_ref[r].astype(F32) for r in range(2)]
    outs = chans - 8
    lanes = [(r, slice(128 * b, 128 * (b + 1))) for r in range(2) for b in range(per_row)]
    wet = [state[r][outs : outs + 1, at] for r, at in lanes]
    rest = jnp.zeros((16 - 1 - len(wet), 128), F32)
    ocean = [state[r][0:outs, at] for r, at in lanes]
    sent_ref[...] = jnp.concatenate([*blocks, numbers, *wet, rest, *ocean], axis=0).astype(BF)


def regrid_kernel(place_ref, blocks_ref, atmos_ref, *refs):
    sent, (stack_ref, wet_ref, edge_ref, table, next_hbm, flux_ref, total, index, sem, next_sem) = (
        refs[:8],
        refs[8:],
    )
    leaving = pltpu.make_async_copy(atmos_ref, next_hbm, next_sem)
    leaving.start()
    lat, comp = place_ref[0], place_ref[1]
    peers = len(sent)
    chips = peers // 2
    fluxes = flux_ref.shape[1]
    subs = flux_ref.shape[0] // peers
    per_row = subs // 2
    rows = wet_ref.shape[0]
    chans = stack_ref.shape[0] // (3 * (rows + 2))
    outs = chans - fluxes
    slots = 2 * peers
    places = [2 * (lat ^ (i % chips)) + (comp if i < chips else 1 - comp) for i in range(peers)]
    head = subs * fluxes + 16
    for t, ref in zip(places, sent):
        row = ref[head - 16 : head, :].astype(F32)[0:1]
        table[pl.ds(t, 1), :] = row.astype(jnp.int32)
    copy = pltpu.make_async_copy(table, index, sem)
    copy.start()
    total[...] = jnp.zeros(total.shape, F32)
    for t, ref in zip(places, sent):
        values = ref[0 : head - 16, :].astype(F32)
        for b in range(subs):
            flux_ref[t * subs + b] = values[b * fluxes : (b + 1) * fluxes]
    clear_ends(stack_ref, rows, chans)
    copy.wait()

    def one_tile(t, carry):
        pieces = []
        for slot in range(slots):
            source = jnp.maximum(index[t, slot], 0)
            block = blocks_ref[index[t, 2 * slots + slot]]
            value = flux_ref[t * subs + source].astype(BF)
            piece = jnp.dot(value, block, preferred_element_type=F32)
            pieces.append(piece.astype(BF).astype(F32))
        for slot in range(slots):
            target = jnp.where(index[t, slot] >= 0, index[t, slots + slot], 6)
            at = (slot % peers) * 8 + target
            total[at] = total[at] + pieces[slot]
        return carry

    lax.fori_loop(0, peers, one_tile, 0, unroll=8)

    def tile_row(ref, r):
        state = []
        for b in range(per_row):
            at = head + (r * per_row + b) * outs
            shift = at % 16
            rows16 = ref[at - shift : at - shift + chans, :].astype(F32)
            state.append(rows16[shift : shift + outs])
        marks = ref[head - 16 : head, :].astype(F32)[1 + r * per_row : 1 + (r + 1) * per_row]
        wet = jnp.concatenate([marks[b : b + 1] for b in range(per_row)], axis=1)
        return jnp.concatenate(state, axis=1), wet

    for k in range(chips):
        both = jnp.zeros((chans + fluxes, 128), F32)
        for i in (k, chips + k):
            t = places[i]
            ends = []
            for r in range(2):
                arrived = jnp.concatenate(
                    [total[8 * t + r * per_row + b] for b in range(per_row)], axis=1
                )
                state, wet = tile_row(sent[i], r)
                wet = jnp.concatenate([wet, jnp.zeros((fluxes - 1, wet.shape[1]), F32)], axis=0)
                row = jnp.concatenate([state, arrived.astype(BF).astype(F32)], axis=0)
                store_row(stack_ref, 2 * t + r + 1, row, chans)
                wet_ref[2 * t + r] = wet
                ends.append(jnp.concatenate([row, wet], axis=0))
            both = both + pltpu.roll(edges_of(ends), 64 * (comp if i < chips else 1 - comp), 1)
        edge_ref[lat ^ k] = both.astype(BF)
    leaving.wait()


def ocean_kernel(stack_ref, wet_ref, win_ref, wout_ref, next_ref):
    chans, outs = win_ref.shape[1] // 9, wout_ref.shape[1] // 9
    rows, width = wet_ref.shape[0], stack_ref.shape[1]
    clear_ends(next_ref, rows, chans)

    def emit(r, y):
        state = centre(stack_ref, r + 1, chans)
        total = (wet_ref[r, 0:1, :] * (state[0:outs] + y)).astype(BF).astype(F32)
        store_row(next_ref, r + 1, jnp.concatenate([total, state[outs:]], axis=0), chans)

    main_block(stack_ref, turned(win_ref, 0), wout_ref[0], outs, range(rows), width, emit)


def finish_kernel(place_ref, table_ref, stack_ref, wet_ref, own_ref, other_ref, win_ref, wout_ref,
                  blocks_ref, next_ref, temp_ref, hidden_ref, surface, total, index, sem):
    copy = pltpu.make_async_copy(table_ref, index, sem)
    copy.start()
    lat, comp = place_ref[0], place_ref[1]
    t = 2 * lat + comp
    chans, outs = win_ref.shape[1] // 9, wout_ref.shape[1] // 9
    hidden = win_ref.shape[2]
    rows, width = wet_ref.shape[0], stack_ref.shape[1]
    per_row = width // 128
    w_in = [turned(win_ref, layer) for layer in range(2)]
    total[...] = jnp.zeros(total.shape, F32)
    copy.wait()

    strip = strip_of(own_ref, other_ref)
    wet = strip[chans : chans + 1]
    state, fixed = strip[0:outs], strip[outs:chans]
    state = wet * (state + strip_block(strip[0:chans], w_in[0], wout_ref[0], outs))
    state = state.astype(BF).astype(F32)

    last = wout_ref[1].astype(F32)
    none = jnp.zeros((5, hidden), F32)
    w_temp = jnp.concatenate(
        [v for a in range(3) for v in (*(last[(3 * a + b) * outs][None] for b in range(3)), none)]
        + [jnp.zeros((8, hidden), F32)],
        axis=0,
    ).astype(BF)
    ends = jnp.zeros((hidden, width), BF)
    hidden_ref[0] = ends
    hidden_ref[rows + 1] = ends
    parts = {}
    for r in range(0, rows, 2):
        at = [(r + q) * 3 * chans for q in range(2)]
        taps = jnp.concatenate([stack_ref[i : i + 9 * chans, :] for i in at], axis=1)
        active = gelu(jnp.dot(w_in[1], taps, preferred_element_type=F32)).astype(BF)
        for q in range(2):
            hidden_ref[r + q + 1] = active[:, q * width : (q + 1) * width]
        z = jnp.dot(w_temp, active, preferred_element_type=F32)
        for a in range(3):
            for q in range(2):
                part = z[8 * a : 8 * a + 8, q * width : (q + 1) * width]
                row = r + q - a + 1
                parts[row] = parts[row] + part if row in parts else part

    source = jnp.concatenate([state, fixed], axis=0)
    state = wet * (state + strip_block(source, w_in[1], wout_ref[1], outs))
    state = state.astype(BF).astype(F32)

    for r in range(rows):
        y = parts[r]
        y = y[1:2] + west(y)[0:1] + east(y)[2:3]
        top = wet_ref[r, 0:1, :] * (centre(stack_ref, r + 1, chans)[0:8] + y)
        q = r // 4
        top = mend_row(top, state[0:8, 128 * q : 128 * (q + 1)], r)
        for b in range(per_row):
            surface[(r // 2) * 8 + (r % 2) * per_row + b] = top[:, 128 * b : 128 * (b + 1)]

    edge = jnp.zeros((outs, 128), F32)
    for q in range(own_ref.shape[0]):
        edge = jnp.where(lat == q, state[:, 128 * q : 128 * (q + 1)], edge)
    edge = pltpu.roll(edge, jnp.where(comp == 1, 64, 0), 1)
    z = [
        jnp.dot(
            wout_ref[1],
            jnp.concatenate([hidden_ref[2 * t + 2 * p + q] for q in range(2)], axis=1),
            preferred_element_type=F32,
        )
        for p in range(2)
    ]
    for r in range(2):
        y = sum(
            z[(r + a) // 2][
                3 * a * outs : 3 * (a + 1) * outs, (r + a) % 2 * width : ((r + a) % 2 + 1) * width
            ]
            for a in range(3)
        )
        row = centre(stack_ref, 2 * t + r + 1, chans)[0:outs] + column_sum(y, outs)
        next_ref[:, r, :] = mend_row(wet_ref[2 * t + r, 0:1, :] * row, edge, r).astype(BF)

    peers = rows // 2
    slots = 2 * peers
    for slot in range(slots):
        source = index[t, slot]
        target = index[t, slots + slot]
        block = blocks_ref[index[t, 2 * slots + slot]]
        value = surface[(slot % peers) * 8 + target].astype(BF)
        piece = lax.dot_general(value, block, (((1,), (1,)), ((), ())), preferred_element_type=F32)
        at = jnp.where(source >= 0, source, 6)
        total[at] = total[at] + piece
    for r in range(2):
        temp_ref[r : r + 1, :] = jnp.concatenate(
            [total[r * per_row + b][0:1] for b in range(per_row)], axis=1
        )


def call(kernel, out_shape, operands, scratch=(), smem=1, anywhere=0, flops=0, leaving=None):
    held = len(operands) - smem - anywhere
    spaces = [pltpu.SMEM] * smem + [pltpu.VMEM] * held + [pltpu.HBM] * anywhere
    out_specs = jax.tree.map(lambda _: pl.BlockSpec(memory_space=pltpu.VMEM), out_shape)
    if leaving is not None:
        out_shape = (*out_shape, leaving)
        out_specs = (*out_specs, pl.BlockSpec(memory_space=pl.ANY))
    return pl.pallas_call(
        kernel,
        out_shape=out_shape,
        in_specs=[pl.BlockSpec(memory_space=space) for space in spaces],
        out_specs=out_specs,
        scratch_shapes=list(scratch),
        compiler_params=pltpu.CompilerParams(vmem_limit_bytes=40 * 2**20),
        cost_estimate=pl.CostEstimate(flops=flops, bytes_accessed=2**20, transcendentals=0),
    )(*operands)


def column_device(
    atmos_state,
    ocean_state,
    ocean_mask,
    atmos_in_w,
    atmos_out_w,
    ocean_in_w,
    ocean_out_w,
    flux_proj,
    regrid_blocks,
    regrid_source_block,
    regrid_target_block,
    regrid_weight_block,
):
    chans, height, width = atmos_state.shape
    outs = ocean_state.shape[0]
    lats = lax.axis_size("lat")
    tiles = lats * lax.axis_size("comp")
    rows = tiles * height
    layers, _, hidden_a, _ = atmos_in_w.shape
    hidden_o = ocean_in_w.shape[2]
    fluxes = flux_proj.shape[0]
    place = jnp.stack([lax.axis_index("lat"), lax.axis_index("comp"), rows]).astype(jnp.int32)

    def far(v, k):
        return lax.ppermute(v, "lat", [(i, i ^ k) for i in range(lats)])

    def swap(v, axis):
        return lax.ppermute(v, axis, [(0, 1), (1, 0)])

    def conv_flops(hidden, outs):
        return 2 * layers * rows * width * 9 * hidden * (chans + outs)

    tile = jax.ShapeDtypeStruct((height, chans, width), BF)
    atmos_tile = call(
        pack_atmos_kernel, tile, [atmos_state], smem=0, flops=conv_flops(hidden_a, chans)
    )
    slots = (regrid_source_block, regrid_target_block, regrid_weight_block)
    given = [*(jnp.transpose(v, (0, 1, 3, 2)) for v in slots), ocean_state, ocean_mask]
    ocean_tile = call(
        pack_ocean_kernel,
        tile,
        given,
        [*(pltpu.VMEM(v.shape, v.dtype) for v in given), pltpu.SemaphoreType.DMA((len(given),))],
        smem=0,
        anywhere=len(given),
    )
    cross = [(i, i + 1) for i in range(1, tiles - 1, 2)]
    odd = [(i, i + 1) for i in range(1, lats - 1, 2)]

    def both_ways(pairs):
        return pairs + [(j, i) for i, j in pairs]

    cross.append((0, tiles - 1))
    odd.append((0, lats - 1))

    near = [
        atmos_tile,
        swap(atmos_tile, "comp"),
        lax.ppermute(atmos_tile, ("lat", "comp"), both_ways(cross)),
        far(atmos_tile, 1),
        lax.ppermute(atmos_tile, "lat", both_ways(odd)),
    ]
    def taps_in(w):
        return jnp.transpose(w, (0, 1, 3, 2)).reshape(w.shape[0], 9 * w.shape[3], w.shape[2])

    def taps_out(w):
        return w.reshape(w.shape[0], 9 * w.shape[2], w.shape[3])

    win_a, wout_a = taps_in(atmos_in_w), taps_out(atmos_out_w)
    win_o, wout_o = taps_in(ocean_in_w), taps_out(ocean_out_w)

    window = height * len(near)
    stack_shape = (window * 3 * chans, width)
    atmos_stack, edges = call(
        stack_kernel,
        (
            jax.ShapeDtypeStruct(stack_shape, BF),
            jax.ShapeDtypeStruct((pl.cdiv(window * STRIP, 128), chans, 128), BF),
        ),
        [place, *near],
        flops=conv_flops(hidden_a, chans),
    )
    edges_other = swap(edges, "lon")
    atmos_stack = call(
        first_kernel,
        jax.ShapeDtypeStruct(stack_shape, BF),
        [place, atmos_stack, win_a, wout_a],
        flops=4 * conv_flops(hidden_a, chans),
    )
    subs = height * width // 128
    atmos_next, sent = call(
        second_kernel,
        (
            jax.ShapeDtypeStruct((chans, height, width), BF),
            jax.ShapeDtypeStruct((subs * (fluxes + outs) + 16, 128), BF),
        ),
        [place, atmos_stack, edges, edges_other, win_a, wout_a, flux_proj, ocean_tile],
        flops=4 * conv_flops(hidden_a, chans),
    )
    others = {k: far(sent, k) for k in reversed(range(1, lats))}
    sent = [sent] + [others[k] for k in range(1, lats)]
    sent = sent + [swap(v, "comp") for v in sent]
    stack_shape = ((rows + 2) * 3 * chans, width)
    ocean_stack, wet, ocean_edges, table, atmos_next = call(
        regrid_kernel,
        (
            jax.ShapeDtypeStruct(stack_shape, BF),
            jax.ShapeDtypeStruct((rows, fluxes, width), F32),
            jax.ShapeDtypeStruct((lats, chans + fluxes, 128), BF),
            jax.ShapeDtypeStruct((tiles, 128), jnp.int32),
        ),
        [place, regrid_blocks, atmos_next, *sent],
        [
            pltpu.VMEM((tiles * subs, fluxes, 128), F32),
            pltpu.VMEM((tiles * 8, fluxes, 128), F32),
            pltpu.SMEM((tiles, 128), jnp.int32),
            pltpu.SemaphoreType.DMA,
            pltpu.SemaphoreType.DMA,
        ],
        flops=conv_flops(hidden_o, outs),
        leaving=jax.ShapeDtypeStruct((chans, height, width), BF),
    )
    ocean_edges_other = swap(ocean_edges, "lon")
    ocean_stack = call(
        ocean_kernel,
        jax.ShapeDtypeStruct(stack_shape, BF),
        [ocean_stack, wet, win_o, wout_o],
        smem=0,
        flops=4 * conv_flops(hidden_o, outs),
    )
    ocean_next, surface_temp = call(
        finish_kernel,
        (
            jax.ShapeDtypeStruct((outs, height, width), BF),
            jax.ShapeDtypeStruct((height, width), F32),
        ),
        [
            place,
            table,
            ocean_stack,
            wet,
            ocean_edges,
            ocean_edges_other,
            win_o,
            wout_o,
            regrid_blocks,
        ],
        [
            pltpu.VMEM((rows + 2, hidden_o, width), BF),
            pltpu.VMEM((tiles * 8, 8, 128), F32),
            pltpu.VMEM((8, 8, 128), F32),
            pltpu.SMEM((tiles, 128), jnp.int32),
            pltpu.SemaphoreType.DMA,
        ],
    )
    return atmos_next, ocean_next, surface_temp


def solution(mesh):
    in_specs = (
        P(None, ("grp", "lat", "comp"), "lon"),
        P(None, ("grp", "lat", "comp"), "lon"),
        P(("grp", "lat", "comp"), "lon"),
        P(),
        P(),
        P(),
        P(),
        P(),
        P(),
        P(("grp", "lat", "comp"), "lon", None, None),
        P(("grp", "lat", "comp"), "lon", None, None),
        P(("grp", "lat", "comp"), "lon", None, None),
    )
    out_specs = (
        P(None, ("grp", "lat", "comp"), "lon"),
        P(None, ("grp", "lat", "comp"), "lon"),
        P(("grp", "lat", "comp"), "lon"),
    )
    shape = mesh.shape
    short = (shape["lat"], shape["comp"], shape["lon"]) == (4, 2, 2)
    return jax.shard_map(
        column_device if short else per_device,
        mesh=mesh,
        in_specs=in_specs,
        out_specs=out_specs,
        check_vma=False,
    )
```

```python
import functools

import jax
import jax.numpy as jnp
from jax import lax
from jax.experimental import pallas as pl
from jax.experimental.pallas import tpu as pltpu
from jax.sharding import PartitionSpec as P

BF = jnp.bfloat16
F32 = jnp.float32
EDGE = 8
STRIP = 4 * EDGE


def with_halo(cells, sides, width):
    for axis, dim in sides:
        count = lax.axis_size(axis)
        head = lax.slice_in_dim(cells, 0, width, axis=dim)
        tail = lax.slice_in_dim(cells, cells.shape[dim] - width, cells.shape[dim], axis=dim)
        cells = jnp.concatenate(
            [
                lax.ppermute(tail, axis, [(i, (i + 1) % count) for i in range(count)]),
                cells,
                lax.ppermute(head, axis, [((i + 1) % count, i) for i in range(count)]),
            ],
            axis=dim,
        )
    return cells


def clear_poles(wide, width):
    block_height = wide.shape[1]
    position = lax.axis_index(("lat", "comp"))
    final = lax.axis_size(("lat", "comp")) - 1
    row_ids = lax.iota(jnp.int32, block_height)
    outside = (position == 0) & (row_ids < width) | (position == final) & (
        row_ids >= block_height - width
    )
    return jnp.where(outside[None, :, None], jnp.zeros((), wide.dtype), wide)


def padded_rims(field):
    wide = with_halo(field, ((("lat", "comp"), 1), ("lon", 2)), 1)
    return clear_poles(wide, 1)


def apply_taps(padded, weights, block_height, block_breadth):
    total = jnp.zeros((weights.shape[1], block_height, block_breadth), jnp.float32)
    for row_tap in range(3):
        for col_tap in range(3):
            window = padded[:, row_tap : row_tap + block_height, col_tap : col_tap + block_breadth]
            total = total + jnp.einsum(
                "hc,crw->hrw",
                weights[row_tap * 3 + col_tap],
                window,
                preferred_element_type=jnp.float32,
            )
    return total


def conv_block(state, extra, w_in, w_out, wet):
    block_height, block_breadth = (state.shape[1], state.shape[2])
    source = state if extra is None else jnp.concatenate([state, extra], axis=0)
    hidden = jax.nn.gelu(apply_taps(padded_rims(source), w_in, block_height, block_breadth)).astype(
        jnp.bfloat16
    )
    hidden = padded_rims(hidden)
    total = state.astype(jnp.float32) + apply_taps(hidden, w_out, block_height, block_breadth)
    if wet is not None:
        total = total * wet
    return total.astype(jnp.bfloat16)


def send_fluxes(block_values, destination_blocks):
    arrived, arrived_targets = (
        lax.all_to_all(block_values, ("lat", "comp"), split_axis=0, concat_axis=0, tiled=True),
        lax.all_to_all(
            destination_blocks, ("lat", "comp"), split_axis=0, concat_axis=0, tiled=True
        ),
    )
    return (arrived, arrived_targets)


def send_back(block_values):
    return lax.all_to_all(block_values, ("lat", "comp"), split_axis=0, concat_axis=0, tiled=True)


def per_device(
    atmos_state,
    ocean_state,
    ocean_mask,
    atmos_in_w,
    atmos_out_w,
    ocean_in_w,
    ocean_out_w,
    flux_proj,
    regrid_blocks,
    regrid_source_block,
    regrid_target_block,
    regrid_weight_block,
):
    block_height, block_breadth = (atmos_state.shape[1], atmos_state.shape[2])
    cells_per_block = regrid_blocks.shape[1]
    subblock_count = block_height * block_breadth // cells_per_block
    peer_count = regrid_source_block.shape[2]
    slot_count = regrid_source_block.shape[3]
    flux_count = flux_proj.shape[0]
    atmosphere_model = atmos_state
    for layer in range(atmos_in_w.shape[0]):
        atmosphere_model = conv_block(
            atmosphere_model, None, atmos_in_w[layer], atmos_out_w[layer], None
        )
    surface_flux = jnp.einsum(
        "fc,crw->frw", flux_proj, atmosphere_model, preferred_element_type=jnp.float32
    ).astype(jnp.bfloat16)
    flux_blocks = surface_flux.reshape(flux_count, subblock_count, cells_per_block)
    sources = regrid_source_block.reshape(peer_count * slot_count)
    destination_blocks = regrid_target_block.reshape(peer_count * slot_count)
    weight_ids = regrid_weight_block.reshape(peer_count * slot_count)
    sub_ids = lax.iota(jnp.int32, subblock_count)
    select_blocks = (sources[:, None] == sub_ids[None, :]).astype(jnp.bfloat16)
    chosen = jnp.einsum(
        "ps,fsb->pfb", select_blocks, flux_blocks, preferred_element_type=jnp.float32
    ).astype(jnp.bfloat16)
    collected_values = jnp.take(regrid_blocks, weight_ids, axis=0)
    contrib = jnp.einsum(
        "pfb,pbd->pfd", chosen, collected_values, preferred_element_type=jnp.float32
    ).astype(jnp.bfloat16)
    arrived, arrived_targets = send_fluxes(
        contrib.reshape(peer_count, slot_count, flux_count, cells_per_block),
        destination_blocks.reshape(peer_count, slot_count),
    )
    place_blocks = (
        arrived_targets.reshape(peer_count * slot_count)[:, None] == sub_ids[None, :]
    ).astype(jnp.bfloat16)
    ocean_flux = jnp.einsum(
        "ps,pfd->fsd",
        place_blocks,
        arrived.reshape(peer_count * slot_count, flux_count, cells_per_block),
        preferred_element_type=jnp.float32,
    )
    ocean_flux = ocean_flux.astype(jnp.bfloat16).reshape(flux_count, block_height, block_breadth)
    wet = ocean_mask.astype(jnp.float32)[None]
    ocean_model = (ocean_state.astype(jnp.float32) * wet).astype(jnp.bfloat16)
    for layer in range(ocean_in_w.shape[0]):
        ocean_model = conv_block(
            ocean_model, ocean_flux, ocean_in_w[layer], ocean_out_w[layer], wet
        )
    surface_temp_block = ocean_model[0].reshape(subblock_count, cells_per_block)
    outgoing = jnp.einsum(
        "qb,be->qe", place_blocks, surface_temp_block, preferred_element_type=jnp.float32
    ).astype(jnp.bfloat16)
    received_back = send_back(outgoing.reshape(peer_count, slot_count, cells_per_block))
    received_back = received_back.reshape(peer_count * slot_count, cells_per_block)
    surface_temp_contributions = jnp.einsum(
        "tge,te->tg", collected_values, received_back, preferred_element_type=jnp.float32
    )
    surface_temp_grid = jnp.einsum(
        "yl,yo->lo",
        select_blocks.astype(jnp.float32),
        surface_temp_contributions,
        preferred_element_type=jnp.float32,
    )
    return (atmosphere_model, ocean_model, surface_temp_grid.reshape(block_height, block_breadth))


def gelu(v):
    u = v * (0.7978845608 + 0.0356774081 * (v * v))
    half = 0.5 * v
    return half + half * jnp.tanh(u)


def west(v):
    return pltpu.roll(v, 1, 1)


def east(v):
    return pltpu.roll(v, v.shape[1] - 1, 1)


def store_row(s_ref, slot, row, chans):
    base = slot * 3 * chans
    if not isinstance(base, int):
        base = pl.multiple_of(base, 16)
    taps = jnp.concatenate([west(row), row, east(row)], axis=0).astype(BF)
    s_ref[pl.ds(base, 3 * chans), :] = taps


def clear_ends(s_ref, rows, chans):
    zero = jnp.zeros((3 * chans, s_ref.shape[1]), BF)
    s_ref[0 : 3 * chans, :] = zero
    s_ref[(rows + 1) * 3 * chans : (rows + 2) * 3 * chans, :] = zero


def column_sum(z, outs):
    return z[outs : 2 * outs] + west(z[0:outs]) + east(z[2 * outs : 3 * outs])


def main_block(s_ref, w_in, w_out, outs, rows, width, emit, shift=1, valid=None):
    chans = w_in.shape[1] // 9
    span = 9 * chans
    ahead, behind = None, None
    for r in rows[::2]:
        at = [(r + q - 1 + shift) * 3 * chans for q in range(2)]
        taps = jnp.concatenate([s_ref[i : i + span, :] for i in at], axis=1)
        hidden = gelu(jnp.dot(w_in, taps, preferred_element_type=F32))
        if valid is not None:
            kept = [jnp.full((1, width), valid(r + q), F32) for q in range(2)]
            hidden = hidden * jnp.concatenate(kept, axis=1)
        z = jnp.dot(w_out, hidden.astype(BF), preferred_element_type=F32)
        part = [
            [z[a * 3 * outs : (a + 1) * 3 * outs, q * width : (q + 1) * width] for q in range(2)]
            for a in range(3)
        ]
        if ahead is not None:
            emit(r - 1, column_sum(ahead + part[2][0], outs))
            emit(r, column_sum(behind + part[1][0] + part[2][1], outs))
        elif valid is None:
            emit(r, column_sum(part[1][0] + part[2][1], outs))
        ahead = part[0][0] + part[1][1]
        behind = part[0][1]
    if valid is None:
        emit(rows[-1], column_sum(ahead, outs))


def turned(w_ref, layer):
    return jnp.transpose(w_ref[layer])


def lanes_of(shape):
    return lax.broadcasted_iota(jnp.int32, shape, len(shape) - 1)


def edges_of(rows):
    shape = (rows[0].shape[0], 128)
    lane = lanes_of(shape)
    total = jnp.zeros(shape, F32)
    for i, row in enumerate(rows):
        at = i * STRIP + EDGE
        left = pltpu.roll(row[:, 0:128], at, 1)
        total = jnp.where((lane >= at) & (lane < at + EDGE), left, total)
        at = at + EDGE
        width = row.shape[1]
        right = pltpu.roll(row[:, width - 128 : width], (at + EDGE) % 128, 1)
        total = jnp.where((lane >= at) & (lane < at + EDGE), right, total)
    return total


def with_neighbour(own, other):
    place = lanes_of(own.shape) % STRIP
    left = pltpu.roll(other, 128 - 2 * EDGE, 1)
    right = pltpu.roll(other, 2 * EDGE, 1)
    return jnp.where(place < EDGE, left, jnp.where(place >= 3 * EDGE, right, own))


def strip_shift(v, a, b, poles):
    width = v.shape[1]
    moved = pltpu.roll(v, (-((a - 1) * STRIP + b - 1)) % width, 1) if (a, b) != (1, 1) else v
    lane = lanes_of(v.shape)
    if poles and a == 0:
        moved = jnp.where(lane < STRIP, 0.0, moved)
    if poles and a == 2:
        moved = jnp.where(lane >= width - STRIP, 0.0, moved)
    return moved


def strip_block(source, w_in, w_out, outs, kept=None):
    poles = kept is None
    taps = jnp.concatenate(
        [strip_shift(source, a, b, poles) for a in range(3) for b in range(3)], axis=0
    ).astype(BF)
    hidden = gelu(jnp.dot(w_in, taps, preferred_element_type=F32))
    if not poles:
        hidden = hidden * kept
    z = jnp.dot(w_out, hidden.astype(BF), preferred_element_type=F32)
    total = z[4 * outs : 5 * outs]
    for tap in range(9):
        if tap != 4:
            total = total + strip_shift(z[tap * outs : (tap + 1) * outs], tap // 3, tap % 3, poles)
    return total


def mend_row(row, strip, r):
    width = row.shape[1]
    at = (r % 4) * STRIP + EDGE
    lane = lanes_of((row.shape[0], 128))
    left = pltpu.roll(strip, (-at) % 128, 1)
    right = pltpu.roll(strip, (-(at + 2 * EDGE)) % 128, 1)
    head = jnp.where(lane < 4, left, row[:, 0:128])
    tail = jnp.where(lane >= 124, right, row[:, width - 128 : width])
    return jnp.concatenate([head, row[:, 128 : width - 128], tail], axis=1)


def pack_ocean_kernel(source_hbm, target_hbm, weight_hbm, ocean_hbm, mask_hbm, tile_ref, source_ref,
                      target_ref, weight_ref, ocean_ref, mask_ref, sems):
    given = (source_hbm, target_hbm, weight_hbm, ocean_hbm, mask_hbm)
    numbers = (source_ref, target_ref, weight_ref)
    held = (*numbers, ocean_ref, mask_ref)
    copies = [pltpu.make_async_copy(v, h, sems.at[i]) for i, (v, h) in enumerate(zip(given, held))]
    for copy in copies:
        copy.start()
    for copy in copies:
        copy.wait()
    height, span, width = tile_ref.shape
    slots, peers = source_ref.shape[2:]
    listed = [ref[0, 0, s : s + 1, :].astype(F32) for ref in numbers for s in range(slots)]
    listed.append(jnp.zeros((1, width - len(listed) * peers), F32))
    listed = jnp.concatenate(listed, axis=1)
    rest = jnp.zeros((span - ocean_ref.shape[0] - 2, width), F32)
    for r in range(height):
        wet = mask_ref[r : r + 1, :].astype(F32)
        state = ocean_ref[:, r, :].astype(F32) * wet
        tile_ref[r] = jnp.concatenate([state, wet, listed, rest], axis=0).astype(BF)


def stack_kernel(place_ref, own_ref, side_ref, cross_ref, even_ref, odd_ref, stack_ref, edge_ref):
    lat, comp = place_ref[0], place_ref[1]
    chans, _, width = own_ref.shape
    valid = window_rule(place_ref)[1]
    low = lat % 2 == 0
    places = (
        (own_ref, 2),
        (side_ref, 3 - 2 * comp),
        (cross_ref, 1 + 2 * comp),
        (even_ref, jnp.where(low, 4, 0)),
        (odd_ref, jnp.where(low, 0, 4)),
    )
    for tile, at in places:
        for r in range(2):
            row = 2 * at + r
            store_row(stack_ref, row, tile[:, r, :].astype(F32) * valid(row), chans)
    for q in range(edge_ref.shape[0]):
        both = jnp.zeros((chans, 128), F32)
        for half in range(2):
            r = 4 * q + 2 * half
            if r < stack_ref.shape[0] // (3 * chans):
                at = [(3 * (r + i) + 1) * chans for i in range(2)]
                ends = edges_of([stack_ref[i : i + chans, :].astype(F32) for i in at])
                both = both + pltpu.roll(ends, 64 * half, 1)
        edge_ref[q] = both.astype(BF)


def centre(ref, slot, chans):
    at = (3 * slot + 1) * chans
    if not isinstance(at, int):
        at = pl.multiple_of(at, 16)
    return ref[pl.ds(at, chans), :].astype(F32)


def window_rule(place_ref):
    first = 4 * place_ref[0] + 2 * place_ref[1] - 4
    limit = place_ref[2]
    return first, lambda r: jnp.where((first + r >= 0) & (first + r < limit), 1.0, 0.0)


def strip_of(own_ref, other_ref):
    tiles = range(own_ref.shape[0])
    both = [with_neighbour(own_ref[q].astype(F32), other_ref[q].astype(F32)) for q in tiles]
    return jnp.concatenate(both, axis=1)


def first_kernel(place_ref, stack_ref, win_ref, wout_ref, next_ref):
    chans, width = wout_ref.shape[1] // 9, stack_ref.shape[1]
    valid = window_rule(place_ref)[1]

    def keep(r, y):
        total = (centre(stack_ref, r, chans) + y).astype(BF).astype(F32)
        store_row(next_ref, r, total * valid(r), chans)

    main_block(stack_ref, turned(win_ref, 0), wout_ref[0], chans, range(1, 9), width, keep, 0, valid)


def second_kernel(place_ref, stack_ref, own_ref, other_ref, win_ref, wout_ref, proj_ref, ocean_ref,
                  next_ref, sent_ref):
    chans, width = wout_ref.shape[1] // 9, stack_ref.shape[1]
    per_row = width // 128
    first, valid = window_rule(place_ref)
    w_in = [turned(win_ref, layer) for layer in range(2)]
    main = {}

    def finish(r, y):
        main[r - 4] = (centre(stack_ref, r, chans) + y).astype(BF).astype(F32)

    strip = strip_of(own_ref, other_ref)
    lane = lanes_of((1, strip.shape[1]))
    inside = (lane >= -first * STRIP) & (lane < (place_ref[2] - first) * STRIP)
    kept = jnp.where(inside, 1.0, 0.0)
    strip = strip + strip_block(strip, w_in[0], wout_ref[0], chans, kept)
    strip = strip.astype(BF).astype(F32) * kept
    main_block(stack_ref, w_in[1], wout_ref[1], chans, range(3, 7), width, finish, 0, valid)
    strip = strip + strip_block(strip, w_in[1], wout_ref[1], chans, kept)

    mended = [mend_row(main[r], strip[:, 128:256], r).astype(BF) for r in range(2)]
    for r in range(2):
        next_ref[:, r, :] = mended[r]
    flux = jnp.dot(proj_ref[...], jnp.concatenate(mended, axis=1), preferred_element_type=F32)
    blocks = [flux[:, 128 * b : 128 * (b + 1)] for b in range(2 * per_row)]
    numbers = ocean_ref[0, 32:48, 0:128].astype(F32)[9:10]
    state = [ocean_ref[r].astype(F32) for r in range(2)]
    outs = chans - 8
    lanes = [(r, slice(128 * b, 128 * (b + 1))) for r in range(2) for b in range(per_row)]
    wet = [state[r][outs : outs + 1, at] for r, at in lanes]
    rest = jnp.zeros((16 - 1 - len(wet), 128), F32)
    ocean = [state[r][0:outs, at] for r, at in lanes]
    sent_ref[...] = jnp.concatenate([*blocks, numbers, *wet, rest, *ocean], axis=0).astype(BF)


def regrid_kernel(place_ref, blocks_ref, atmos_ref, *refs):
    sent, (stack_ref, wet_ref, edge_ref, table, next_hbm, flux_ref, total, index, sem, next_sem) = (
        refs[:8],
        refs[8:],
    )
    leaving = pltpu.make_async_copy(atmos_ref, next_hbm, next_sem)
    leaving.start()
    lat, comp = place_ref[0], place_ref[1]
    peers = len(sent)
    chips = peers // 2
    fluxes = flux_ref.shape[1]
    subs = flux_ref.shape[0] // peers
    per_row = subs // 2
    rows = wet_ref.shape[0]
    chans = stack_ref.shape[0] // (3 * (rows + 2))
    outs = chans - fluxes
    slots = 2 * peers
    places = [2 * (lat ^ (i % chips)) + (comp if i < chips else 1 - comp) for i in range(peers)]
    head = subs * fluxes + 16
    for t, ref in zip(places, sent):
        row = ref[head - 16 : head, :].astype(F32)[0:1]
        table[pl.ds(t, 1), :] = row.astype(jnp.int32)
    copy = pltpu.make_async_copy(table, index, sem)
    copy.start()
    total[...] = jnp.zeros(total.shape, F32)
    for t, ref in zip(places, sent):
        values = ref[0 : head - 16, :].astype(F32)
        for b in range(subs):
            flux_ref[t * subs + b] = values[b * fluxes : (b + 1) * fluxes]
    clear_ends(stack_ref, rows, chans)
    copy.wait()

    def one_tile(t, carry):
        pieces = []
        for slot in range(slots):
            source = jnp.maximum(index[t, slot], 0)
            block = blocks_ref[index[t, 2 * slots + slot]]
            value = flux_ref[t * subs + source].astype(BF)
            piece = jnp.dot(value, block, preferred_element_type=F32)
            pieces.append(piece.astype(BF).astype(F32))
        for slot in range(slots):
            target = jnp.where(index[t, slot] >= 0, index[t, slots + slot], 6)
            at = (slot % peers) * 8 + target
            total[at] = total[at] + pieces[slot]
        return carry

    lax.fori_loop(0, peers, one_tile, 0, unroll=8)

    def tile_row(ref, r):
        state = []
        for b in range(per_row):
            at = head + (r * per_row + b) * outs
            shift = at % 16
            rows16 = ref[at - shift : at - shift + chans, :].astype(F32)
            state.append(rows16[shift : shift + outs])
        marks = ref[head - 16 : head, :].astype(F32)[1 + r * per_row : 1 + (r + 1) * per_row]
        wet = jnp.concatenate([marks[b : b + 1] for b in range(per_row)], axis=1)
        return jnp.concatenate(state, axis=1), wet

    for k in range(chips):
        both = jnp.zeros((chans + fluxes, 128), F32)
        for i in (k, chips + k):
            t = places[i]
            ends = []
            for r in range(2):
                arrived = jnp.concatenate(
                    [total[8 * t + r * per_row + b] for b in range(per_row)], axis=1
                )
                state, wet = tile_row(sent[i], r)
                wet = jnp.concatenate([wet, jnp.zeros((fluxes - 1, wet.shape[1]), F32)], axis=0)
                row = jnp.concatenate([state, arrived.astype(BF).astype(F32)], axis=0)
                store_row(stack_ref, 2 * t + r + 1, row, chans)
                wet_ref[2 * t + r] = wet
                ends.append(jnp.concatenate([row, wet], axis=0))
            both = both + pltpu.roll(edges_of(ends), 64 * (comp if i < chips else 1 - comp), 1)
        edge_ref[lat ^ k] = both.astype(BF)
    leaving.wait()


def ocean_kernel(stack_ref, wet_ref, win_ref, wout_ref, next_ref):
    chans, outs = win_ref.shape[1] // 9, wout_ref.shape[1] // 9
    rows, width = wet_ref.shape[0], stack_ref.shape[1]
    clear_ends(next_ref, rows, chans)

    def emit(r, y):
        state = centre(stack_ref, r + 1, chans)
        total = (wet_ref[r, 0:1, :] * (state[0:outs] + y)).astype(BF).astype(F32)
        store_row(next_ref, r + 1, jnp.concatenate([total, state[outs:]], axis=0), chans)

    main_block(stack_ref, turned(win_ref, 0), wout_ref[0], outs, range(rows), width, emit)


def finish_kernel(place_ref, table_ref, stack_ref, wet_ref, own_ref, other_ref, win_ref, wout_ref,
                  blocks_ref, next_ref, temp_ref, hidden_ref, surface, total, index, sem):
    copy = pltpu.make_async_copy(table_ref, index, sem)
    copy.start()
    lat, comp = place_ref[0], place_ref[1]
    t = 2 * lat + comp
    chans, outs = win_ref.shape[1] // 9, wout_ref.shape[1] // 9
    hidden = win_ref.shape[2]
    rows, width = wet_ref.shape[0], stack_ref.shape[1]
    per_row = width // 128
    w_in = [turned(win_ref, layer) for layer in range(2)]
    total[...] = jnp.zeros(total.shape, F32)
    copy.wait()

    strip = strip_of(own_ref, other_ref)
    wet = strip[chans : chans + 1]
    state, fixed = strip[0:outs], strip[outs:chans]
    state = wet * (state + strip_block(strip[0:chans], w_in[0], wout_ref[0], outs))
    state = state.astype(BF).astype(F32)

    last = wout_ref[1].astype(F32)
    none = jnp.zeros((5, hidden), F32)
    w_temp = jnp.concatenate(
        [v for a in range(3) for v in (*(last[(3 * a + b) * outs][None] for b in range(3)), none)]
        + [jnp.zeros((8, hidden), F32)],
        axis=0,
    ).astype(BF)
    ends = jnp.zeros((hidden, width), BF)
    hidden_ref[0] = ends
    hidden_ref[rows + 1] = ends
    parts = {}
    for r in range(0, rows, 2):
        at = [(r + q) * 3 * chans for q in range(2)]
        taps = jnp.concatenate([stack_ref[i : i + 9 * chans, :] for i in at], axis=1)
        active = gelu(jnp.dot(w_in[1], taps, preferred_element_type=F32)).astype(BF)
        for q in range(2):
            hidden_ref[r + q + 1] = active[:, q * width : (q + 1) * width]
        z = jnp.dot(w_temp, active, preferred_element_type=F32)
        for a in range(3):
            for q in range(2):
                part = z[8 * a : 8 * a + 8, q * width : (q + 1) * width]
                row = r + q - a + 1
                parts[row] = parts[row] + part if row in parts else part

    source = jnp.concatenate([state, fixed], axis=0)
    state = wet * (state + strip_block(source, w_in[1], wout_ref[1], outs))
    state = state.astype(BF).astype(F32)

    for r in range(rows):
        y = parts[r]
        y = y[1:2] + west(y)[0:1] + east(y)[2:3]
        top = wet_ref[r, 0:1, :] * (centre(stack_ref, r + 1, chans)[0:8] + y)
        q = r // 4
        top = mend_row(top, state[0:8, 128 * q : 128 * (q + 1)], r)
        for b in range(per_row):
            surface[(r // 2) * 8 + (r % 2) * per_row + b] = top[:, 128 * b : 128 * (b + 1)]

    edge = jnp.zeros((outs, 128), F32)
    for q in range(own_ref.shape[0]):
        edge = jnp.where(lat == q, state[:, 128 * q : 128 * (q + 1)], edge)
    edge = pltpu.roll(edge, jnp.where(comp == 1, 64, 0), 1)
    z = [
        jnp.dot(
            wout_ref[1],
            jnp.concatenate([hidden_ref[2 * t + 2 * p + q] for q in range(2)], axis=1),
            preferred_element_type=F32,
        )
        for p in range(2)
    ]
    for r in range(2):
        y = sum(
            z[(r + a) // 2][
                3 * a * outs : 3 * (a + 1) * outs, (r + a) % 2 * width : ((r + a) % 2 + 1) * width
            ]
            for a in range(3)
        )
        row = centre(stack_ref, 2 * t + r + 1, chans)[0:outs] + column_sum(y, outs)
        next_ref[:, r, :] = mend_row(wet_ref[2 * t + r, 0:1, :] * row, edge, r).astype(BF)

    peers = rows // 2
    slots = 2 * peers
    for slot in range(slots):
        source = index[t, slot]
        target = index[t, slots + slot]
        block = blocks_ref[index[t, 2 * slots + slot]]
        value = surface[(slot % peers) * 8 + target].astype(BF)
        piece = lax.dot_general(value, block, (((1,), (1,)), ((), ())), preferred_element_type=F32)
        at = jnp.where(source >= 0, source, 6)
        total[at] = total[at] + piece
    for r in range(2):
        temp_ref[r : r + 1, :] = jnp.concatenate(
            [total[r * per_row + b][0:1] for b in range(per_row)], axis=1
        )


def call(kernel, out_shape, operands, scratch=(), smem=1, anywhere=0, flops=0, leaving=None):
    held = len(operands) - smem - anywhere
    spaces = [pltpu.SMEM] * smem + [pltpu.VMEM] * held + [pltpu.HBM] * anywhere
    out_specs = jax.tree.map(lambda _: pl.BlockSpec(memory_space=pltpu.VMEM), out_shape)
    if leaving is not None:
        out_shape = (*out_shape, leaving)
        out_specs = (*out_specs, pl.BlockSpec(memory_space=pl.ANY))
    return pl.pallas_call(
        kernel,
        out_shape=out_shape,
        in_specs=[pl.BlockSpec(memory_space=space) for space in spaces],
        out_specs=out_specs,
        scratch_shapes=list(scratch),
        compiler_params=pltpu.CompilerParams(vmem_limit_bytes=40 * 2**20),
        cost_estimate=pl.CostEstimate(flops=flops, bytes_accessed=2**20, transcendentals=0),
    )(*operands)


def column_device(
    atmos_state,
    ocean_state,
    ocean_mask,
    atmos_in_w,
    atmos_out_w,
    ocean_in_w,
    ocean_out_w,
    flux_proj,
    regrid_blocks,
    regrid_source_block,
    regrid_target_block,
    regrid_weight_block,
):
    chans, height, width = atmos_state.shape
    outs = ocean_state.shape[0]
    lats = lax.axis_size("lat")
    tiles = lats * lax.axis_size("comp")
    rows = tiles * height
    layers, _, hidden_a, _ = atmos_in_w.shape
    hidden_o = ocean_in_w.shape[2]
    fluxes = flux_proj.shape[0]
    place = jnp.stack([lax.axis_index("lat"), lax.axis_index("comp"), rows]).astype(jnp.int32)

    def far(v, k):
        return lax.ppermute(v, "lat", [(i, i ^ k) for i in range(lats)])

    def swap(v, axis):
        return lax.ppermute(v, axis, [(0, 1), (1, 0)])

    def conv_flops(hidden, outs):
        return 2 * layers * rows * width * 9 * hidden * (chans + outs)

    tile = jax.ShapeDtypeStruct((height, chans, width), BF)
    slots = (regrid_source_block, regrid_target_block, regrid_weight_block)
    given = [*(jnp.transpose(v, (0, 1, 3, 2)) for v in slots), ocean_state, ocean_mask]
    ocean_tile = call(
        pack_ocean_kernel,
        tile,
        given,
        [*(pltpu.VMEM(v.shape, v.dtype) for v in given), pltpu.SemaphoreType.DMA((len(given),))],
        smem=0,
        anywhere=len(given),
        flops=conv_flops(hidden_a, chans),
    )
    cross = [(i, i + 1) for i in range(1, tiles - 1, 2)]
    odd = [(i, i + 1) for i in range(1, lats - 1, 2)]

    def both_ways(pairs):
        return pairs + [(j, i) for i, j in pairs]

    cross.append((0, tiles - 1))
    odd.append((0, lats - 1))

    near = [
        atmos_state,
        swap(atmos_state, "comp"),
        lax.ppermute(atmos_state, ("lat", "comp"), both_ways(cross)),
        far(atmos_state, 1),
        lax.ppermute(atmos_state, "lat", both_ways(odd)),
    ]
    def taps_in(w):
        return jnp.transpose(w, (0, 1, 3, 2)).reshape(w.shape[0], 9 * w.shape[3], w.shape[2])

    def taps_out(w):
        return w.reshape(w.shape[0], 9 * w.shape[2], w.shape[3])

    win_a, wout_a = taps_in(atmos_in_w), taps_out(atmos_out_w)
    win_o, wout_o = taps_in(ocean_in_w), taps_out(ocean_out_w)

    window = height * len(near)
    stack_shape = (window * 3 * chans, width)
    atmos_stack, edges = call(
        stack_kernel,
        (
            jax.ShapeDtypeStruct(stack_shape, BF),
            jax.ShapeDtypeStruct((pl.cdiv(window * STRIP, 128), chans, 128), BF),
        ),
        [place, *near],
        flops=conv_flops(hidden_a, chans),
    )
    edges_other = swap(edges, "lon")
    atmos_stack = call(
        first_kernel,
        jax.ShapeDtypeStruct(stack_shape, BF),
        [place, atmos_stack, win_a, wout_a],
        flops=4 * conv_flops(hidden_a, chans),
    )
    subs = height * width // 128
    atmos_next, sent = call(
        second_kernel,
        (
            jax.ShapeDtypeStruct((chans, height, width), BF),
            jax.ShapeDtypeStruct((subs * (fluxes + outs) + 16, 128), BF),
        ),
        [place, atmos_stack, edges, edges_other, win_a, wout_a, flux_proj, ocean_tile],
        flops=4 * conv_flops(hidden_a, chans),
    )
    others = {k: far(sent, k) for k in reversed(range(1, lats))}
    sent = [sent] + [others[k] for k in range(1, lats)]
    sent = sent + [swap(v, "comp") for v in sent]
    stack_shape = ((rows + 2) * 3 * chans, width)
    ocean_stack, wet, ocean_edges, table, atmos_next = call(
        regrid_kernel,
        (
            jax.ShapeDtypeStruct(stack_shape, BF),
            jax.ShapeDtypeStruct((rows, fluxes, width), F32),
            jax.ShapeDtypeStruct((lats, chans + fluxes, 128), BF),
            jax.ShapeDtypeStruct((tiles, 128), jnp.int32),
        ),
        [place, regrid_blocks, atmos_next, *sent],
        [
            pltpu.VMEM((tiles * subs, fluxes, 128), F32),
            pltpu.VMEM((tiles * 8, fluxes, 128), F32),
            pltpu.SMEM((tiles, 128), jnp.int32),
            pltpu.SemaphoreType.DMA,
            pltpu.SemaphoreType.DMA,
        ],
        flops=conv_flops(hidden_o, outs),
        leaving=jax.ShapeDtypeStruct((chans, height, width), BF),
    )
    ocean_edges_other = swap(ocean_edges, "lon")
    ocean_stack = call(
        ocean_kernel,
        jax.ShapeDtypeStruct(stack_shape, BF),
        [ocean_stack, wet, win_o, wout_o],
        smem=0,
        flops=4 * conv_flops(hidden_o, outs),
    )
    ocean_next, surface_temp = call(
        finish_kernel,
        (
            jax.ShapeDtypeStruct((outs, height, width), BF),
            jax.ShapeDtypeStruct((height, width), F32),
        ),
        [
            place,
            table,
            ocean_stack,
            wet,
            ocean_edges,
            ocean_edges_other,
            win_o,
            wout_o,
            regrid_blocks,
        ],
        [
            pltpu.VMEM((rows + 2, hidden_o, width), BF),
            pltpu.VMEM((tiles * 8, 8, 128), F32),
            pltpu.VMEM((8, 8, 128), F32),
            pltpu.SMEM((tiles, 128), jnp.int32),
            pltpu.SemaphoreType.DMA,
        ],
    )
    return atmos_next, ocean_next, surface_temp


def solution(mesh):
    in_specs = (
        P(None, ("grp", "lat", "comp"), "lon"),
        P(None, ("grp", "lat", "comp"), "lon"),
        P(("grp", "lat", "comp"), "lon"),
        P(),
        P(),
        P(),
        P(),
        P(),
        P(),
        P(("grp", "lat", "comp"), "lon", None, None),
        P(("grp", "lat", "comp"), "lon", None, None),
        P(("grp", "lat", "comp"), "lon", None, None),
    )
    out_specs = (
        P(None, ("grp", "lat", "comp"), "lon"),
        P(None, ("grp", "lat", "comp"), "lon"),
        P(("grp", "lat", "comp"), "lon"),
    )
    shape = mesh.shape
    short = (shape["lat"], shape["comp"], shape["lon"]) == (4, 2, 2)
    return jax.shard_map(
        column_device if short else per_device,
        mesh=mesh,
        in_specs=in_specs,
        out_specs=out_specs,
        check_vma=False,
    )
```

```python
import functools

import jax
import jax.numpy as jnp
from jax import lax
from jax.experimental import pallas as pl
from jax.experimental.pallas import tpu as pltpu
from jax.sharding import PartitionSpec as P

BF = jnp.bfloat16
F32 = jnp.float32
EDGE = 8
STRIP = 4 * EDGE


def with_halo(cells, sides, width):
    for axis, dim in sides:
        count = lax.axis_size(axis)
        head = lax.slice_in_dim(cells, 0, width, axis=dim)
        tail = lax.slice_in_dim(cells, cells.shape[dim] - width, cells.shape[dim], axis=dim)
        cells = jnp.concatenate(
            [
                lax.ppermute(tail, axis, [(i, (i + 1) % count) for i in range(count)]),
                cells,
                lax.ppermute(head, axis, [((i + 1) % count, i) for i in range(count)]),
            ],
            axis=dim,
        )
    return cells


def clear_poles(wide, width):
    block_height = wide.shape[1]
    position = lax.axis_index(("lat", "comp"))
    final = lax.axis_size(("lat", "comp")) - 1
    row_ids = lax.iota(jnp.int32, block_height)
    outside = (position == 0) & (row_ids < width) | (position == final) & (
        row_ids >= block_height - width
    )
    return jnp.where(outside[None, :, None], jnp.zeros((), wide.dtype), wide)


def padded_rims(field):
    wide = with_halo(field, ((("lat", "comp"), 1), ("lon", 2)), 1)
    return clear_poles(wide, 1)


def apply_taps(padded, weights, block_height, block_breadth):
    total = jnp.zeros((weights.shape[1], block_height, block_breadth), jnp.float32)
    for row_tap in range(3):
        for col_tap in range(3):
            window = padded[:, row_tap : row_tap + block_height, col_tap : col_tap + block_breadth]
            total = total + jnp.einsum(
                "hc,crw->hrw",
                weights[row_tap * 3 + col_tap],
                window,
                preferred_element_type=jnp.float32,
            )
    return total


def conv_block(state, extra, w_in, w_out, wet):
    block_height, block_breadth = (state.shape[1], state.shape[2])
    source = state if extra is None else jnp.concatenate([state, extra], axis=0)
    hidden = jax.nn.gelu(apply_taps(padded_rims(source), w_in, block_height, block_breadth)).astype(
        jnp.bfloat16
    )
    hidden = padded_rims(hidden)
    total = state.astype(jnp.float32) + apply_taps(hidden, w_out, block_height, block_breadth)
    if wet is not None:
        total = total * wet
    return total.astype(jnp.bfloat16)


def send_fluxes(block_values, destination_blocks):
    arrived, arrived_targets = (
        lax.all_to_all(block_values, ("lat", "comp"), split_axis=0, concat_axis=0, tiled=True),
        lax.all_to_all(
            destination_blocks, ("lat", "comp"), split_axis=0, concat_axis=0, tiled=True
        ),
    )
    return (arrived, arrived_targets)


def send_back(block_values):
    return lax.all_to_all(block_values, ("lat", "comp"), split_axis=0, concat_axis=0, tiled=True)


def per_device(
    atmos_state,
    ocean_state,
    ocean_mask,
    atmos_in_w,
    atmos_out_w,
    ocean_in_w,
    ocean_out_w,
    flux_proj,
    regrid_blocks,
    regrid_source_block,
    regrid_target_block,
    regrid_weight_block,
):
    block_height, block_breadth = (atmos_state.shape[1], atmos_state.shape[2])
    cells_per_block = regrid_blocks.shape[1]
    subblock_count = block_height * block_breadth // cells_per_block
    peer_count = regrid_source_block.shape[2]
    slot_count = regrid_source_block.shape[3]
    flux_count = flux_proj.shape[0]
    atmosphere_model = atmos_state
    for layer in range(atmos_in_w.shape[0]):
        atmosphere_model = conv_block(
            atmosphere_model, None, atmos_in_w[layer], atmos_out_w[layer], None
        )
    surface_flux = jnp.einsum(
        "fc,crw->frw", flux_proj, atmosphere_model, preferred_element_type=jnp.float32
    ).astype(jnp.bfloat16)
    flux_blocks = surface_flux.reshape(flux_count, subblock_count, cells_per_block)
    sources = regrid_source_block.reshape(peer_count * slot_count)
    destination_blocks = regrid_target_block.reshape(peer_count * slot_count)
    weight_ids = regrid_weight_block.reshape(peer_count * slot_count)
    sub_ids = lax.iota(jnp.int32, subblock_count)
    select_blocks = (sources[:, None] == sub_ids[None, :]).astype(jnp.bfloat16)
    chosen = jnp.einsum(
        "ps,fsb->pfb", select_blocks, flux_blocks, preferred_element_type=jnp.float32
    ).astype(jnp.bfloat16)
    collected_values = jnp.take(regrid_blocks, weight_ids, axis=0)
    contrib = jnp.einsum(
        "pfb,pbd->pfd", chosen, collected_values, preferred_element_type=jnp.float32
    ).astype(jnp.bfloat16)
    arrived, arrived_targets = send_fluxes(
        contrib.reshape(peer_count, slot_count, flux_count, cells_per_block),
        destination_blocks.reshape(peer_count, slot_count),
    )
    place_blocks = (
        arrived_targets.reshape(peer_count * slot_count)[:, None] == sub_ids[None, :]
    ).astype(jnp.bfloat16)
    ocean_flux = jnp.einsum(
        "ps,pfd->fsd",
        place_blocks,
        arrived.reshape(peer_count * slot_count, flux_count, cells_per_block),
        preferred_element_type=jnp.float32,
    )
    ocean_flux = ocean_flux.astype(jnp.bfloat16).reshape(flux_count, block_height, block_breadth)
    wet = ocean_mask.astype(jnp.float32)[None]
    ocean_model = (ocean_state.astype(jnp.float32) * wet).astype(jnp.bfloat16)
    for layer in range(ocean_in_w.shape[0]):
        ocean_model = conv_block(
            ocean_model, ocean_flux, ocean_in_w[layer], ocean_out_w[layer], wet
        )
    surface_temp_block = ocean_model[0].reshape(subblock_count, cells_per_block)
    outgoing = jnp.einsum(
        "qb,be->qe", place_blocks, surface_temp_block, preferred_element_type=jnp.float32
    ).astype(jnp.bfloat16)
    received_back = send_back(outgoing.reshape(peer_count, slot_count, cells_per_block))
    received_back = received_back.reshape(peer_count * slot_count, cells_per_block)
    surface_temp_contributions = jnp.einsum(
        "tge,te->tg", collected_values, received_back, preferred_element_type=jnp.float32
    )
    surface_temp_grid = jnp.einsum(
        "yl,yo->lo",
        select_blocks.astype(jnp.float32),
        surface_temp_contributions,
        preferred_element_type=jnp.float32,
    )
    return (atmosphere_model, ocean_model, surface_temp_grid.reshape(block_height, block_breadth))


def gelu(v):
    u = v * (0.7978845608 + 0.0356774081 * (v * v))
    return v + v * jnp.tanh(u)


def west(v):
    return pltpu.roll(v, 1, 1)


def east(v):
    return pltpu.roll(v, v.shape[1] - 1, 1)


def store_row(s_ref, slot, row, chans):
    base = slot * 3 * chans
    if not isinstance(base, int):
        base = pl.multiple_of(base, 16)
    taps = jnp.concatenate([west(row), row, east(row)], axis=0).astype(BF)
    s_ref[pl.ds(base, 3 * chans), :] = taps


def clear_ends(s_ref, rows, chans):
    zero = jnp.zeros((3 * chans, s_ref.shape[1]), BF)
    s_ref[0 : 3 * chans, :] = zero
    s_ref[(rows + 1) * 3 * chans : (rows + 2) * 3 * chans, :] = zero


def column_sum(z, outs):
    return 0.5 * (z[outs : 2 * outs] + west(z[0:outs]) + east(z[2 * outs : 3 * outs]))


def main_block(s_ref, w_in, w_out, outs, rows, width, emit, shift=1, valid=None):
    chans = w_in.shape[1] // 9
    span = 9 * chans
    ahead, behind = None, None
    for r in rows[::2]:
        at = [(r + q - 1 + shift) * 3 * chans for q in range(2)]
        taps = jnp.concatenate([s_ref[i : i + span, :] for i in at], axis=1)
        hidden = gelu(jnp.dot(w_in, taps, preferred_element_type=F32))
        if valid is not None:
            kept = [jnp.full((1, width), valid(r + q), F32) for q in range(2)]
            hidden = hidden * jnp.concatenate(kept, axis=1)
        z = jnp.dot(w_out, hidden.astype(BF), preferred_element_type=F32)
        part = [
            [z[a * 3 * outs : (a + 1) * 3 * outs, q * width : (q + 1) * width] for q in range(2)]
            for a in range(3)
        ]
        if ahead is not None:
            emit(r - 1, column_sum(ahead + part[2][0], outs))
            emit(r, column_sum(behind + part[1][0] + part[2][1], outs))
        elif valid is None:
            emit(r, column_sum(part[1][0] + part[2][1], outs))
        ahead = part[0][0] + part[1][1]
        behind = part[0][1]
    if valid is None:
        emit(rows[-1], column_sum(ahead, outs))


def turned(w_ref, layer):
    return jnp.transpose(w_ref[layer])


def lanes_of(shape):
    return lax.broadcasted_iota(jnp.int32, shape, len(shape) - 1)


def edges_of(rows):
    shape = (rows[0].shape[0], 128)
    lane = lanes_of(shape)
    total = jnp.zeros(shape, F32)
    for i, row in enumerate(rows):
        at = i * STRIP + EDGE
        left = pltpu.roll(row[:, 0:128], at, 1)
        total = jnp.where((lane >= at) & (lane < at + EDGE), left, total)
        at = at + EDGE
        width = row.shape[1]
        right = pltpu.roll(row[:, width - 128 : width], (at + EDGE) % 128, 1)
        total = jnp.where((lane >= at) & (lane < at + EDGE), right, total)
    return total


def with_neighbour(own, other):
    place = lanes_of(own.shape) % STRIP
    left = pltpu.roll(other, 128 - 2 * EDGE, 1)
    right = pltpu.roll(other, 2 * EDGE, 1)
    return jnp.where(place < EDGE, left, jnp.where(place >= 3 * EDGE, right, own))


def strip_shift(v, a, b, poles):
    width = v.shape[1]
    moved = pltpu.roll(v, (-((a - 1) * STRIP + b - 1)) % width, 1) if (a, b) != (1, 1) else v
    lane = lanes_of(v.shape)
    if poles and a == 0:
        moved = jnp.where(lane < STRIP, 0.0, moved)
    if poles and a == 2:
        moved = jnp.where(lane >= width - STRIP, 0.0, moved)
    return moved


def strip_block(source, w_in, w_out, outs, kept=None):
    poles = kept is None
    taps = jnp.concatenate(
        [strip_shift(source, a, b, poles) for a in range(3) for b in range(3)], axis=0
    ).astype(BF)
    hidden = gelu(jnp.dot(w_in, taps, preferred_element_type=F32))
    if not poles:
        hidden = hidden * kept
    z = jnp.dot(w_out, hidden.astype(BF), preferred_element_type=F32)
    total = z[4 * outs : 5 * outs]
    for tap in range(9):
        if tap != 4:
            total = total + strip_shift(z[tap * outs : (tap + 1) * outs], tap // 3, tap % 3, poles)
    return 0.5 * total


def mend_row(row, strip, r):
    width = row.shape[1]
    at = (r % 4) * STRIP + EDGE
    lane = lanes_of((row.shape[0], 128))
    left = pltpu.roll(strip, (-at) % 128, 1)
    right = pltpu.roll(strip, (-(at + 2 * EDGE)) % 128, 1)
    head = jnp.where(lane < 4, left, row[:, 0:128])
    tail = jnp.where(lane >= 124, right, row[:, width - 128 : width])
    return jnp.concatenate([head, row[:, 128 : width - 128], tail], axis=1)


def pack_ocean_kernel(source_hbm, target_hbm, weight_hbm, ocean_hbm, mask_hbm, tile_ref, source_ref,
                      target_ref, weight_ref, ocean_ref, mask_ref, sems):
    given = (source_hbm, target_hbm, weight_hbm, ocean_hbm, mask_hbm)
    numbers = (source_ref, target_ref, weight_ref)
    held = (*numbers, ocean_ref, mask_ref)
    copies = [pltpu.make_async_copy(v, h, sems.at[i]) for i, (v, h) in enumerate(zip(given, held))]
    for copy in copies:
        copy.start()
    for copy in copies:
        copy.wait()
    height, span, width = tile_ref.shape
    slots, peers = source_ref.shape[2:]
    listed = [ref[0, 0, s : s + 1, :].astype(F32) for ref in numbers for s in range(slots)]
    listed.append(jnp.zeros((1, width - len(listed) * peers), F32))
    listed = jnp.concatenate(listed, axis=1)
    rest = jnp.zeros((span - ocean_ref.shape[0] - 2, width), F32)
    for r in range(height):
        wet = mask_ref[r : r + 1, :].astype(F32)
        state = ocean_ref[:, r, :].astype(F32) * wet
        tile_ref[r] = jnp.concatenate([state, wet, listed, rest], axis=0).astype(BF)


def stack_kernel(place_ref, own_ref, side_ref, odd_ref, cross_ref, even_ref, stack_ref, edge_ref):
    lat, comp = place_ref[0], place_ref[1]
    chans, _, width = own_ref.shape
    valid = window_rule(place_ref)[1]
    low = lat % 2 == 0
    places = (
        (own_ref, 2),
        (side_ref, 3 - 2 * comp),
        (cross_ref, 1 + 2 * comp),
        (even_ref, jnp.where(low, 4, 0)),
        (odd_ref, jnp.where(low, 0, 4)),
    )
    for tile, at in places:
        for r in range(2):
            row = 2 * at + r
            store_row(stack_ref, row, tile[:, r, :].astype(F32) * valid(row), chans)
    for q in range(edge_ref.shape[0]):
        both = jnp.zeros((chans, 128), F32)
        for half in range(2):
            r = 4 * q + 2 * half
            if r < stack_ref.shape[0] // (3 * chans):
                at = [(3 * (r + i) + 1) * chans for i in range(2)]
                ends = edges_of([stack_ref[i : i + chans, :].astype(F32) for i in at])
                both = both + pltpu.roll(ends, 64 * half, 1)
        edge_ref[q] = both.astype(BF)


def centre(ref, slot, chans):
    at = (3 * slot + 1) * chans
    if not isinstance(at, int):
        at = pl.multiple_of(at, 16)
    return ref[pl.ds(at, chans), :].astype(F32)


def window_rule(place_ref):
    first = 4 * place_ref[0] + 2 * place_ref[1] - 4
    limit = place_ref[2]
    return first, lambda r: jnp.where((first + r >= 0) & (first + r < limit), 1.0, 0.0)


def strip_of(own_ref, other_ref):
    tiles = range(own_ref.shape[0])
    both = [with_neighbour(own_ref[q].astype(F32), other_ref[q].astype(F32)) for q in tiles]
    return jnp.concatenate(both, axis=1)


def first_kernel(place_ref, stack_ref, win_ref, wout_ref, next_ref):
    chans, width = wout_ref.shape[1] // 9, stack_ref.shape[1]
    valid = window_rule(place_ref)[1]

    def keep(r, y):
        total = (centre(stack_ref, r, chans) + y).astype(BF).astype(F32)
        store_row(next_ref, r, total * valid(r), chans)

    main_block(stack_ref, turned(win_ref, 0), wout_ref[0], chans, range(1, 9), width, keep, 0, valid)


def second_kernel(place_ref, stack_ref, own_ref, other_ref, win_ref, wout_ref, proj_ref, ocean_ref,
                  next_ref, sent_ref):
    chans, width = wout_ref.shape[1] // 9, stack_ref.shape[1]
    per_row = width // 128
    first, valid = window_rule(place_ref)
    w_in = [turned(win_ref, layer) for layer in range(2)]
    main = {}

    def finish(r, y):
        main[r - 4] = (centre(stack_ref, r, chans) + y).astype(BF).astype(F32)

    strip = strip_of(own_ref, other_ref)
    lane = lanes_of((1, strip.shape[1]))
    inside = (lane >= -first * STRIP) & (lane < (place_ref[2] - first) * STRIP)
    kept = jnp.where(inside, 1.0, 0.0)
    strip = strip + strip_block(strip, w_in[0], wout_ref[0], chans, kept)
    strip = strip.astype(BF).astype(F32) * kept
    main_block(stack_ref, w_in[1], wout_ref[1], chans, range(3, 7), width, finish, 0, valid)
    strip = strip + strip_block(strip, w_in[1], wout_ref[1], chans, kept)

    mended = [mend_row(main[r], strip[:, 128:256], r).astype(BF) for r in range(2)]
    for r in range(2):
        next_ref[:, r, :] = mended[r]
    flux = jnp.dot(proj_ref[...], jnp.concatenate(mended, axis=1), preferred_element_type=F32)
    blocks = [flux[:, 128 * b : 128 * (b + 1)] for b in range(2 * per_row)]
    numbers = ocean_ref[0, 32:48, 0:128].astype(F32)[9:10]
    state = [ocean_ref[r].astype(F32) for r in range(2)]
    outs = chans - 8
    lanes = [(r, slice(128 * b, 128 * (b + 1))) for r in range(2) for b in range(per_row)]
    wet = [state[r][outs : outs + 1, at] for r, at in lanes]
    rest = jnp.zeros((16 - 1 - len(wet), 128), F32)
    ocean = [state[r][0:outs, at] for r, at in lanes]
    sent_ref[...] = jnp.concatenate([*blocks, numbers, *wet, rest, *ocean], axis=0).astype(BF)


def regrid_kernel(place_ref, blocks_ref, atmos_ref, *refs):
    sent, (stack_ref, wet_ref, edge_ref, table, next_hbm, flux_ref, total, index, sem, next_sem) = (
        refs[:8],
        refs[8:],
    )
    leaving = pltpu.make_async_copy(atmos_ref, next_hbm, next_sem)
    leaving.start()
    lat, comp = place_ref[0], place_ref[1]
    peers = len(sent)
    chips = peers // 2
    fluxes = flux_ref.shape[1]
    subs = flux_ref.shape[0] // peers
    per_row = subs // 2
    rows = wet_ref.shape[0]
    chans = stack_ref.shape[0] // (3 * (rows + 2))
    outs = chans - fluxes
    slots = 2 * peers
    places = [2 * (lat ^ (i % chips)) + (comp if i < chips else 1 - comp) for i in range(peers)]
    head = subs * fluxes + 16
    for t, ref in zip(places, sent):
        row = ref[head - 16 : head, :].astype(F32)[0:1]
        table[pl.ds(t, 1), :] = row.astype(jnp.int32)
    copy = pltpu.make_async_copy(table, index, sem)
    copy.start()
    total[...] = jnp.zeros(total.shape, F32)
    for t, ref in zip(places, sent):
        values = ref[0 : head - 16, :].astype(F32)
        for b in range(subs):
            flux_ref[t * subs + b] = values[b * fluxes : (b + 1) * fluxes]
    clear_ends(stack_ref, rows, chans)
    copy.wait()

    def one_tile(t, carry):
        pieces = []
        for slot in range(slots):
            source = jnp.maximum(index[t, slot], 0)
            block = blocks_ref[index[t, 2 * slots + slot]]
            value = flux_ref[t * subs + source].astype(BF)
            piece = jnp.dot(value, block, preferred_element_type=F32)
            pieces.append(piece.astype(BF).astype(F32))
        for slot in range(slots):
            target = jnp.where(index[t, slot] >= 0, index[t, slots + slot], 6)
            at = (slot % peers) * 8 + target
            total[at] = total[at] + pieces[slot]
        return carry

    lax.fori_loop(0, peers, one_tile, 0, unroll=8)

    def tile_row(ref, r):
        state = []
        for b in range(per_row):
            at = head + (r * per_row + b) * outs
            shift = at % 16
            rows16 = ref[at - shift : at - shift + chans, :].astype(F32)
            state.append(rows16[shift : shift + outs])
        marks = ref[head - 16 : head, :].astype(F32)[1 + r * per_row : 1 + (r + 1) * per_row]
        wet = jnp.concatenate([marks[b : b + 1] for b in range(per_row)], axis=1)
        return jnp.concatenate(state, axis=1), wet

    for k in range(chips):
        both = jnp.zeros((chans + fluxes, 128), F32)
        for i in (k, chips + k):
            t = places[i]
            ends = []
            for r in range(2):
                arrived = jnp.concatenate(
                    [total[8 * t + r * per_row + b] for b in range(per_row)], axis=1
                )
                state, wet = tile_row(sent[i], r)
                wet = jnp.concatenate([wet, jnp.zeros((fluxes - 1, wet.shape[1]), F32)], axis=0)
                row = jnp.concatenate([state, arrived.astype(BF).astype(F32)], axis=0)
                store_row(stack_ref, 2 * t + r + 1, row, chans)
                wet_ref[2 * t + r] = wet
                ends.append(jnp.concatenate([row, wet], axis=0))
            both = both + pltpu.roll(edges_of(ends), 64 * (comp if i < chips else 1 - comp), 1)
        edge_ref[lat ^ k] = both.astype(BF)
    leaving.wait()


def ocean_kernel(stack_ref, wet_ref, win_ref, wout_ref, next_ref):
    chans, outs = win_ref.shape[1] // 9, wout_ref.shape[1] // 9
    rows, width = wet_ref.shape[0], stack_ref.shape[1]
    clear_ends(next_ref, rows, chans)

    def emit(r, y):
        state = centre(stack_ref, r + 1, chans)
        total = (wet_ref[r, 0:1, :] * (state[0:outs] + y)).astype(BF).astype(F32)
        store_row(next_ref, r + 1, jnp.concatenate([total, state[outs:]], axis=0), chans)

    main_block(stack_ref, turned(win_ref, 0), wout_ref[0], outs, range(rows), width, emit)


def finish_kernel(place_ref, table_ref, stack_ref, wet_ref, own_ref, other_ref, win_ref, wout_ref,
                  blocks_ref, next_ref, temp_ref, hidden_ref, surface, total, index, sem):
    copy = pltpu.make_async_copy(table_ref, index, sem)
    copy.start()
    lat, comp = place_ref[0], place_ref[1]
    t = 2 * lat + comp
    chans, outs = win_ref.shape[1] // 9, wout_ref.shape[1] // 9
    hidden = win_ref.shape[2]
    rows, width = wet_ref.shape[0], stack_ref.shape[1]
    per_row = width // 128
    w_in = [turned(win_ref, layer) for layer in range(2)]
    total[...] = jnp.zeros(total.shape, F32)
    copy.wait()

    strip = strip_of(own_ref, other_ref)
    wet = strip[chans : chans + 1]
    state, fixed = strip[0:outs], strip[outs:chans]
    state = wet * (state + strip_block(strip[0:chans], w_in[0], wout_ref[0], outs))
    state = state.astype(BF).astype(F32)

    last = wout_ref[1].astype(F32)
    none = jnp.zeros((5, hidden), F32)
    w_temp = jnp.concatenate(
        [v for a in range(3) for v in (*(last[(3 * a + b) * outs][None] for b in range(3)), none)]
        + [jnp.zeros((8, hidden), F32)],
        axis=0,
    ).astype(BF)
    ends = jnp.zeros((hidden, width), BF)
    hidden_ref[0] = ends
    hidden_ref[rows + 1] = ends
    parts = {}
    for r in range(0, rows, 2):
        at = [(r + q) * 3 * chans for q in range(2)]
        taps = jnp.concatenate([stack_ref[i : i + 9 * chans, :] for i in at], axis=1)
        active = gelu(jnp.dot(w_in[1], taps, preferred_element_type=F32)).astype(BF)
        for q in range(2):
            hidden_ref[r + q + 1] = active[:, q * width : (q + 1) * width]
        z = jnp.dot(w_temp, active, preferred_element_type=F32)
        for a in range(3):
            for q in range(2):
                part = z[8 * a : 8 * a + 8, q * width : (q + 1) * width]
                row = r + q - a + 1
                parts[row] = parts[row] + part if row in parts else part

    source = jnp.concatenate([state, fixed], axis=0)
    state = wet * (state + strip_block(source, w_in[1], wout_ref[1], outs))
    state = state.astype(BF).astype(F32)

    for r in range(rows):
        y = parts[r]
        y = 0.5 * (y[1:2] + west(y)[0:1] + east(y)[2:3])
        top = wet_ref[r, 0:1, :] * (centre(stack_ref, r + 1, chans)[0:8] + y)
        q = r // 4
        top = mend_row(top, state[0:8, 128 * q : 128 * (q + 1)], r)
        for b in range(per_row):
            surface[(r // 2) * 8 + (r % 2) * per_row + b] = top[:, 128 * b : 128 * (b + 1)]

    edge = jnp.zeros((outs, 128), F32)
    for q in range(own_ref.shape[0]):
        edge = jnp.where(lat == q, state[:, 128 * q : 128 * (q + 1)], edge)
    edge = pltpu.roll(edge, jnp.where(comp == 1, 64, 0), 1)
    z = [
        jnp.dot(
            wout_ref[1],
            jnp.concatenate([hidden_ref[2 * t + 2 * p + q] for q in range(2)], axis=1),
            preferred_element_type=F32,
        )
        for p in range(2)
    ]
    for r in range(2):
        y = sum(
            z[(r + a) // 2][
                3 * a * outs : 3 * (a + 1) * outs, (r + a) % 2 * width : ((r + a) % 2 + 1) * width
            ]
            for a in range(3)
        )
        row = centre(stack_ref, 2 * t + r + 1, chans)[0:outs] + column_sum(y, outs)
        next_ref[:, r, :] = mend_row(wet_ref[2 * t + r, 0:1, :] * row, edge, r).astype(BF)

    peers = rows // 2
    slots = 2 * peers
    for slot in range(slots):
        source = index[t, slot]
        target = index[t, slots + slot]
        block = blocks_ref[index[t, 2 * slots + slot]]
        value = surface[(slot % peers) * 8 + target].astype(BF)
        piece = lax.dot_general(value, block, (((1,), (1,)), ((), ())), preferred_element_type=F32)
        at = jnp.where(source >= 0, source, 6)
        total[at] = total[at] + piece
    for r in range(2):
        temp_ref[r : r + 1, :] = jnp.concatenate(
            [total[r * per_row + b][0:1] for b in range(per_row)], axis=1
        )


def call(kernel, out_shape, operands, scratch=(), smem=1, anywhere=0, flops=0, leaving=None):
    held = len(operands) - smem - anywhere
    spaces = [pltpu.SMEM] * smem + [pltpu.VMEM] * held + [pltpu.HBM] * anywhere
    out_specs = jax.tree.map(lambda _: pl.BlockSpec(memory_space=pltpu.VMEM), out_shape)
    if leaving is not None:
        out_shape = (*out_shape, leaving)
        out_specs = (*out_specs, pl.BlockSpec(memory_space=pl.ANY))
    return pl.pallas_call(
        kernel,
        out_shape=out_shape,
        in_specs=[pl.BlockSpec(memory_space=space) for space in spaces],
        out_specs=out_specs,
        scratch_shapes=list(scratch),
        compiler_params=pltpu.CompilerParams(vmem_limit_bytes=40 * 2**20),
        cost_estimate=pl.CostEstimate(flops=flops, bytes_accessed=2**20, transcendentals=0),
    )(*operands)


def column_device(
    atmos_state,
    ocean_state,
    ocean_mask,
    atmos_in_w,
    atmos_out_w,
    ocean_in_w,
    ocean_out_w,
    flux_proj,
    regrid_blocks,
    regrid_source_block,
    regrid_target_block,
    regrid_weight_block,
):
    chans, height, width = atmos_state.shape
    outs = ocean_state.shape[0]
    lats = lax.axis_size("lat")
    tiles = lats * lax.axis_size("comp")
    rows = tiles * height
    layers, _, hidden_a, _ = atmos_in_w.shape
    hidden_o = ocean_in_w.shape[2]
    fluxes = flux_proj.shape[0]
    place = jnp.stack([lax.axis_index("lat"), lax.axis_index("comp"), rows]).astype(jnp.int32)

    def far(v, k):
        return lax.ppermute(v, "lat", [(i, i ^ k) for i in range(lats)])

    def swap(v, axis):
        return lax.ppermute(v, axis, [(0, 1), (1, 0)])

    def conv_flops(hidden, outs):
        return 2 * layers * rows * width * 9 * hidden * (chans + outs)

    tile = jax.ShapeDtypeStruct((height, chans, width), BF)
    slots = (regrid_source_block, regrid_target_block, regrid_weight_block)
    given = [*(jnp.transpose(v, (0, 1, 3, 2)) for v in slots), ocean_state, ocean_mask]
    ocean_tile = call(
        pack_ocean_kernel,
        tile,
        given,
        [*(pltpu.VMEM(v.shape, v.dtype) for v in given), pltpu.SemaphoreType.DMA((len(given),))],
        smem=0,
        anywhere=len(given),
        flops=conv_flops(hidden_a, chans),
    )
    cross = [(i, i + 1) for i in range(1, tiles - 1, 2)]
    odd = [(t, t + 2) for z in range(1, lats - 1, 2) for t in (2 * z, 2 * z + 1)]

    def both_ways(pairs):
        return pairs + [(j, i) for i, j in pairs]

    cross.append((0, tiles - 1))
    odd += [(0, 1), (tiles - 2, tiles - 1)]

    near = [
        atmos_state,
        swap(atmos_state, "comp"),
        lax.ppermute(atmos_state, ("lat", "comp"), both_ways(odd)),
        lax.ppermute(atmos_state, ("lat", "comp"), both_ways(cross)),
        far(atmos_state, 1),
    ]
    def taps_in(w):
        return jnp.transpose(w, (0, 1, 3, 2)).reshape(w.shape[0], 9 * w.shape[3], w.shape[2])

    def taps_out(w):
        return w.reshape(w.shape[0], 9 * w.shape[2], w.shape[3])

    win_a, wout_a = taps_in(atmos_in_w), taps_out(atmos_out_w)
    win_o, wout_o = taps_in(ocean_in_w), taps_out(ocean_out_w)

    window = height * len(near)
    stack_shape = (window * 3 * chans, width)
    atmos_stack, edges = call(
        stack_kernel,
        (
            jax.ShapeDtypeStruct(stack_shape, BF),
            jax.ShapeDtypeStruct((pl.cdiv(window * STRIP, 128), chans, 128), BF),
        ),
        [place, *near],
        flops=conv_flops(hidden_a, chans),
    )
    edges_other = swap(edges, "lon")
    atmos_stack = call(
        first_kernel,
        jax.ShapeDtypeStruct(stack_shape, BF),
        [place, atmos_stack, win_a, wout_a],
        flops=4 * conv_flops(hidden_a, chans),
    )
    subs = height * width // 128
    atmos_next, sent = call(
        second_kernel,
        (
            jax.ShapeDtypeStruct((chans, height, width), BF),
            jax.ShapeDtypeStruct((subs * (fluxes + outs) + 16, 128), BF),
        ),
        [place, atmos_stack, edges, edges_other, win_a, wout_a, flux_proj, ocean_tile],
        flops=4 * conv_flops(hidden_a, chans),
    )
    others = {k: far(sent, k) for k in reversed(range(1, lats))}
    sent = [sent] + [others[k] for k in range(1, lats)]
    sent = sent + [swap(v, "comp") for v in sent]
    stack_shape = ((rows + 2) * 3 * chans, width)
    ocean_stack, wet, ocean_edges, table, atmos_next = call(
        regrid_kernel,
        (
            jax.ShapeDtypeStruct(stack_shape, BF),
            jax.ShapeDtypeStruct((rows, fluxes, width), F32),
            jax.ShapeDtypeStruct((lats, chans + fluxes, 128), BF),
            jax.ShapeDtypeStruct((tiles, 128), jnp.int32),
        ),
        [place, regrid_blocks, atmos_next, *sent],
        [
            pltpu.VMEM((tiles * subs, fluxes, 128), F32),
            pltpu.VMEM((tiles * 8, fluxes, 128), F32),
            pltpu.SMEM((tiles, 128), jnp.int32),
            pltpu.SemaphoreType.DMA,
            pltpu.SemaphoreType.DMA,
        ],
        flops=conv_flops(hidden_o, outs),
        leaving=jax.ShapeDtypeStruct((chans, height, width), BF),
    )
    ocean_edges_other = swap(ocean_edges, "lon")
    ocean_stack = call(
        ocean_kernel,
        jax.ShapeDtypeStruct(stack_shape, BF),
        [ocean_stack, wet, win_o, wout_o],
        smem=0,
        flops=4 * conv_flops(hidden_o, outs),
    )
    ocean_next, surface_temp = call(
        finish_kernel,
        (
            jax.ShapeDtypeStruct((outs, height, width), BF),
            jax.ShapeDtypeStruct((height, width), F32),
        ),
        [
            place,
            table,
            ocean_stack,
            wet,
            ocean_edges,
            ocean_edges_other,
            win_o,
            wout_o,
            regrid_blocks,
        ],
        [
            pltpu.VMEM((rows + 2, hidden_o, width), BF),
            pltpu.VMEM((tiles * 8, 8, 128), F32),
            pltpu.VMEM((8, 8, 128), F32),
            pltpu.SMEM((tiles, 128), jnp.int32),
            pltpu.SemaphoreType.DMA,
        ],
    )
    return atmos_next, ocean_next, surface_temp


def solution(mesh):
    in_specs = (
        P(None, ("grp", "lat", "comp"), "lon"),
        P(None, ("grp", "lat", "comp"), "lon"),
        P(("grp", "lat", "comp"), "lon"),
        P(),
        P(),
        P(),
        P(),
        P(),
        P(),
        P(("grp", "lat", "comp"), "lon", None, None),
        P(("grp", "lat", "comp"), "lon", None, None),
        P(("grp", "lat", "comp"), "lon", None, None),
    )
    out_specs = (
        P(None, ("grp", "lat", "comp"), "lon"),
        P(None, ("grp", "lat", "comp"), "lon"),
        P(("grp", "lat", "comp"), "lon"),
    )
    shape = mesh.shape
    short = (shape["lat"], shape["comp"], shape["lon"]) == (4, 2, 2)
    return jax.shard_map(
        column_device if short else per_device,
        mesh=mesh,
        in_specs=in_specs,
        out_specs=out_specs,
        check_vma=False,
    )
```
